32 devices in a mesh: expert: 16 (over z, x, core), shard: 2 (over y).
Axes of the slice: x: 2, y: 2, z: 4, core: 2. Of those that a mesh axis runs over, the one named last changes fastest.
Arguments:
- tokens: bfloat16 [8192, 1536], P(('expert', 'shard')), may hold values from -6 to 6
- segment_ids: int32 [8192], P(('expert', 'shard')), may hold values from 0 to 2, as said below
- routes: int32 [8192, 8], P(('expert', 'shard')), may hold values from 0 to 15, all different within a row; in each aligned block of 256 rows (0 to 255, 256 to 511, ...) at most 256 rows name the same one
- norm1_gain: bfloat16 [1536], P('shard'), may hold values from 0.099609375 to 1.8984375
- norm2_gain: bfloat16 [1536], P('shard'), may hold values from 0.099609375 to 1.8984375
- query_key_value_weight: bfloat16 [1536, 2560], P('shard'), may hold values from -0.4375 to 0.4375
- out_weight: bfloat16 [1536, 1536], P('shard'), may hold values from -2.5 to 2.5
- route_weight: bfloat16 [1536, 16], P('shard'), may hold values from -0.078125 to 0.078125
- expert_in: bfloat16 [16, 1536, 1024], P('expert', 'shard'), may hold values from -0.15625 to 0.15625
- expert_down: bfloat16 [16, 512, 1536], P('expert', None, 'shard'), may hold values from -6 to 6
- cotangent: bfloat16 [8192, 1536], P(('expert', 'shard')), may hold values from -6 to 6
Outputs:
- block_out: bfloat16 [8192, 1536], P(('expert', 'shard'))
- grad_tokens: float32 [8192, 1536], P(('expert', 'shard'))
- grad_norm1: float32 [1536], P('shard')
- grad_norm2: float32 [1536], P('shard')
- grad_qkv: float32 [1536, 2560], P('shard')
- grad_out: float32 [1536, 1536], P('shard')
- grad_route: float32 [1536, 16], P('shard')
- grad_in: float32 [16, 1536, 1024], P('expert', 'shard')
- grad_down: float32 [16, 512, 1536], P('expert', None, 'shard')
The draws below stay inside these ranges and needn't reach their ends.
Inputs may be any that keep to these rules, and one draw needn't show every extreme that they name: `segment_ids`: within each sequence of 512 consecutive rows the ids number its documents from 0 and never fall. `routes`: each row names 8 different experts; among the 256 rows of one device no expert is named more than 256 times.
All inputs are finite; a program needn't handle non-finite values.
Results may differ from the reference program's by a relative error of at most 0.02.
Values may be sent and summed in bfloat16 or wider, within the bound.
No kernel may reach another device: no remote copies, remote signals or barrier semaphores. Data moves between devices by JAX's collectives and lax.ppermute only.
A program may use at most 256 MiB of HBM per device.

```python
import math
from functools import partial
import jax
import jax.numpy as jnp
import numpy as np
from jax import lax

MODEL_WIDTH = 1536
QUERY_HEADS = 24
KEY_VALUE_HEADS = 8
HEAD_SIZE = 64
FFE = 512
TOPK = 8
TOK_DEV = 256
EXPERTS = 16
CAP = 256
LENGTH = 512
TOKENS = 8192


def draw_segment_ids(key, part):
    key = jax.random.fold_in(key, 11)
    first_key, last_key = jax.random.split(key)
    num_seqs = TOKENS // LENGTH
    starts = jax.random.randint(first_key, (num_seqs,), 1, TOK_DEV)
    finishes = jax.random.randint(last_key, (num_seqs,), LENGTH - TOK_DEV + 1, LENGTH)
    places = jnp.arange(LENGTH)[None, :]
    doc_ids = (places >= starts[:, None]).astype(jnp.int32) + (places >= finishes[:, None]).astype(jnp.int32)
    return doc_ids.reshape(-1)


def shard_levels(own_key, dims, pieces, low, top_value):
    factor_of = 1.0
    for dim, shards_of in pieces:
        heights = jax.random.uniform(jax.random.fold_in(jax.random.fold_in(own_key, 6), dim), (shards_of,), jnp.float32, low / len(pieces), top_value / len(pieces))
        factor_of = factor_of * jnp.repeat(jnp.exp(heights), dims[dim] // shards_of).reshape((-1,) + (1,) * (len(dims) - 1 - dim))
    return factor_of


def shared_out(own_key, own, number, rows, amount, top, bound, lean):
    order = jax.random.permutation(own_key, amount)
    crowded, common = shares(amount, rows * top, bound, lean, True), shares(amount, rows * top, bound, lean, False)
    places = jnp.arange(amount)

    def named(tallies, offset_by):
        used = int((tallies > 0).sum())
        fixed = max(1, used // 4)
        shifted = fixed + (places - fixed + offset_by * (used - fixed)) % max(1, amount - fixed)
        return jnp.zeros((amount,), jnp.int32).at[order[jnp.where(places < fixed, places, shifted)]].set(jnp.asarray(tallies, jnp.int32))

    tallies = jnp.where(number % 4 == 0, named(crowded, number // 4), named(common, number - number // 4 - 1))
    mixed = jax.random.permutation(jax.random.fold_in(own, 3), amount)
    source_of, receiver = mixed[0:amount // 2 * 2:2], mixed[1:amount // 2 * 2:2]
    room = jnp.minimum(tallies[source_of] - 1, bound - tallies[receiver]) // 2
    room = jnp.where((source_of == order[0]) | (receiver == order[0]) | (tallies[receiver] == 0), 0, jnp.maximum(room, 0))
    shifted = jax.random.randint(jax.random.fold_in(own, 4), (amount // 2,), 0, 1 << 20) % (room + 1)
    tallies = tallies.at[source_of].add(-shifted).at[receiver].add(shifted)
    members = jnp.searchsorted(jnp.cumsum(tallies), jnp.arange(rows * top), side="right").astype(jnp.int32)
    listing = members.reshape(top, rows).T
    listing = listing[jax.random.permutation(jax.random.fold_in(own, 1), rows)]
    offset_by = jax.random.randint(jax.random.fold_in(own, 2), (rows, 1), 0, top)
    return jnp.take_along_axis(listing, (jnp.arange(top)[None, :] + offset_by) % top, axis=1)


def shares(amount, total, bound, slope, full):
    loads = [(1 << 20) // math.isqrt(grade ** slope) + 1 for grade in range(1, amount + 1)]
    largest = bound if full else min(bound, max(-(-total // amount), total * loads[0] // sum(loads)))
    least = 1 if total - largest >= amount - 1 else 0
    holding, rest = [largest] + [least] * (amount - 1), total - largest - least * (amount - 1)
    while rest > 0:
        candidates = [i for i in range(1, amount) if holding[i] < largest] or [i for i in range(1, amount) if holding[i] < bound]
        whole, remaining = sum([loads[i] for i in candidates]), rest
        for i in candidates:
            addition = min(bound - holding[i], max(1, remaining * loads[i] // whole), rest)
            holding[i] = holding[i] + addition
            rest = rest - addition
    return np.array(holding)


def gaussian(own_key, shape, spread, reach, shards=(), kind=jnp.bfloat16):
    loudness = shard_levels(own_key, shape, shards, -0.22, 0.18) if shards else 1.0
    values = jax.random.normal(own_key, shape, jnp.float32) * spread * loudness
    return jnp.minimum(jnp.maximum(values, -reach), reach).astype(kind)


def setup_inputs(seed: int = 0) -> dict:
    streams_of = jax.random.split(jax.random.key(seed), 12)
    tokens = gaussian(streams_of[0], (TOKENS, MODEL_WIDTH), 1.0, 6.0, ((0, 32),))
    segment_ids = draw_segment_ids(jax.random.fold_in(streams_of[11], 71), 0)
    routes_keys = jax.random.split(jax.random.fold_in(streams_of[2], 1), TOKENS // TOK_DEV)
    routes_turns = jax.random.permutation(jax.random.fold_in(streams_of[2], 3), TOKENS // TOK_DEV)
    routes = jax.vmap(lambda own, number: shared_out(jax.random.fold_in(streams_of[2], 2), own, number, TOK_DEV, EXPERTS, TOPK, CAP, 2))(routes_keys, routes_turns).reshape((TOKENS, TOPK))
    norm1_gain = jnp.clip(1.0 + 0.18 * jax.random.normal(streams_of[3], (MODEL_WIDTH,), jnp.float32), 0.099609375, 1.8984375).astype(jnp.bfloat16)
    norm2_gain = jnp.clip(1.0 + 0.18 * jax.random.normal(streams_of[4], (MODEL_WIDTH,), jnp.float32), 0.099609375, 1.8984375).astype(jnp.bfloat16)
    query_key_value_weight = gaussian(streams_of[5], (MODEL_WIDTH, (QUERY_HEADS + 2 * KEY_VALUE_HEADS) * HEAD_SIZE), (MODEL_WIDTH // 9) ** -0.5, 0.4375, ((0, 2),))
    out_weight = gaussian(streams_of[6], (QUERY_HEADS * HEAD_SIZE, MODEL_WIDTH), 6 ** -0.5, 2.5, ((0, 2),))
    route_weight = gaussian(streams_of[7], (MODEL_WIDTH, EXPERTS), (4 * MODEL_WIDTH) ** -0.5, 0.078125, ((0, 2),))
    expert_in = gaussian(streams_of[8], (EXPERTS, MODEL_WIDTH, 2 * FFE), MODEL_WIDTH ** -0.5, 0.15625, ((0, 16), (1, 2)))
    expert_down = gaussian(streams_of[9], (EXPERTS, FFE, MODEL_WIDTH), 1 ** -0.5, 6.0, ((0, 16), (2, 2)))
    cotangent = gaussian(streams_of[10], (TOKENS, MODEL_WIDTH), 1.0, 6.0, ((0, 32),))
    return {"tokens": tokens, "segment_ids": segment_ids, "routes": routes, "norm1_gain": norm1_gain, "norm2_gain": norm2_gain, "query_key_value_weight": query_key_value_weight, "out_weight": out_weight, "route_weight": route_weight, "expert_in": expert_in, "expert_down": expert_down, "cotangent": cotangent}


PRECISE = lax.Precision.HIGHEST
RES_SCALE = 0.22
ATT_SCALE = 0.015625
EPSILON = 1e-06
ROPE_BASE = 10000.0
MASKED = -1000000000.0

@jax.custom_vjp
def lower_bound(v):
    return lax.optimization_barrier(v.astype(jnp.bfloat16)).astype(jnp.float32)

@jax.custom_vjp
def low_back(v):
    return v

def low_keep(v):
    return (lower_bound(v), None)

def low_pass(kept, grad):
    return (grad,)

def back_keep(v):
    return (v, None)

def back_low(kept, grad):
    return (lower_bound(grad),)
lower_bound.defvjp(low_keep, low_pass)
low_back.defvjp(back_keep, back_low)

def norm_apply(value_rows, scaling):
    return value_rows * lax.rsqrt(lax.optimization_barrier(jnp.mean(value_rows * value_rows, axis=-1, keepdims=True)) + EPSILON) * scaling

def rotation(positions, half_dim):
    inverse = jnp.power(ROPE_BASE, -(jnp.arange(half_dim) * 2.0 / (2 * half_dim)))
    angles = positions.astype(jnp.float32)[:, None] * inverse[None, :]
    return (jnp.cos(angles), jnp.sin(angles))

def apply_rotary(value_rows, cosine_table, sine_lookup):
    half_dim = value_rows.shape[-1] // 2
    shape_out = (value_rows.shape[0],) + (1,) * (value_rows.ndim - 2) + (half_dim,)
    cosine_table = cosine_table.reshape(shape_out)
    sine_lookup = sine_lookup.reshape(shape_out)
    first_half = value_rows[..., :half_dim]
    second_half = value_rows[..., half_dim:]
    return jnp.concatenate([first_half * cosine_table - second_half * sine_lookup, second_half * cosine_table + first_half * sine_lookup], axis=-1)

def attend(projected_rows, segments):
    span_length = projected_rows.shape[0]
    query_width = QUERY_HEADS * HEAD_SIZE
    pair_width = KEY_VALUE_HEADS * HEAD_SIZE
    positions = jnp.arange(span_length)
    cosine_table, sine_lookup = rotation(positions, HEAD_SIZE // 2)
    query_rows = lower_bound(apply_rotary(projected_rows[:, :query_width].reshape(span_length, KEY_VALUE_HEADS, QUERY_HEADS // KEY_VALUE_HEADS, HEAD_SIZE), cosine_table, sine_lookup))
    heads_of_keys = lower_bound(apply_rotary(projected_rows[:, query_width:query_width + pair_width].reshape(span_length, KEY_VALUE_HEADS, HEAD_SIZE), cosine_table, sine_lookup))
    value_rows = lower_bound(projected_rows[:, query_width + pair_width:].reshape(span_length, KEY_VALUE_HEADS, HEAD_SIZE))
    scores = low_back(jnp.einsum('qgjd,kgd->gjqk', query_rows, heads_of_keys, precision=PRECISE) * ATT_SCALE)
    allowed = (segments[:, None] == segments[None, :]) & (positions[:, None] >= positions[None, :])
    scores = jnp.where(allowed[None, None], scores, MASKED)
    attn_probs = lower_bound(jax.nn.softmax(scores, axis=-1))
    return jnp.einsum('gjqk,kgd->qgjd', attn_probs, value_rows, precision=PRECISE).reshape(span_length, query_width)

def attend_packed(packed):
    return attend(packed[0], packed[1])

def experts_block(inputs, mixing, expert_in, expert_down):
    num_experts = expert_in.shape[0]
    copies = low_back(jnp.broadcast_to(inputs[None], (num_experts,) + inputs.shape))
    gate_up = low_back(jnp.einsum('ebd,edf->ebf', copies, expert_in, precision=PRECISE))
    hidden = lower_bound(jax.nn.silu(gate_up[..., :FFE]) * gate_up[..., FFE:])
    result = lower_bound(low_back(jnp.einsum('ebf,efd->ebd', hidden, expert_down, precision=PRECISE)))
    return jnp.einsum('be,ebd->bd', mixing, result, precision=PRECISE)

def experts_packed(expert_in, expert_down, packed):
    return experts_block(packed[0], packed[1], expert_in, expert_down)

def forward(inputs, gain_one, gain_two, query_key_value_weight, out_weight, route_weight, expert_in, expert_down, segment_ids, routes):
    num_rows = inputs.shape[0]
    num_seqs = num_rows // LENGTH
    normed = lower_bound(norm_apply(inputs, gain_one))
    projected_rows = low_back(jnp.dot(normed, query_key_value_weight, precision=PRECISE))
    attended = lax.map(jax.checkpoint(attend_packed), (projected_rows.reshape(num_seqs, LENGTH, -1), segment_ids.reshape(num_seqs, LENGTH)))
    head_out = lower_bound(low_back(attended.reshape(num_rows, QUERY_HEADS * HEAD_SIZE)))
    branch_out = low_back(jnp.dot(head_out, out_weight, precision=PRECISE))
    middle = inputs + RES_SCALE * branch_out
    second = lower_bound(norm_apply(middle, gain_two))
    logits = low_back(jnp.dot(second, route_weight, precision=PRECISE))
    chosen = jnp.take_along_axis(logits, routes, axis=1)
    gate_probs = jax.nn.softmax(chosen, axis=-1)
    picks = routes[:, :, None] == jnp.arange(route_weight.shape[1])[None, None, :]
    mixing = lax.optimization_barrier(jnp.sum(gate_probs[:, :, None] * picks, axis=1))
    expert_sum = lax.map(jax.checkpoint(partial(experts_packed, expert_in, expert_down)), (second.reshape(num_seqs, LENGTH, -1), mixing.reshape(num_seqs, LENGTH, -1)))
    return middle + RES_SCALE * expert_sum.reshape(inputs.shape)

def reference(tokens, segment_ids, routes, norm1_gain, norm2_gain, query_key_value_weight, out_weight, route_weight, expert_in, expert_down, cotangent):

    def forward_all(inputs, gain_one, gain_two, weight_qkv, weight_out, weight_route, weight_in, weight_down):
        return forward(inputs, gain_one, gain_two, weight_qkv, weight_out, weight_route, weight_in, weight_down, segment_ids, routes)
    output, pullback = jax.vjp(forward_all, tokens.astype(jnp.float32), norm1_gain.astype(jnp.float32), norm2_gain.astype(jnp.float32), query_key_value_weight.astype(jnp.float32), out_weight.astype(jnp.float32), route_weight.astype(jnp.float32), expert_in.astype(jnp.float32), expert_down.astype(jnp.float32))
    grads = pullback(cotangent.astype(jnp.float32))
    return (output.astype(jnp.bfloat16), grads[0], grads[1], grads[2], grads[3], grads[4], grads[5], grads[6], grads[7])
```

```python
from functools import partial

import jax
import jax.numpy as jnp
import numpy as np
from jax import lax
from jax.experimental import pallas as pl
from jax.experimental.pallas import tpu as pltpu
from jax.sharding import Mesh, PartitionSpec as P

QUERY_HEADS = 24
KEY_VALUE_HEADS = 8
HEAD_SIZE = 64
GROUP = QUERY_HEADS // KEY_VALUE_HEADS
RES_SCALE = 0.22
ATT_SCALE = 0.015625
EPSILON = 1e-06
ROPE_BASE = 10000.0
MASKED = -1000000000.0
F32 = jnp.float32
BF16 = jnp.bfloat16
MIB = 1024 * 1024
BIG_VMEM = 60 * MIB


def mm(a, b, dims):
    return lax.dot_general(a, b, (dims, ((), ())), preferred_element_type=F32)


def nn(a, b):
    return mm(a, b, ((1,), (0,)))


def nt(a, b):
    return mm(a, b, ((1,), (1,)))


def tn(a, b):
    return mm(a, b, ((0,), (0,)))


def tie(values, after):
    return lax.optimization_barrier((values, after))[0]


def ring_chips(chips):
    depth = 4 if chips % 4 == 0 else 2
    width = max(1, chips // depth)
    walk = [(z, 0) for z in range(depth)]
    for z in reversed(range(depth)):
        line = range(1, width) if (depth - 1 - z) % 2 == 0 else reversed(range(1, width))
        walk += [(z, x) for x in line]
    return [z * width + x for z, x in walk]


def add_low(a, b):
    return (a.astype(F32) + b.astype(F32)).astype(BF16)


def rms_scale(rows):
    return lax.rsqrt(jnp.mean(rows * rows, axis=-1, keepdims=True) + EPSILON)


def rms_back(rows, scale, gain, grad):
    weighted = grad * gain
    dot = jnp.mean(weighted * rows, axis=-1, keepdims=True)
    return scale * weighted - rows * (scale * scale * scale * dot)


def turn(value, cosine, sine, first):
    swapped = jnp.where(first, pltpu.roll(value, 96, 1), pltpu.roll(value, 32, 1))
    return value * cosine + swapped * sine


def attend_kernel(
    q_ref, k_ref, v_ref, cos_ref, sin_ref, seg_col, seg_row, qkv_out, p_out, head_out, bias, turned
):
    pair, pairs = pl.program_id(0), pl.num_programs(0)
    length = q_ref.shape[0]
    block = min(256, length)
    q_cols = pairs * 2 * GROUP * HEAD_SIZE
    wide = 2 * GROUP * HEAD_SIZE
    first = lax.broadcasted_iota(jnp.int32, (length, 128), 1) % HEAD_SIZE < HEAD_SIZE // 2

    @pl.when(pair == 0)
    def _():
        keys = lax.broadcasted_iota(jnp.int32, (length, length), 0)
        rows = lax.broadcasted_iota(jnp.int32, (length, length), 1)
        allowed = (seg_col[...] == seg_row[...]) & (keys <= rows)
        bias[...] = jnp.where(allowed, 0.0, MASKED)

    cosine, sine = cos_ref[...], sin_ref[...]
    for c in range(wide // 128):
        at = pl.ds(c * 128, 128)
        turned[:, at] = turn(q_ref[:, at], cosine, sine, first).astype(BF16)
    key = turn(k_ref[...], cosine, sine, first).astype(BF16)
    value = v_ref[...].astype(BF16)
    qkv_out[:, pl.ds(pl.multiple_of(pair * wide, 128), wide)] = turned[...]
    qkv_out[:, pl.ds(pl.multiple_of(q_cols + pair * 128, 128), 128)] = key
    qkv_out[:, pl.ds(pl.multiple_of(q_cols + (pairs + pair) * 128, 128), 128)] = value
    value_t = jnp.transpose(v_ref[...]).astype(BF16)
    for r in range(length // block):
        rows = pl.ds(r * block, block)
        end = (r + 1) * block
        mask = bias[0:end, rows]
        mask = jnp.concatenate([mask] * GROUP, axis=1)
        both = []
        for g in range(2):
            query = jnp.concatenate(
                [
                    turned[rows, pl.ds((g * GROUP + j) * HEAD_SIZE, HEAD_SIZE)]
                    for j in range(GROUP)
                ],
                axis=0,
            )
            own_key = key[:end, g * HEAD_SIZE : (g + 1) * HEAD_SIZE]
            scores = nt(own_key, query) * ATT_SCALE + mask
            grown = jnp.exp(scores - jnp.max(scores, axis=0, keepdims=True))
            probs = grown * (1.0 / jnp.sum(grown, axis=0, keepdims=True))
            probs = probs.astype(BF16)
            p_out[g, 0:end, pl.ds(r * GROUP * block, GROUP * block)] = probs
            both.append(nn(value_t[g * HEAD_SIZE : (g + 1) * HEAD_SIZE, :end], probs))
        laid = jnp.transpose(jnp.concatenate(both, axis=0))
        for g in range(2):
            for j in range(GROUP):
                head_out[rows, pl.ds((g * GROUP + j) * HEAD_SIZE, HEAD_SIZE)] = laid[
                    j * block : (j + 1) * block, g * HEAD_SIZE : (g + 1) * HEAD_SIZE
                ].astype(BF16)


def attend(projected, cosine, sine, segments):
    length, cols = projected.shape
    q_cols = cols * 3 // 5
    pairs = q_cols // (2 * GROUP * HEAD_SIZE)
    wide = 2 * GROUP * HEAD_SIZE
    key_at = q_cols // 128
    return pl.pallas_call(
        attend_kernel,
        grid=(pairs,),
        in_specs=[
            pl.BlockSpec((length, wide), lambda i: (0, i)),
            pl.BlockSpec((length, 128), lambda i: (0, key_at + i)),
            pl.BlockSpec((length, 128), lambda i: (0, key_at + pairs + i)),
            pl.BlockSpec((length, 128), lambda i: (0, 0)),
            pl.BlockSpec((length, 128), lambda i: (0, 0)),
            pl.BlockSpec((length, 1), lambda i: (0, 0)),
            pl.BlockSpec((1, length), lambda i: (0, 0)),
        ],
        out_specs=[
            pl.BlockSpec((length, cols), lambda i: (0, 0)),
            pl.BlockSpec((2, length, GROUP * length), lambda i: (i, 0, 0)),
            pl.BlockSpec((length, wide), lambda i: (0, i)),
        ],
        out_shape=[
            jax.ShapeDtypeStruct((length, cols), BF16),
            jax.ShapeDtypeStruct((2 * pairs, length, GROUP * length), BF16),
            jax.ShapeDtypeStruct((length, q_cols), BF16),
        ],
        scratch_shapes=[pltpu.VMEM((length, length), F32), pltpu.VMEM((length, wide), BF16)],
        compiler_params=pltpu.CompilerParams(vmem_limit_bytes=40 * MIB),
        cost_estimate=pl.CostEstimate(
            flops=8 * pairs * GROUP * length * length * 256,
            bytes_accessed=4 * pairs * GROUP * length * length,
            transcendentals=2 * pairs * GROUP * length * length,
        ),
    )(projected, projected, projected, cosine, sine, segments[:, None], segments[None, :])


def attend_back_kernel(shards, info, q_ref, k_ref, v_ref, p_ref, w_ref, cos_ref, sin_ref, *refs):
    upstream, refs = refs[:shards], refs[shards:]
    grad_out, all_out, all_s, d_s, dq_s, dk_s, dv_s, sems = refs
    pair, pairs = pl.program_id(0), pl.num_programs(0)
    length = q_ref.shape[0]
    rows_of = length // shards

    def kept():
        return pltpu.make_async_copy(all_s, all_out, sems.at[shards])

    @pl.when(pair == 0)
    def _():
        made = [
            pltpu.make_async_copy(
                upstream[s],
                all_s.at[pl.ds(pl.multiple_of(info[2 + s] * rows_of, 16), rows_of)],
                sems.at[s],
            )
            for s in range(shards)
        ]
        for one in made:
            one.start()
        finish(made)
        kept().start()
        grads = nt(all_s[...], w_ref[...]).astype(BF16)
        for i in range(d_s.shape[0]):
            d_s[i] = grads[:, i * d_s.shape[2] : (i + 1) * d_s.shape[2]]

    @pl.when(pair == pairs - 1)
    def _():
        kept().wait()

    d_ref = d_s.at[pair]
    block = min(256, length)
    q_cols = pairs * 2 * GROUP * HEAD_SIZE
    wide = 2 * GROUP * HEAD_SIZE
    first = lax.broadcasted_iota(jnp.int32, (length, 128), 1) % HEAD_SIZE < HEAD_SIZE // 2
    key_t = jnp.transpose(k_ref[...].astype(F32)).astype(BF16)
    for r in reversed(range(length // block)):
        rows = pl.ds(r * block, block)
        end = (r + 1) * block
        both = []
        for g in range(2):
            own = pl.ds(g * HEAD_SIZE, HEAD_SIZE)
            heads = [
                pl.ds((g * GROUP + j) * HEAD_SIZE, HEAD_SIZE) for j in range(GROUP)
            ]
            query = jnp.concatenate([q_ref[rows, h] for h in heads], axis=0)
            grad = jnp.concatenate([d_ref[rows, h] for h in heads], axis=0)
            probs = p_ref[g, 0:end, pl.ds(r * GROUP * block, GROUP * block)]
            prob_grad = nt(v_ref[0:end, own], grad)
            wide_probs = probs.astype(F32)
            dots = jnp.sum(wide_probs * prob_grad, axis=0, keepdims=True)
            score_grad = (wide_probs * (prob_grad - dots)).astype(BF16)
            key_grad = nn(score_grad, query)
            value_grad = nn(probs, grad)
            if end == length:
                dk_s[0:end, own] = key_grad
                dv_s[0:end, own] = value_grad
            else:
                dk_s[0:end, own] += key_grad
                dv_s[0:end, own] += value_grad
            both.append(nn(key_t[g * HEAD_SIZE : (g + 1) * HEAD_SIZE, :end], score_grad))
        laid = jnp.transpose(jnp.concatenate(both, axis=0))
        for g in range(2):
            for j in range(GROUP):
                dq_s[rows, pl.ds((g * GROUP + j) * HEAD_SIZE, HEAD_SIZE)] = laid[
                    j * block : (j + 1) * block, g * HEAD_SIZE : (g + 1) * HEAD_SIZE
                ]
    cosine, sine = cos_ref[...] * ATT_SCALE, sin_ref[...] * -ATT_SCALE
    for c in range(wide // 128):
        at = pl.ds(c * 128, 128)
        grad_out[:, pl.ds(pl.multiple_of(pair * wide + c * 128, 128), 128)] = turn(
            dq_s[:, at], cosine, sine, first
        ).astype(BF16)
    grad_out[:, pl.ds(pl.multiple_of(q_cols + pair * 128, 128), 128)] = turn(
        dk_s[...], cosine, sine, first
    ).astype(BF16)
    grad_out[:, pl.ds(pl.multiple_of(q_cols + (pairs + pair) * 128, 128), 128)] = dv_s[
        ...
    ].astype(BF16)


def attend_back(info, qkv, probs, out_weight, cosine, sine, upstream):
    length, cols = qkv.shape
    q_cols = cols * 3 // 5
    pairs = q_cols // (2 * GROUP * HEAD_SIZE)
    wide = 2 * GROUP * HEAD_SIZE
    width = out_weight.shape[1]
    key_at = q_cols // 128
    shards = len(upstream)
    anywhere = pl.BlockSpec(memory_space=pltpu.HBM)
    return pl.pallas_call(
        partial(attend_back_kernel, shards),
        grid=(pairs,),
        in_specs=[
            pl.BlockSpec(memory_space=pltpu.SMEM),
            pl.BlockSpec((length, wide), lambda i: (0, i)),
            pl.BlockSpec((length, 128), lambda i: (0, key_at + i)),
            pl.BlockSpec((length, 128), lambda i: (0, key_at + pairs + i)),
            pl.BlockSpec((2, length, GROUP * length), lambda i: (i, 0, 0)),
            pl.BlockSpec((q_cols, width), lambda i: (0, 0)),
            pl.BlockSpec((length, 128), lambda i: (0, 0)),
            pl.BlockSpec((length, 128), lambda i: (0, 0)),
        ]
        + [anywhere] * shards,
        out_specs=[pl.BlockSpec((length, cols), lambda i: (0, 0)), anywhere],
        out_shape=[
            jax.ShapeDtypeStruct((length, cols), BF16),
            jax.ShapeDtypeStruct((length, width), BF16),
        ],
        scratch_shapes=[
            pltpu.VMEM((length, width), BF16),
            pltpu.VMEM((pairs, length, wide), BF16),
            pltpu.VMEM((length, wide), F32),
            pltpu.VMEM((length, 128), F32),
            pltpu.VMEM((length, 128), F32),
            pltpu.SemaphoreType.DMA((shards + 1,)),
        ],
        compiler_params=pltpu.CompilerParams(vmem_limit_bytes=40 * MIB),
        cost_estimate=pl.CostEstimate(
            flops=16 * pairs * GROUP * length * length * 256 + 2 * length * q_cols * width,
            bytes_accessed=4 * pairs * GROUP * length * length,
            transcendentals=0,
        ),
    )(info, qkv, qkv, qkv, probs, out_weight, cosine, sine, *upstream)


class Copies:
    def __init__(self, sems):
        self.sems, self.used = sems, 0

    def make(self, src, dst):
        made = pltpu.make_async_copy(src, dst, self.sems.at[self.used])
        self.used += 1
        return made

    def start(self, src, dst):
        made = self.make(src, dst)
        made.start()
        return made


def finish(copies):
    for made in copies:
        made.wait()


def load_weights(copies, info, refs, layout, scratch, base, cols):
    made = []
    for ref, (s, first, number, many) in zip(refs, layout):
        at = pl.ds(pl.multiple_of(info[2 + s] * many + first, 128 if cols else 16), number)
        if cols:
            made.append(copies.start(ref, scratch.at[pl.ds(base, ref.shape[0]), at]))
        else:
            made.append(copies.start(ref, scratch.at[at, pl.ds(base, ref.shape[1])]))
    return made


def expert_kernel(slots, in_layout, down_layout, info, *refs):
    parts = len(slots)
    refs = list(refs)
    take = lambda n: [refs.pop(0) for _ in range(n)]
    x_refs, d_refs = take(parts), take(parts)
    route_refs, (router_ref,) = take(parts), take(1)
    in_refs = [take(len(in_layout)), take(len(in_layout))]
    down_refs = [take(len(down_layout)), take(len(down_layout))]
    low_out, mixed_out = take(2)
    row_outs, gate_outs = take(parts), take(parts)
    (share_out,) = take(1)
    x_s, d_s, in_s, down_s, router_s, route_s, low_s, mixed_s, row_s, gate_s, pulled_s, sems = refs
    rows, width = x_refs[0].shape
    total = parts * rows
    ffe = in_s.shape[1] // 4
    tile = min(256, ffe)
    copies = Copies(sems)
    place = [pl.ds(p * rows, rows) for p in range(parts)]
    got_x = [copies.start(x_refs[p], x_s.at[place[p]]) for p in range(parts)]
    got_x.append(copies.start(router_ref, router_s))
    for p in range(parts):
        at, _, seen = slots[p]
        got_x.append(copies.start(route_refs[p].at[pl.ds(at, 16), pl.ds(0, seen)], route_s.at[p]))
    got_in, got_down = [], []
    for e in range(2):
        got_in.append(load_weights(copies, info, in_refs[e], in_layout, in_s, 2 * e * ffe, False))
        if e == 0:
            got_d = [copies.start(d_refs[p], d_s.at[place[p]]) for p in range(parts)]
        got_down.append(
            load_weights(copies, info, down_refs[e], down_layout, down_s, e * ffe, True)
        )
    lanes = lax.broadcasted_iota(jnp.int32, (rows, 128), 1)
    finish(got_x)
    bias = []
    for p in range(parts):
        first = slots[p][1]
        named = jnp.transpose(route_s[p].astype(F32))[first : first + rows].astype(jnp.int32)
        hit = named[:, 0:1] == lanes
        for k in range(1, 8):
            hit = hit | (named[:, k : k + 1] == lanes)
        bias.append(jnp.where(hit, 0.0, -1e30))
    logits = nn(x_s[...], router_s[...]) + jnp.concatenate(bias, axis=0)
    grown = jnp.exp(logits - jnp.max(logits, axis=-1, keepdims=True))
    shares = grown / jnp.sum(grown, axis=-1, keepdims=True)
    share_out[...] = shares
    lanes = lax.broadcasted_iota(jnp.int32, (total, 128), 1)
    gate_cols = jnp.zeros((total, 128), F32)
    sent = []
    for e in range(2):
        share = RES_SCALE * jnp.sum(
            jnp.where(lanes == info[e], shares, 0.0), axis=1, keepdims=True
        )
        gate_grad = jnp.zeros((total, 1), F32)
        finish(got_in[e])
        gate_s[...] = nn(x_s[...], in_s[:, pl.ds(2 * e * ffe, 2 * ffe)])
        finish((got_d if e == 0 else []) + got_down[e])
        pulled_s[...] = nt(d_s[...], down_s[pl.ds(e * ffe, ffe), :])
        for j in range(ffe // tile):
            gate_at = 2 * e * ffe + j * tile
            gate = gate_s[:, pl.ds(j * tile, tile)]
            up = gate_s[:, pl.ds(ffe + j * tile, tile)]
            pulled = pulled_s[:, pl.ds(j * tile, tile)]
            sigmoid = 0.5 * jnp.tanh(0.5 * gate) + 0.5
            swish = gate * sigmoid
            hidden = swish * up
            gate_grad = gate_grad + jnp.sum(hidden * pulled, axis=1, keepdims=True)
            hidden_grad = share * pulled
            low_s[:, pl.ds(gate_at, tile)] = (
                hidden_grad * up * (sigmoid * (1.0 + gate - swish))
            ).astype(BF16)
            low_s[:, pl.ds(gate_at + ffe, tile)] = (hidden_grad * swish).astype(BF16)
            mixed_s[:, pl.ds(e * ffe + j * tile, tile)] = (
                share * (1.0 / RES_SCALE) * hidden
            ).astype(BF16)
        gate_cols = gate_cols + jnp.where(lanes == e, RES_SCALE * gate_grad, 0.0)
    sent.append(copies.start(low_s, low_out))
    sent.append(copies.start(mixed_s, mixed_out))
    step = 768
    for n in range(width // step):
        at = pl.ds(n * step, step)
        row_s[:, at] = nt(low_s[...], in_s[at, :]).astype(BF16)
        for p in range(parts):
            sent.append(copies.start(row_s.at[place[p], at], row_outs[p].at[:, at]))
    for p in range(parts):
        gate_outs[p][...] = jnp.transpose(gate_cols[p * rows : (p + 1) * rows])[:8]
    finish(sent)


def run_experts(slots, info, x_list, d_list, routes, router, weights, layouts):
    parts = len(slots)
    rows, width = x_list[0].shape
    ffe = weights[0][0].shape[1] // 2
    total = parts * rows
    out_shape = [
        jax.ShapeDtypeStruct((total, 4 * ffe), BF16),
        jax.ShapeDtypeStruct((total, 2 * ffe), BF16),
    ]
    out_shape += [jax.ShapeDtypeStruct((rows, width), BF16)] * parts
    out_shape += [jax.ShapeDtypeStruct((8, rows), F32)] * parts
    out_shape += [jax.ShapeDtypeStruct((total, 128), F32)]
    operands = [*x_list, *d_list, *routes, router]
    for group in (weights[0], weights[2], weights[1], weights[3]):
        operands += list(group)
    here = pl.BlockSpec(memory_space=pltpu.VMEM)
    anywhere = pl.BlockSpec(memory_space=pltpu.HBM)
    copies = 3 * parts + 1 + sum(len(w) for w in weights) + 2 + parts * (width // 256)
    in_specs = [anywhere] * len(operands)
    outs = pl.pallas_call(
        partial(expert_kernel, slots, *layouts),
        in_specs=[pl.BlockSpec(memory_space=pltpu.SMEM)] + in_specs,
        out_specs=[anywhere] * (2 + parts) + [here] * (parts + 1),
        out_shape=out_shape,
        scratch_shapes=[
            pltpu.VMEM((total, width), BF16),
            pltpu.VMEM((total, width), BF16),
            pltpu.VMEM((width, 4 * ffe), BF16),
            pltpu.VMEM((2 * ffe, width), BF16),
            pltpu.VMEM((width, 128), BF16),
            pltpu.VMEM((parts, 16, slots[0][2]), BF16),
            pltpu.VMEM((total, 4 * ffe), BF16),
            pltpu.VMEM((total, 2 * ffe), BF16),
            pltpu.VMEM((total, width), BF16),
            pltpu.VMEM((total, 2 * ffe), F32),
            pltpu.VMEM((total, ffe), F32),
            pltpu.SemaphoreType.DMA((copies,)),
        ],
        compiler_params=pltpu.CompilerParams(vmem_limit_bytes=BIG_VMEM),
        cost_estimate=pl.CostEstimate(
            flops=20 * total * width * ffe,
            bytes_accessed=12 * ffe * width + 12 * total * width,
            transcendentals=total * ffe * 2,
        ),
    )(info, *operands)
    return outs[0], outs[1], outs[2 : 2 + parts], outs[2 + parts : 2 + 2 * parts], outs[-1]


def result_kernel(heights, out_heights, down_layout, info, *refs):
    refs = list(refs)
    take = lambda n: [refs.pop(0) for _ in range(n)]
    mixed_refs = take(len(heights))
    down_refs = [take(len(down_layout)), take(len(down_layout))]
    outs = take(len(out_heights))
    mixed_s, down_s, out_s, sems = refs
    ffe = down_s.shape[0] // 2
    copies = Copies(sems)
    got = [
        made
        for e in range(2)
        for made in load_weights(copies, info, down_refs[e], down_layout, down_s, e * ffe, True)
    ]
    start, waits = 0, []
    for ref, height in zip(mixed_refs, heights):
        waits.append(copies.start(ref, mixed_s.at[pl.ds(start, height)]))
        start += height
    finish(got)
    sent, start, place, at = [], 0, 0, 0
    for i, height in enumerate(heights):
        finish([waits[i]])
        rows = pl.ds(start, height)
        for n in range(down_s.shape[1] // 512):
            cols = pl.ds(n * 512, 512)
            out_s[rows, cols] = nn(mixed_s[rows, :], down_s[:, cols]).astype(BF16)
        start += height
        while place < len(outs) and at + out_heights[place] <= start:
            sent.append(copies.start(out_s.at[pl.ds(at, out_heights[place])], outs[place]))
            at += out_heights[place]
            place += 1
    finish(sent)


def run_results(info, mixeds, weights, layouts, out_heights):
    heights = [m.shape[0] for m in mixeds]
    total, cols = sum(heights), mixeds[0].shape[1]
    width = sum(number for _, _, number, _ in layouts[1])
    anywhere = pl.BlockSpec(memory_space=pltpu.HBM)
    operands = [*mixeds, *weights[1], *weights[3]]
    return pl.pallas_call(
        partial(result_kernel, heights, out_heights, layouts[1]),
        in_specs=[pl.BlockSpec(memory_space=pltpu.SMEM)] + [anywhere] * len(operands),
        out_specs=[anywhere] * len(out_heights),
        out_shape=[jax.ShapeDtypeStruct((h, width), BF16) for h in out_heights],
        scratch_shapes=[
            pltpu.VMEM((total, cols), BF16),
            pltpu.VMEM((cols, width), BF16),
            pltpu.VMEM((total, width), BF16),
            pltpu.SemaphoreType.DMA((len(operands) + len(out_heights),)),
        ],
        compiler_params=pltpu.CompilerParams(vmem_limit_bytes=BIG_VMEM),
        cost_estimate=pl.CostEstimate(
            flops=2 * total * cols * width,
            bytes_accessed=2 * (total * (cols + width) + cols * width),
            transcendentals=0,
        ),
    )(info, *operands)


def sort_gates_kernel(counts, info, *refs):
    out = refs[-1]
    for i, many in enumerate(counts):
        pieces = refs[sum(counts[:i]) : sum(counts[: i + 1])]
        at = 0
        for ref in pieces:
            cols = ref.shape[1]
            out[info[info.shape[0] - len(counts) + i], :, at : at + cols] = ref[0:2, :]
            at += cols


def sort_gates(info, parts, rows):
    flat = [ref for part in parts for ref in part]
    return pl.pallas_call(
        partial(sort_gates_kernel, [len(p) for p in parts]),
        in_specs=[pl.BlockSpec(memory_space=pltpu.SMEM)]
        + [pl.BlockSpec(memory_space=pltpu.VMEM)] * len(flat),
        out_specs=pl.BlockSpec(memory_space=pltpu.VMEM),
        out_shape=jax.ShapeDtypeStruct((len(parts), 2, rows), F32),
    )(info, *flat)


def spread_kernel(widths, kept, first, places, *refs):
    count = len(refs) - kept - 2 * len(widths) - 1
    blocks, refs = refs[:count], refs[count + kept :]
    outs, scratch, sems = refs[: len(widths)], refs[len(widths) : -1], refs[-1]
    copies, sent = Copies(sems), []
    for i, ref in enumerate(blocks):
        at = 0
        for out, buffer, wide in zip(outs, scratch, widths):
            buffer[i] = ref[:, at : at + wide].astype(F32)
            sent.append(copies.start(buffer.at[i], out.at[places[first + i]]))
            at += wide
    finish(sent)


def spread(places, first, blocks, widths, total, kept=()):
    count, height = len(blocks), blocks[0].shape[0]
    anywhere = pl.BlockSpec(memory_space=pltpu.HBM)
    return pl.pallas_call(
        partial(spread_kernel, widths, len(kept), first),
        in_specs=[pl.BlockSpec(memory_space=pltpu.SMEM)]
        + [pl.BlockSpec(memory_space=pltpu.VMEM)] * count
        + [anywhere] * len(kept),
        out_specs=[anywhere] * len(widths),
        out_shape=[jax.ShapeDtypeStruct((total, height, wide), F32) for wide in widths],
        scratch_shapes=[pltpu.VMEM((count, height, wide), F32) for wide in widths]
        + [pltpu.SemaphoreType.DMA((count * len(widths),))],
        input_output_aliases={1 + count + i: i for i in range(len(kept))},
        compiler_params=pltpu.CompilerParams(vmem_limit_bytes=40 * MIB),
    )(places, *blocks, *kept)


def weight_grad_kernel(heights, a_at, b_at, scale, by_rows, added, info, *refs):
    refs = list(refs)
    take = lambda n: [refs.pop(0) for _ in range(n)]
    a_refs, b_refs, more = take(len(heights[0])), take(len(heights[1])), take(added)
    a_s, b_s, sems = refs[-3:]
    outs = refs[:-3]
    step, steps = pl.program_id(0), pl.num_programs(0)
    tile = outs[0].shape[0 if by_rows else 1]

    def loads(parts, heights_of, scratch, at, tiled):
        made, start = [], 0
        for ref, height in zip(parts, heights_of):
            for t in range(steps_static if tiled else 1):
                wide = tile if tiled else scratch.shape[1]
                made.append(
                    (
                        t,
                        ref.at[:, pl.ds(at + t * wide, wide)],
                        scratch.at[pl.ds(start, height), pl.ds(t * wide, wide)],
                    )
                )
            start += height
        return made

    steps_static = (a_s if by_rows else b_s).shape[1] // tile
    first = loads(a_refs, heights[0], a_s, a_at, by_rows)
    second = loads(b_refs, heights[1], b_s, b_at, not by_rows)
    whole, tiled = (second, first) if by_rows else (first, second)
    tiled.sort(key=lambda entry: entry[0])
    copies = Copies(sems)
    made_whole = [copies.make(src, dst) for _, src, dst in whole]
    made_tiled = [(t, copies.make(src, dst)) for t, src, dst in tiled]

    @pl.when(step == 0)
    def _():
        for made in made_whole:
            made.start()
        for _, made in made_tiled:
            made.start()
        finish(made_whole)

    for t in range(steps_static):

        @pl.when(step == t)
        def _(t=t):
            finish([made for at, made in made_tiled if at == t])

    at = pl.ds(pl.multiple_of(step * tile, 128), tile)
    if by_rows:
        grad = tn(a_s[:, at], b_s[...])
    else:
        grad = tn(a_s[...], b_s[:, at])
    grad = scale * grad
    shards = len(outs) // (1 if by_rows else 2)
    place = lax.rem(step // (steps // shards) - info[2] + shards, shards)
    count = outs[0].shape[0]
    for i, out in enumerate(outs):
        value = grad if by_rows else grad[i // shards * count : (i // shards + 1) * count]

        @pl.when(place == i % shards)
        def _(i=i, out=out, value=value):
            if added:
                out[...] = (value + more[i][...].astype(F32)).astype(BF16)
            else:
                out[...] = value.astype(BF16)


def weight_grad(
    info, shards, a_list, a_at, a_cols, b_list, b_at, b_cols, scale=1.0, by_rows=True, more=()
):
    heights = ([a.shape[0] for a in a_list], [b.shape[0] for b in b_list])
    total = sum(heights[0])
    each = (a_cols if by_rows else b_cols) // shards
    tile = 256 if each % 256 == 0 else each
    tiles = each // tile
    shape = (each, b_cols) if by_rows else (a_cols // 2, each)
    many = shards if by_rows else 2 * shards
    anywhere = pl.BlockSpec(memory_space=pltpu.HBM)

    def tile_of(r):
        def index(i, info):
            at = jnp.clip(i - lax.rem(info[2] + r, shards) * tiles, 0, tiles - 1)
            return (at, 0) if by_rows else (0, at)

        block = (tile, b_cols) if by_rows else (a_cols // 2, tile)
        return pl.BlockSpec(block, index)

    parts_a = len(a_list) * (shards * tiles if by_rows else 1)
    parts_b = len(b_list) * (1 if by_rows else shards * tiles)
    return pl.pallas_call(
        partial(weight_grad_kernel, heights, a_at, b_at, scale, by_rows, len(more)),
        grid_spec=pltpu.PrefetchScalarGridSpec(
            num_scalar_prefetch=1,
            grid=(shards * tiles,),
            in_specs=[anywhere] * (len(a_list) + len(b_list))
            + [tile_of(r) for r in range(len(more))],
            out_specs=[tile_of(i % shards) for i in range(many)],
            scratch_shapes=[
                pltpu.VMEM((total, a_cols), BF16),
                pltpu.VMEM((total, b_cols), BF16),
                pltpu.SemaphoreType.DMA((parts_a + parts_b,)),
            ],
        ),
        out_shape=[jax.ShapeDtypeStruct(shape, BF16)] * many,
        compiler_params=pltpu.CompilerParams(vmem_limit_bytes=BIG_VMEM),
        cost_estimate=pl.CostEstimate(
            flops=2 * total * a_cols * b_cols,
            bytes_accessed=2 * (total * (a_cols + b_cols) + a_cols * b_cols),
            transcendentals=0,
        ),
    )(info, *a_list, *b_list, *more)


def dense_grad_kernel(unit, shards, small_too, info, places, *refs):
    sources, refs = refs[:2], refs[2:]
    extras, refs = (refs[:3], refs[3:]) if small_too else ((), refs)
    mine, theirs, a_s, b_s, scratch, sems = refs[:6]
    copies, sent = Copies(sems), []
    got = [copies.start(ref, to) for ref, to in zip(sources, (a_s, b_s))]
    flat = len(scratch.shape) == 2
    cols = b_s.shape[1]
    count = 2 * mine.shape[0]
    wide = mine.shape[2] // shards
    tile = 256 if flat else 384
    core = info[0] % 2
    if small_too:
        small, width = refs[6], a_s.shape[1]
        turned = jnp.transpose(
            jnp.concatenate([extras[0][...], extras[1][...], jnp.zeros((6, width), F32)], axis=0)
        )
        lanes = lax.broadcasted_iota(jnp.int32, (width, 128), 1)
        small[...] = jnp.where(
            lanes == count,
            turned[:, 0:1],
            jnp.where(lanes == count + 1, turned[:, 1:2], extras[2][...]),
        ).astype(BF16)
        if flat:
            scratch[:, cols:] = small[...]
    finish(got)
    ready = 0
    for t in range(a_s.shape[1] // tile):
        grad = tn(a_s[:, t * tile : (t + 1) * tile], b_s[...]).astype(BF16)
        if flat:
            scratch[t * tile : (t + 1) * tile, 0:cols] = grad
        while (ready + 1) * unit <= (t + 1) * tile:
            if flat:
                block = scratch.at[pl.ds(ready * unit, unit), :]
            else:
                first = ready * unit - t * tile
                scratch[ready, :, 0:cols] = grad[first : first + unit]
                if small_too:
                    scratch[ready, :, cols:] = small[ready * unit : (ready + 1) * unit, :]
                block = scratch.at[ready]
            name, turn = ready % count, ready // count
            place = places[name // 2]
            if shards > 1:
                turn = lax.rem(turn - info[2] + shards, shards)
            at = pl.ds(pl.multiple_of(turn * wide, 128), wide)
            to_mine = copies.make(block, mine.at[place, :, at])
            to_theirs = pltpu.make_async_copy(
                block, theirs.at[place, :, at], sems.at[copies.used - 1]
            )

            @pl.when(core == name % 2)
            def _(one=to_mine):
                one.start()

            @pl.when(core != name % 2)
            def _(one=to_theirs):
                one.start()

            sent.append(to_mine)
            ready += 1
    finish(sent)


def dense_grad(info, places, unit, shards, a, b, extras=()):
    length, rows = a.shape
    cols = b.shape[1]
    chips = places.shape[0]
    wide = cols + (128 if extras else 0)
    here = pl.BlockSpec(memory_space=pltpu.VMEM)
    anywhere = pl.BlockSpec(memory_space=pltpu.HBM)
    small = pl.BlockSpec(memory_space=pltpu.SMEM)
    flat = unit % 16 == 0
    many = rows // unit
    scratch = [
        pltpu.VMEM(a.shape, BF16),
        pltpu.VMEM(b.shape, BF16),
        pltpu.VMEM((rows, wide) if flat else (many, unit, wide), BF16),
        pltpu.SemaphoreType.DMA((2 + many,)),
    ]
    if extras:
        scratch.append(pltpu.VMEM((rows, 128), BF16))
    return pl.pallas_call(
        partial(dense_grad_kernel, unit, shards, bool(extras)),
        in_specs=[small] * 2 + [anywhere] * 2 + [here] * len(extras),
        out_specs=[anywhere] * 2,
        out_shape=[jax.ShapeDtypeStruct((chips, unit, shards * wide), BF16)] * 2,
        scratch_shapes=scratch,
        compiler_params=pltpu.CompilerParams(vmem_limit_bytes=BIG_VMEM),
        cost_estimate=pl.CostEstimate(
            flops=2 * length * rows * cols,
            bytes_accessed=2 * length * (rows + cols),
            transcendentals=0,
        ),
    )(info, places, a, b, *extras)


def normed_back_kernel(grads, weight, tokens, low_out, gain_out):
    grad = nt(grads[...], weight[...])
    rows = tokens[...].astype(F32)
    unit = rows * lax.rsqrt(jnp.mean(rows * rows, axis=-1, keepdims=True) + EPSILON)
    gain_out[...] = jnp.sum(grad * unit, axis=0, keepdims=True)
    low_out[...] = grad.astype(BF16)


def normed_back(grads, weight, tokens):
    length, width = tokens.shape
    here = pl.BlockSpec(memory_space=pltpu.VMEM)
    return pl.pallas_call(
        normed_back_kernel,
        in_specs=[here] * 3,
        out_specs=[here] * 2,
        out_shape=[
            jax.ShapeDtypeStruct((length, width), BF16),
            jax.ShapeDtypeStruct((1, width), F32),
        ],
        compiler_params=pltpu.CompilerParams(vmem_limit_bytes=40 * MIB),
        cost_estimate=pl.CostEstimate(
            flops=2 * length * width * grads.shape[1],
            bytes_accessed=2 * (grads.size + weight.size + 2 * tokens.size),
            transcendentals=0,
        ),
    )(grads, weight, tokens)


def project_kernel(shards, q_cols, k_cols, unit, info, places, own_ref, gain_ref, *refs):
    token_refs, refs = refs[:shards], refs[shards:]
    blocks, (normed_out, cols_out, out, tokens_out, w_s, t_s, sems) = refs[:-7], refs[-7:]
    count = own_ref.shape[0]
    rows = token_refs[0].shape[0]
    copies = Copies(sems)
    shard = info[2]
    key_at, value_at = q_cols * shards, (q_cols + k_cols) * shards
    made, to = [], 0
    for s in range(shards):
        at = pl.ds(pl.multiple_of(info[2 + s] * rows, 16), rows)
        made.append(copies.start(token_refs[s], t_s.at[at]))
    for at, wide in ((0, q_cols), (key_at, k_cols), (value_at, k_cols)):
        cols = pl.ds(pl.multiple_of(at + shard * wide, 128), wide)
        made.append(
            copies.start(
                own_ref.at[:, cols],
                w_s.at[pl.ds(pl.multiple_of(shard * count, 16), count), pl.ds(to, wide)],
            )
        )
        to += wide
    for i, ref in enumerate(blocks):
        at = pl.ds(pl.multiple_of(places[i] * unit, 16), unit)
        made.append(copies.start(ref.at[pl.ds(0, unit)], w_s.at[at]))
    finish(made[:shards])
    value = t_s[...].astype(F32)
    normed_out[...] = (
        value
        * lax.rsqrt(jnp.mean(value * value, axis=-1, keepdims=True) + EPSILON)
        * gain_ref[...]
    ).astype(BF16)
    finish(made[shards:])
    sent = [copies.start(w_s, cols_out), copies.start(t_s, tokens_out)]
    out[...] = nn(normed_out[...], w_s[...])
    finish(sent)


def project(info, places, own, gain, tokens, blocks, shards, q_cols, k_cols, unit):
    rows, width = tokens[0].shape
    cols = q_cols + 2 * k_cols
    anywhere = pl.BlockSpec(memory_space=pltpu.HBM)
    here = pl.BlockSpec(memory_space=pltpu.VMEM)
    small = pl.BlockSpec(memory_space=pltpu.SMEM)
    return pl.pallas_call(
        partial(project_kernel, shards, q_cols, k_cols, unit),
        in_specs=[small, small, anywhere, here] + [anywhere] * (shards + len(blocks)),
        out_specs=[here, anywhere, here, anywhere],
        out_shape=[
            jax.ShapeDtypeStruct((shards * rows, width), BF16),
            jax.ShapeDtypeStruct((width, cols), BF16),
            jax.ShapeDtypeStruct((shards * rows, cols), F32),
            jax.ShapeDtypeStruct((shards * rows, width), BF16),
        ],
        scratch_shapes=[
            pltpu.VMEM((width, cols), BF16),
            pltpu.VMEM((shards * rows, width), BF16),
            pltpu.SemaphoreType.DMA((shards + 5 + len(blocks),)),
        ],
        compiler_params=pltpu.CompilerParams(vmem_limit_bytes=BIG_VMEM),
        cost_estimate=pl.CostEstimate(
            flops=2 * shards * rows * width * cols,
            bytes_accessed=2 * (width * cols + shards * rows * (2 * width + 2 * cols)),
            transcendentals=0,
        ),
    )(info, places, own, gain, *tokens, *blocks)


def router_back_kernel(experts, info, gate_ref, share_ref, second_ref, router_ref, grad_ref, add_ref):
    core = info[0] % 2
    rows = second_ref.shape[0]
    turned = jnp.transpose(
        jnp.concatenate([gate_ref[c] for c in range(experts // 2)], axis=0)
    )
    kept = jnp.concatenate([turned, jnp.zeros((rows, 128 - experts), F32)], axis=1)
    lanes = lax.broadcasted_iota(jnp.int32, (rows, 128), 1)
    swapped = jnp.where(lanes % 2 == 0, pltpu.roll(kept, 127, 1), pltpu.roll(kept, 1, 1))
    gates = jnp.where(core == 0, kept, swapped)
    share = share_ref[...]
    dot = jnp.sum(share * gates, axis=1, keepdims=True)
    low = (share * (gates - dot)).astype(BF16)
    grad_ref[...] = tn(second_ref[...], low)
    add_ref[...] = nt(low, router_ref[...])


def router_back(info, gates, shares, second, router, experts):
    rows, width = second.shape
    here = pl.BlockSpec(memory_space=pltpu.VMEM)
    return pl.pallas_call(
        partial(router_back_kernel, experts),
        in_specs=[pl.BlockSpec(memory_space=pltpu.SMEM)] + [here] * 4,
        out_specs=[here] * 2,
        out_shape=[
            jax.ShapeDtypeStruct((width, 128), F32),
            jax.ShapeDtypeStruct((rows, width), F32),
        ],
        compiler_params=pltpu.CompilerParams(vmem_limit_bytes=16 * MIB),
    )(info, gates, shares, second, router)


def middle_back_kernel(own, right, left, add, middle, gain, upstream, low_out, grad_out, gain_out):
    grad = own[...].astype(F32) + right[...].astype(F32) + left[...].astype(F32) + add[...]
    rows = middle[...]
    scale = lax.rsqrt(jnp.mean(rows * rows, axis=-1, keepdims=True) + EPSILON)
    unit = rows * scale
    share = jnp.sum(grad * unit, axis=0, keepdims=True)
    gain_out[...] = share + jnp.where(pl.program_id(0) == 0, 0.0, gain_out[...])
    weighted = grad * gain[...]
    dot = jnp.mean(weighted * unit, axis=-1, keepdims=True)
    total = upstream[...].astype(F32) + scale * (weighted - unit * dot)
    grad_out[...] = total
    low_out[...] = (RES_SCALE * total).astype(BF16)


def middle_back(own, right, left, add, middle, gain, upstream):
    rows, width = middle.shape
    block = rows // 4
    some = pl.BlockSpec((block, width), lambda i: (i, 0))
    one = pl.BlockSpec((1, width), lambda i: (0, 0))
    return pl.pallas_call(
        middle_back_kernel,
        grid=(4,),
        in_specs=[some] * 5 + [one, some],
        out_specs=[some, some, one],
        out_shape=[
            jax.ShapeDtypeStruct((rows, width), BF16),
            jax.ShapeDtypeStruct((rows, width), F32),
            jax.ShapeDtypeStruct((1, width), F32),
        ],
        compiler_params=pltpu.CompilerParams(vmem_limit_bytes=BIG_VMEM),
    )(own, right, left, add, middle, gain, upstream)


def ring_add_kernel(right, left, front, back, *outs):
    half = right.shape[0]
    if half < front.shape[0]:
        right_out, left_out = outs
        right_out[:half] = add_low(right[...], front[:half])
        right_out[half:] = front[half:]
        left_out[:half] = back[:half]
        left_out[half:] = add_low(left[...], back[half:])
        return
    for came, own, places in ((right, front, outs[: len(outs) // 2]), (left, back, outs[len(outs) // 2 :])):
        at = 0
        for out in places:
            rows = out.shape[0]
            out[...] = add_low(came[at : at + rows], own[at : at + rows])
            at += rows


def add_both(right, left, front, back, halved=False):
    here = pl.BlockSpec(memory_space=pltpu.VMEM)
    rows, width = front.shape
    shapes = [(rows // 2, width)] * 4 if halved else [(rows, width)] * 2
    return pl.pallas_call(
        ring_add_kernel,
        in_specs=[here] * 4,
        out_specs=[here] * len(shapes),
        out_shape=[jax.ShapeDtypeStruct(shape, front.dtype) for shape in shapes],
        compiler_params=pltpu.CompilerParams(vmem_limit_bytes=16 * MIB),
        cost_estimate=pl.CostEstimate(flops=1, bytes_accessed=12 * front.size, transcendentals=0),
    )(right, left, front, back)


def sum_blocks_kernel(plan, starts, *refs):
    arrays, refs = refs[: 2 * len(starts)], refs[2 * len(starts) :]
    many = len(plan)
    total = sum(len(came) for _, _, _, came in plan)
    refs, outs, (scratch, sems) = refs[:total], refs[total : total + many], refs[-2:]
    copies = Copies(sems)
    made = []
    for i, (place, low, high, _) in enumerate(plan):
        made.append([])
        for start, pair in zip(starts, (arrays[k : k + 2] for k in range(0, len(arrays), 2))):
            first, last = max(low, start), min(high, start + pair[0].shape[2])
            if first >= last:
                continue
            for j, ref in enumerate(pair):
                made[-1].append(
                    copies.start(
                        ref.at[place, :, pl.ds(first - start, last - first)],
                        scratch.at[2 * i + j, :, pl.ds(first - low, last - first)],
                    )
                )
    at = 0
    for i, (_, low, high, came) in enumerate(plan):
        finish(made[i])
        wide = high - low
        value = scratch[2 * i, :, :wide].astype(F32) + scratch[2 * i + 1, :, :wide].astype(F32)
        outs[i][...] = value.astype(BF16)
        for start, stop in came:
            part = value[:, start - low : stop - low] + refs[at][...].astype(F32)
            at += 1
            if (start, stop) == (low, high):
                value = part
            outs[i][:, start - low : stop - low] = part.astype(BF16)


def sum_blocks(pairs, wanted):
    unit = pairs[0][0].shape[1]
    starts = [sum(p[0].shape[2] for p in pairs[:i]) for i in range(len(pairs))]
    every = sum(p[0].shape[2] for p in pairs)
    plan, flat = [], []
    for place, low, high, came in wanted:
        plan.append((place, low, high, [(at, at + c.shape[1]) for at, c in came]))
        flat += [c for _, c in came]
    anywhere = pl.BlockSpec(memory_space=pltpu.HBM)
    here = pl.BlockSpec(memory_space=pltpu.VMEM)
    arrays = [array for pair in pairs for array in pair]
    return pl.pallas_call(
        partial(sum_blocks_kernel, plan, starts),
        in_specs=[anywhere] * len(arrays) + [here] * len(flat),
        out_specs=[here] * len(plan),
        out_shape=[jax.ShapeDtypeStruct((unit, high - low), BF16) for _, low, high, _ in plan],
        scratch_shapes=[
            pltpu.VMEM((2 * len(plan), unit, every), BF16),
            pltpu.SemaphoreType.DMA((len(arrays) * len(plan),)),
        ],
        compiler_params=pltpu.CompilerParams(vmem_limit_bytes=16 * MIB),
        cost_estimate=pl.CostEstimate(
            flops=1, bytes_accessed=6 * len(plan) * unit * every, transcendentals=0
        ),
    )(*arrays, *flat)


def body(
    tokens,
    segment_ids,
    routes,
    norm1_gain,
    norm2_gain,
    qkv_weight,
    out_weight,
    route_weight,
    expert_in,
    expert_down,
    cotangent,
):
    rows, width = tokens.shape
    shards = lax.axis_size("shard")
    chips = lax.axis_size("chip")
    experts = 2 * chips
    length = rows * shards
    q_cols = QUERY_HEADS // shards * HEAD_SIZE
    k_cols = KEY_VALUE_HEADS // shards * HEAD_SIZE
    own_cols = q_cols + 2 * k_cols
    query_width = QUERY_HEADS * HEAD_SIZE
    pair_width = KEY_VALUE_HEADS * HEAD_SIZE
    ffe = expert_down.shape[1]
    cut = width // shards
    shard = lax.axis_index("shard")
    core = lax.axis_index("core")
    chip = lax.axis_index("chip")
    walk = ring_chips(chips)
    ahead = [(walk[i], walk[(i + 1) % chips]) for i in range(chips)]
    behind = [(b, a) for a, b in ahead]
    half_ring = chips // 2
    order = [0]
    for step in range(1, half_ring):
        order += [-step, step]
    order.append(half_ring)
    place_of = {c: i for i, c in enumerate(walk)}
    chip_tables = np.array([[walk[(place_of[c] + o) % chips] for o in order] for c in range(chips)])
    senders = jnp.asarray(chip_tables, jnp.int32)[chip]
    info = jnp.concatenate(
        [
            jnp.stack([2 * chip + core, 2 * chip + 1 - core]),
            (shard - jnp.arange(shards) + shards) % shards,
            senders,
        ]
    ).astype(jnp.int32)
    slot_of = lambda i: 2 + shards + i
    both_cores = jnp.concatenate([2 * senders + core, 2 * senders + 1 - core])
    rel_tables = np.array([[list(row).index(c) for c in range(chips)] for row in chip_tables])
    chip_places = jnp.asarray(rel_tables, jnp.int32)[chip]

    def to_shard(value, step):
        return lax.ppermute(value, "shard", [(i, (i + step) % shards) for i in range(shards)])

    def to_core(value):
        return lax.ppermute(value, "core", [(0, 1), (1, 0)])

    def in_order(pieces):
        out = []
        for j in range(shards):
            value = pieces[0]
            for s in range(1, shards):
                value = jnp.where((shard - j + shards) % shards == s, pieces[s], value)
            out.append(value)
        return out

    def exchange_shards(piece_for):
        got = [piece_for(shard)]
        for s in range(1, shards):
            got.append(to_shard(piece_for(lax.rem(shard + s, shards)), s))
        return got

    def sum_shards(piece_for):
        got = exchange_shards(piece_for)
        total = got[0].astype(F32)
        for piece in got[1:]:
            total = total + piece.astype(F32)
        return total

    def to_holders(parts):
        return [parts[0]] + [to_shard(parts[s], s) for s in range(1, shards)]

    def ring_step(pair, cut_far=False):
        right, left = pair
        if cut_far:
            right, left = right[: rows // 2], left[rows // 2 :]
        return lax.ppermute(right, "chip", ahead), lax.ppermute(left, "chip", behind)

    def ring_gather(value):
        out, pair = [value], (value, value)
        for step in range(1, half_ring + 1):
            pair = ring_step(pair, step == half_ring)
            out += pair
        return out

    def ring_start(parts):
        return lax.ppermute(parts[-2], "chip", ahead), lax.ppermute(parts[-1], "chip", behind)

    def ring_add(parts, step, got):
        return tuple(add_both(*got, parts[2 * step], parts[2 * step - 1]))

    def ring_send(sent):
        return lax.ppermute(sent[0], "chip", ahead), lax.ppermute(sent[1], "chip", behind)

    def ring_end(parts, got):
        return parts[0].astype(F32) + got[0].astype(F32) + got[1].astype(F32)

    def plane_gather(value, beside, use_early):
        right = left = value
        got = [value]
        half = value.shape[1] // 256 * 128
        for step in range(1, half_ring + 1):
            if step > 1:
                right, left, beside[step] = lax.optimization_barrier(
                    (right, left, beside.get(step, ()))
                )
            if step == half_ring:
                right, left = right[:, :half], left[:, half:]
            right = lax.ppermute(right, "chip", ahead)
            left = lax.ppermute(left, "chip", behind)
            if step < half_ring:
                got += [right, left]
        early = 2 * half_ring - 3
        used = use_early(got[:early] + [to_core(v) for v in got[:early]])
        right, left, used = lax.optimization_barrier((right, left, used))
        late = got[early:] + [jnp.concatenate([right, left], axis=1)]
        return used, late + [to_core(v) for v in late]

    def block_ring(values, beside):
        right = left = values
        got = [values]
        for step in range(1, half_ring + 1):
            if step > 1:
                right, left, beside = lax.optimization_barrier(
                    (right, left, beside)
                ) if step == 3 else (*lax.optimization_barrier((right, left)), beside)
            right = [lax.ppermute(v, "chip", ahead) for v in right]
            got.append(right)
            if step < half_ring:
                left = [lax.ppermute(v, "chip", behind) for v in left]
                got.append(left)
        return got + [[to_core(v) for v in values] for values in got], beside

    def own_columns(rows_at, count, target):
        return jnp.concatenate(
            [
                lax.dynamic_slice(qkv_weight, (rows_at, at + target * cols), (count, cols))
                for at, cols in (
                    (0, q_cols),
                    (query_width, k_cols),
                    (query_width + pair_width, k_cols),
                )
            ],
            axis=1,
        )

    unit = cut // experts
    name = 2 * chip + core
    units = [
        to_shard(own_columns(name * unit, unit, lax.rem(shard + s, shards)), s)
        for s in range(1, shards)
    ]
    tokens_got = [tokens] + [to_shard(tokens, s) for s in range(1, shards)]
    extras = jnp.concatenate(
        [norm1_gain, norm2_gain, segment_ids.astype(BF16), route_weight.reshape(-1)]
    ).reshape(-1, 256)
    extras = [extras] + [to_shard(extras, s) for s in range(1, shards)]
    named = jnp.pad(routes.T.astype(BF16), ((0, 16 - routes.shape[1]), (0, own_cols - rows)))
    together = unit % 16 == 0
    if together:
        units[0] = jnp.concatenate([units[0], named], axis=0)
    else:
        units.append(named)
    blocks, (tokens_got, extras) = block_ring(units, (tokens_got, extras))

    held_in, held_down = tie((expert_in[0], expert_down[0]), tokens_got)
    down_own = [held_down] + [to_shard(held_down, s) for s in range(1, shards)]
    in_own = [held_in] + [to_shard(held_in, s) for s in range(1, shards)]
    layouts = ([(s, 0, cut, cut) for s in range(shards)],) * 2
    extras = jnp.stack(in_order(extras)).reshape(shards, -1)
    gain_one = extras[:, :cut].reshape(1, -1).astype(F32)
    gain_two = extras[:, cut : 2 * cut].reshape(1, -1).astype(F32)
    segments = extras[:, 2 * cut : 2 * cut + rows].reshape(-1).astype(F32)
    router = extras[:, 2 * cut + rows :].reshape(width, experts)
    router_wide = jnp.pad(router, ((0, 0), (0, 128 - experts)))

    inverse = jnp.power(ROPE_BASE, -(jnp.arange(HEAD_SIZE // 2) * 2.0 / HEAD_SIZE))
    angles = jnp.arange(length).astype(F32)[:, None] * inverse[None, :]
    cosine = jnp.concatenate([jnp.cos(angles)] * 4, axis=1)
    sine = jnp.concatenate([-jnp.sin(angles), jnp.sin(angles)] * 2, axis=1)
    ready = (gain_one, gain_two, segments, router_wide, cosine, sine)
    blocks, down_own, upstream, ready = lax.optimization_barrier(
        (blocks, down_own, cotangent, ready)
    )
    gain_one, gain_two, segments, router_wide, cosine, sine = ready
    dy_pair = ring_step((upstream, upstream))
    upstream_chunks = [cotangent, *dy_pair]
    named_chunks = [b[0 if together else -1] for b in blocks[:chips]]
    named_at = unit if together else 0
    block_list = [b[s] for s in range(shards - 1) for b in blocks]
    block_places = jnp.concatenate(
        [info[2 + s] * experts + both_cores for s in range(1, shards)]
    ).astype(jnp.int32)
    inputs = tokens.astype(F32)
    if together:
        normed, qkv_cols, projected, all_tokens = project(
            info, block_places, qkv_weight, gain_one, tokens_got, block_list, shards, q_cols, k_cols, unit
        )
    else:
        placed = jnp.zeros((shards * experts, unit, own_cols), BF16)
        for i, piece in enumerate(block_list):
            placed = lax.dynamic_update_index_in_dim(placed, piece, block_places[i], 0)
        qkv_cols = lax.dynamic_update_slice(
            placed.reshape(width, own_cols), own_columns(0, cut, shard), (shard * cut, 0)
        )
        all_tokens = jnp.concatenate(in_order(tokens_got), axis=0)
        wide_tokens = all_tokens.astype(F32)
        normed = (wide_tokens * rms_scale(wide_tokens) * gain_one).astype(BF16)
        projected = nn(normed, qkv_cols)
    projected, dy_pair = lax.optimization_barrier((projected, dy_pair))
    dy_pair = ring_step(dy_pair)
    upstream_chunks += dy_pair
    qkv, probs, head_out = attend(projected, cosine, sine, segments)
    branch = nn(head_out, out_weight).astype(BF16)
    branch, in_own, dy_pair = lax.optimization_barrier((branch, in_own, dy_pair))
    dy_pair = ring_step(dy_pair)
    upstream_chunks += dy_pair
    rows_of = lambda value, j: lax.dynamic_slice(value, (j * rows, 0), (rows, value.shape[1]))
    middle = inputs + RES_SCALE * sum_shards(lambda j: rows_of(branch, j))
    middle, dy_pair = lax.optimization_barrier((middle, dy_pair))
    weights = [in_own, down_own, [to_core(w) for w in in_own], [to_core(w) for w in down_own]]
    scale_two = rms_scale(middle)
    second = (middle * scale_two * gain_two).astype(BF16)

    second_chunks, pair = [second], (second, second)
    dy_hops = 3
    row_parts, gate_parts, lows, mixeds = [], [], [], []
    for step in range(half_ring + 1):
        first = max(0, 2 * step - 1)
        picks = list(range(first, len(second_chunks)))
        if step < half_ring:
            pair = ring_step(pair, step == half_ring - 1)
            second_chunks += pair
        far = step == half_ring
        slots = [(named_at, 0, rows)] * len(picks)
        if step == half_ring:
            slots = [(named_at, 0, rows), (named_at, rows // 2, rows)]
        low, mixed, row, gate, shares = run_experts(
            slots,
            info,
            [second_chunks[i] for i in picks],
            [upstream_chunks[i] for i in picks],
            [named_chunks[min(i, chips - 1)] for i in picks],
            router_wide,
            weights,
            layouts,
        )
        if step == 0:
            own_shares = shares
        if not far:
            pair, low, dy_pair = lax.optimization_barrier((pair, low, dy_pair))
            second_chunks[-2:] = pair
            last = dy_hops == half_ring - 1
            if dy_hops < half_ring and (not last or step == half_ring - 2):
                dy_hops += 1
                dy_pair = ring_step(tie(dy_pair, pair), last)
                upstream_chunks += dy_pair
        lows.append(low)
        mixeds.append(mixed)
        row_parts += row
        gate_parts += [gate] if far else [[g] for g in gate]

    def make_in(sent, at, more=()):
        return weight_grad(
            info, shards, second_chunks, 0, width, tie(lows, sent), at, 2 * ffe, more=more
        )

    got = ring_start(row_parts)
    made = make_in((), 2 * ffe)
    got, made = lax.optimization_barrier((got, made))
    in_other = [to_core(piece) for piece in made]
    for hop, step in enumerate(range(half_ring - 1, 0, -1)):
        sent = ring_add(row_parts, step, got)
        got = ring_send(sent)
        if hop == 0:
            in_parts = make_in(sent, 0, in_other)
            got, in_parts = lax.optimization_barrier((got, in_parts))
            in_got = to_holders(in_parts)
        if hop == 1:
            out_parts = run_results(
                info, tie(mixeds, sent), weights, layouts, [p.shape[0] for p in row_parts]
            )
            gate_home = sort_gates(info, tie(gate_parts, sent), rows)
            gate_home = lax.all_to_all(
                gate_home, "chip", split_axis=0, concat_axis=0, tiled=True
            )
            got, out_parts, gate_home = lax.optimization_barrier((got, out_parts, gate_home))
        if hop == 2:
            router_add = router_back(
                info, tie(gate_home, sent), own_shares, second, router_wide, experts
            )
            down_parts = weight_grad(
                info,
                shards,
                tie(mixeds, (sent, router_add)),
                0,
                2 * ffe,
                upstream_chunks,
                0,
                width,
                RES_SCALE,
                by_rows=False,
            )
            got, down_parts = lax.optimization_barrier((got, down_parts))
    grad_route, router_add = router_add
    out_got = ring_start(tie(out_parts, got))
    attn_low, middle_grads, grad_gain_two = middle_back(
        row_parts[0], *got, router_add, middle, gain_two, cotangent
    )
    attn_low, out_got = lax.optimization_barrier((attn_low, out_got))
    attn_low, in_got = lax.optimization_barrier((attn_low, in_got))

    low = lambda value: value.astype(BF16)
    got = ring_send(ring_add(out_parts, half_ring - 1, out_got))
    attn_got = [attn_low] + [to_shard(attn_low, s) for s in range(1, shards)]
    down_other = [to_core(piece) for piece in tie(down_parts[shards:], attn_low)]
    down_parts = [add_low(a, b) for a, b in zip(down_parts[:shards], down_other)]
    attn_got, got, down_parts = lax.optimization_barrier((attn_got, got, down_parts))
    if half_ring > 2:
        got = ring_send(ring_add(out_parts, half_ring - 2, got))

    down_got = to_holders(down_parts)
    projected_grads, attn_grads = attend_back(info, qkv, probs, out_weight, cosine, sine, attn_got)
    normed_low, grad_gain_one = normed_back(projected_grads, qkv_cols, all_tokens)
    got, normed_low, grad_gain_one, down_got = lax.optimization_barrier(
        (got, normed_low, grad_gain_one, down_got)
    )
    for step in range(half_ring - 3, 0, -1):
        sent = ring_add(out_parts, step, got)
        projected_grads, sent = lax.optimization_barrier((projected_grads, sent))
        got = ring_send(sent)
    normed_got = exchange_shards(lambda j: rows_of(normed_low, j))

    mine_qkv, theirs_qkv = dense_grad(
        info, chip_places, unit, shards, normed, projected_grads, (grad_gain_one, grad_gain_two, grad_route)
    )
    mine_out, theirs_out = dense_grad(
        info, chip_places, unit, 1, head_out, tie(attn_grads, mine_qkv)
    )
    wide = own_cols + 128
    theirs_qkv = to_core(theirs_qkv)
    theirs_out = to_core(theirs_out)
    mine_out, got = lax.optimization_barrier((mine_out, got))
    pairs = ((mine_qkv, theirs_qkv), (mine_out, theirs_out))
    every = mine_qkv.shape[2] + mine_out.shape[2]
    half = every // 256 * 128
    right, left = sum_blocks(pairs, [(chips - 1, 0, half, []), (chips - 1, half, every, [])])
    right, left = lax.ppermute(right, "chip", ahead), lax.ppermute(left, "chip", behind)
    right, left = lax.optimization_barrier((right, left))
    for hop, step in enumerate(range(half_ring - 1, 0, -1)):
        right, left = sum_blocks(
            pairs,
            [
                (2 * step, 0, every, [(0, right)]),
                (2 * step - 1, 0, every, [(every - left.shape[1], left)]),
            ],
        )
        right = lax.ppermute(right, "chip", ahead)
        left = lax.ppermute(left, "chip", behind)
        right, left = lax.optimization_barrier((right, left))
        if step == half_ring - 2:
            right, left, normed_got = lax.optimization_barrier((right, left, normed_got))
    (dense,) = sum_blocks(pairs, [(0, 0, every, [(0, right), (0, left)])])
    mixed = in_order(
        [dense[:, :wide]]
        + [to_shard(dense[:, s * wide : (s + 1) * wide], s) for s in range(1, shards)]
    )
    merged = jnp.concatenate(
        [g[:, :q_cols] for g in mixed]
        + [g[:, q_cols : q_cols + k_cols] for g in mixed]
        + [g[:, q_cols + k_cols : own_cols] for g in mixed]
        + [low(sum(g[:, own_cols:].astype(F32) for g in mixed)), dense[:, shards * wide :]],
        axis=1,
    )

    total = lambda pieces: sum(p.astype(F32) for p in pieces)
    input_grads = rms_back(inputs, rms_scale(inputs), gain_one, total(normed_got))
    grad_tokens = middle_grads + input_grads
    grad_down, grad_in = total(down_got), total(in_got)

    block_out = low(middle + RES_SCALE * ring_end(out_parts, got))
    beside = {2: block_out, half_ring - 1: grad_tokens, half_ring: (grad_down, grad_in)}
    all_cols = query_width + 2 * pair_width
    widths = [all_cols, 128, width]
    cores = jnp.split(both_cores.astype(jnp.int32), 2)
    count = 2 * half_ring - 3
    places = jnp.concatenate([c[:count] for c in cores] + [c[count:] for c in cores])
    spread_out, late = plane_gather(
        merged, beside, lambda early: spread(places, 0, early, widths, experts)
    )
    block_out, grad_tokens = beside[2], beside[half_ring - 1]
    grad_down, grad_in = beside[half_ring]
    spread_out = spread(places, 2 * count, late, widths, experts, spread_out)
    grad_qkv, small, grad_out = [out.reshape(-1, out.shape[-1]) for out in spread_out]
    return (
        block_out,
        grad_tokens,
        small[:, experts],
        small[:, experts + 1],
        grad_qkv,
        grad_out,
        small[:, :experts],
        grad_in[None],
        grad_down[None],
    )


def solution(mesh):
    chips = mesh.shape["expert"] // 2
    grid = Mesh(
        mesh.devices.reshape(chips, 2, mesh.shape["shard"]), ("chip", "core", "shard")
    )
    expert = ("chip", "core")
    every = ("chip", "core", "shard")
    in_specs = (
        P(every, None),
        P(every),
        P(every, None),
        P("shard"),
        P("shard"),
        P("shard", None),
        P("shard", None),
        P("shard", None),
        P(expert, "shard", None),
        P(expert, None, "shard"),
        P(every, None),
    )
    out_specs = (
        P(every, None),
        P(every, None),
        P("shard"),
        P("shard"),
        P("shard", None),
        P("shard", None),
        P("shard", None),
        P(expert, "shard", None),
        P(expert, None, "shard"),
    )
    return jax.shard_map(body, mesh=grid, in_specs=in_specs, out_specs=out_specs, check_vma=False)
```

```python
from functools import partial

import jax
import jax.numpy as jnp
import numpy as np
from jax import lax
from jax.experimental import pallas as pl
from jax.experimental.pallas import tpu as pltpu
from jax.sharding import Mesh, PartitionSpec as P

QUERY_HEADS = 24
KEY_VALUE_HEADS = 8
HEAD_SIZE = 64
GROUP = QUERY_HEADS // KEY_VALUE_HEADS
RES_SCALE = 0.22
ATT_SCALE = 0.015625
EPSILON = 1e-06
ROPE_BASE = 10000.0
MASKED = -1000000000.0
F32 = jnp.float32
BF16 = jnp.bfloat16
MIB = 1024 * 1024
BIG_VMEM = 60 * MIB


def mm(a, b, dims):
    return lax.dot_general(a, b, (dims, ((), ())), preferred_element_type=F32)


def nn(a, b):
    return mm(a, b, ((1,), (0,)))


def nt(a, b):
    return mm(a, b, ((1,), (1,)))


def tn(a, b):
    return mm(a, b, ((0,), (0,)))


def tie(values, after):
    return lax.optimization_barrier((values, after))[0]


def ring_chips(chips):
    depth = 4 if chips % 4 == 0 else 2
    width = max(1, chips // depth)
    walk = [(z, 0) for z in range(depth)]
    for z in reversed(range(depth)):
        line = range(1, width) if (depth - 1 - z) % 2 == 0 else reversed(range(1, width))
        walk += [(z, x) for x in line]
    return [z * width + x for z, x in walk]


def add_low(a, b):
    return (a.astype(F32) + b.astype(F32)).astype(BF16)


def rms_scale(rows):
    return lax.rsqrt(jnp.mean(rows * rows, axis=-1, keepdims=True) + EPSILON)


def rms_back(rows, scale, gain, grad):
    weighted = grad * gain
    dot = jnp.mean(weighted * rows, axis=-1, keepdims=True)
    return scale * weighted - rows * (scale * scale * scale * dot)


def turn(value, cosine, sine, first):
    swapped = jnp.where(first, pltpu.roll(value, 96, 1), pltpu.roll(value, 32, 1))
    return value * cosine + swapped * sine


def attend_kernel(
    q_ref, k_ref, v_ref, cos_ref, sin_ref, seg_col, seg_row, qkv_out, p_out, head_out, bias, turned
):
    pair, pairs = pl.program_id(0), pl.num_programs(0)
    length = q_ref.shape[0]
    block = min(256, length)
    q_cols = pairs * 2 * GROUP * HEAD_SIZE
    wide = 2 * GROUP * HEAD_SIZE
    first = lax.broadcasted_iota(jnp.int32, (length, 128), 1) % HEAD_SIZE < HEAD_SIZE // 2

    @pl.when(pair == 0)
    def _():
        keys = lax.broadcasted_iota(jnp.int32, (length, length), 0)
        rows = lax.broadcasted_iota(jnp.int32, (length, length), 1)
        allowed = (seg_col[...] == seg_row[...]) & (keys <= rows)
        bias[...] = jnp.where(allowed, 0.0, MASKED)

    cosine, sine = cos_ref[...], sin_ref[...]
    for c in range(wide // 128):
        at = pl.ds(c * 128, 128)
        turned[:, at] = turn(q_ref[:, at], cosine, sine, first).astype(BF16)
    key = turn(k_ref[...], cosine, sine, first).astype(BF16)
    value = v_ref[...].astype(BF16)
    qkv_out[:, pl.ds(pl.multiple_of(pair * wide, 128), wide)] = turned[...]
    qkv_out[:, pl.ds(pl.multiple_of(q_cols + pair * 128, 128), 128)] = key
    qkv_out[:, pl.ds(pl.multiple_of(q_cols + (pairs + pair) * 128, 128), 128)] = value
    value_t = jnp.transpose(v_ref[...]).astype(BF16)
    for r in range(length // block):
        rows = pl.ds(r * block, block)
        end = (r + 1) * block
        mask = bias[0:end, rows]
        mask = jnp.concatenate([mask] * GROUP, axis=1)
        both = []
        for g in range(2):
            query = jnp.concatenate(
                [
                    turned[rows, pl.ds((g * GROUP + j) * HEAD_SIZE, HEAD_SIZE)]
                    for j in range(GROUP)
                ],
                axis=0,
            )
            own_key = key[:end, g * HEAD_SIZE : (g + 1) * HEAD_SIZE]
            scores = nt(own_key, query) * ATT_SCALE + mask
            grown = jnp.exp(scores - jnp.max(scores, axis=0, keepdims=True))
            probs = grown * (1.0 / jnp.sum(grown, axis=0, keepdims=True))
            probs = probs.astype(BF16)
            p_out[g, 0:end, pl.ds(r * GROUP * block, GROUP * block)] = probs
            both.append(nn(value_t[g * HEAD_SIZE : (g + 1) * HEAD_SIZE, :end], probs))
        laid = jnp.transpose(jnp.concatenate(both, axis=0))
        for g in range(2):
            for j in range(GROUP):
                head_out[rows, pl.ds((g * GROUP + j) * HEAD_SIZE, HEAD_SIZE)] = laid[
                    j * block : (j + 1) * block, g * HEAD_SIZE : (g + 1) * HEAD_SIZE
                ].astype(BF16)


def attend(projected, cosine, sine, segments):
    length, cols = projected.shape
    q_cols = cols * 3 // 5
    pairs = q_cols // (2 * GROUP * HEAD_SIZE)
    wide = 2 * GROUP * HEAD_SIZE
    key_at = q_cols // 128
    return pl.pallas_call(
        attend_kernel,
        grid=(pairs,),
        in_specs=[
            pl.BlockSpec((length, wide), lambda i: (0, i)),
            pl.BlockSpec((length, 128), lambda i: (0, key_at + i)),
            pl.BlockSpec((length, 128), lambda i: (0, key_at + pairs + i)),
            pl.BlockSpec((length, 128), lambda i: (0, 0)),
            pl.BlockSpec((length, 128), lambda i: (0, 0)),
            pl.BlockSpec((length, 1), lambda i: (0, 0)),
            pl.BlockSpec((1, length), lambda i: (0, 0)),
        ],
        out_specs=[
            pl.BlockSpec((length, cols), lambda i: (0, 0)),
            pl.BlockSpec((2, length, GROUP * length), lambda i: (i, 0, 0)),
            pl.BlockSpec((length, wide), lambda i: (0, i)),
        ],
        out_shape=[
            jax.ShapeDtypeStruct((length, cols), BF16),
            jax.ShapeDtypeStruct((2 * pairs, length, GROUP * length), BF16),
            jax.ShapeDtypeStruct((length, q_cols), BF16),
        ],
        scratch_shapes=[pltpu.VMEM((length, length), F32), pltpu.VMEM((length, wide), BF16)],
        compiler_params=pltpu.CompilerParams(vmem_limit_bytes=40 * MIB),
        cost_estimate=pl.CostEstimate(
            flops=8 * pairs * GROUP * length * length * 256,
            bytes_accessed=4 * pairs * GROUP * length * length,
            transcendentals=2 * pairs * GROUP * length * length,
        ),
    )(projected, projected, projected, cosine, sine, segments[:, None], segments[None, :])


def attend_back_kernel(shards, info, q_ref, k_ref, v_ref, p_ref, w_ref, cos_ref, sin_ref, *refs):
    upstream, refs = refs[:shards], refs[shards:]
    grad_out, all_out, all_s, d_s, dq_s, dk_s, dv_s, sems = refs
    pair, pairs = pl.program_id(0), pl.num_programs(0)
    length = q_ref.shape[0]
    rows_of = length // shards

    def kept():
        return pltpu.make_async_copy(all_s, all_out, sems.at[shards])

    @pl.when(pair == 0)
    def _():
        made = [
            pltpu.make_async_copy(
                upstream[s],
                all_s.at[pl.ds(pl.multiple_of(info[2 + s] * rows_of, 16), rows_of)],
                sems.at[s],
            )
            for s in range(shards)
        ]
        for one in made:
            one.start()
        finish(made)
        kept().start()
        grads = nt(all_s[...], w_ref[...]).astype(BF16)
        for i in range(d_s.shape[0]):
            d_s[i] = grads[:, i * d_s.shape[2] : (i + 1) * d_s.shape[2]]

    @pl.when(pair == pairs - 1)
    def _():
        kept().wait()

    d_ref = d_s.at[pair]
    block = min(256, length)
    q_cols = pairs * 2 * GROUP * HEAD_SIZE
    wide = 2 * GROUP * HEAD_SIZE
    first = lax.broadcasted_iota(jnp.int32, (length, 128), 1) % HEAD_SIZE < HEAD_SIZE // 2
    key_t = jnp.transpose(k_ref[...].astype(F32)).astype(BF16)
    for r in reversed(range(length // block)):
        rows = pl.ds(r * block, block)
        end = (r + 1) * block
        both = []
        for g in range(2):
            own = pl.ds(g * HEAD_SIZE, HEAD_SIZE)
            heads = [
                pl.ds((g * GROUP + j) * HEAD_SIZE, HEAD_SIZE) for j in range(GROUP)
            ]
            query = jnp.concatenate([q_ref[rows, h] for h in heads], axis=0)
            grad = jnp.concatenate([d_ref[rows, h] for h in heads], axis=0)
            probs = p_ref[g, 0:end, pl.ds(r * GROUP * block, GROUP * block)]
            prob_grad = nt(v_ref[0:end, own], grad)
            wide_probs = probs.astype(F32)
            dots = jnp.sum(wide_probs * prob_grad, axis=0, keepdims=True)
            score_grad = (wide_probs * (prob_grad - dots)).astype(BF16)
            key_grad = nn(score_grad, query)
            value_grad = nn(probs, grad)
            if end == length:
                dk_s[0:end, own] = key_grad
                dv_s[0:end, own] = value_grad
            else:
                dk_s[0:end, own] += key_grad
                dv_s[0:end, own] += value_grad
            both.append(nn(key_t[g * HEAD_SIZE : (g + 1) * HEAD_SIZE, :end], score_grad))
        laid = jnp.transpose(jnp.concatenate(both, axis=0))
        for g in range(2):
            for j in range(GROUP):
                dq_s[rows, pl.ds((g * GROUP + j) * HEAD_SIZE, HEAD_SIZE)] = laid[
                    j * block : (j + 1) * block, g * HEAD_SIZE : (g + 1) * HEAD_SIZE
                ]
    cosine, sine = cos_ref[...] * ATT_SCALE, sin_ref[...] * -ATT_SCALE
    for c in range(wide // 128):
        at = pl.ds(c * 128, 128)
        grad_out[:, pl.ds(pl.multiple_of(pair * wide + c * 128, 128), 128)] = turn(
            dq_s[:, at], cosine, sine, first
        ).astype(BF16)
    grad_out[:, pl.ds(pl.multiple_of(q_cols + pair * 128, 128), 128)] = turn(
        dk_s[...], cosine, sine, first
    ).astype(BF16)
    grad_out[:, pl.ds(pl.multiple_of(q_cols + (pairs + pair) * 128, 128), 128)] = dv_s[
        ...
    ].astype(BF16)


def attend_back(info, qkv, probs, out_weight, cosine, sine, upstream):
    length, cols = qkv.shape
    q_cols = cols * 3 // 5
    pairs = q_cols // (2 * GROUP * HEAD_SIZE)
    wide = 2 * GROUP * HEAD_SIZE
    width = out_weight.shape[1]
    key_at = q_cols // 128
    shards = len(upstream)
    anywhere = pl.BlockSpec(memory_space=pltpu.HBM)
    return pl.pallas_call(
        partial(attend_back_kernel, shards),
        grid=(pairs,),
        in_specs=[
            pl.BlockSpec(memory_space=pltpu.SMEM),
            pl.BlockSpec((length, wide), lambda i: (0, i)),
            pl.BlockSpec((length, 128), lambda i: (0, key_at + i)),
            pl.BlockSpec((length, 128), lambda i: (0, key_at + pairs + i)),
            pl.BlockSpec((2, length, GROUP * length), lambda i: (i, 0, 0)),
            pl.BlockSpec((q_cols, width), lambda i: (0, 0)),
            pl.BlockSpec((length, 128), lambda i: (0, 0)),
            pl.BlockSpec((length, 128), lambda i: (0, 0)),
        ]
        + [anywhere] * shards,
        out_specs=[pl.BlockSpec((length, cols), lambda i: (0, 0)), anywhere],
        out_shape=[
            jax.ShapeDtypeStruct((length, cols), BF16),
            jax.ShapeDtypeStruct((length, width), BF16),
        ],
        scratch_shapes=[
            pltpu.VMEM((length, width), BF16),
            pltpu.VMEM((pairs, length, wide), BF16),
            pltpu.VMEM((length, wide), F32),
            pltpu.VMEM((length, 128), F32),
            pltpu.VMEM((length, 128), F32),
            pltpu.SemaphoreType.DMA((shards + 1,)),
        ],
        compiler_params=pltpu.CompilerParams(vmem_limit_bytes=40 * MIB),
        cost_estimate=pl.CostEstimate(
            flops=16 * pairs * GROUP * length * length * 256 + 2 * length * q_cols * width,
            bytes_accessed=4 * pairs * GROUP * length * length,
            transcendentals=0,
        ),
    )(info, qkv, qkv, qkv, probs, out_weight, cosine, sine, *upstream)


class Copies:
    def __init__(self, sems):
        self.sems, self.used = sems, 0

    def make(self, src, dst):
        made = pltpu.make_async_copy(src, dst, self.sems.at[self.used])
        self.used += 1
        return made

    def start(self, src, dst):
        made = self.make(src, dst)
        made.start()
        return made


def finish(copies):
    for made in copies:
        made.wait()


def load_weights(copies, info, refs, layout, scratch, base, cols):
    made = []
    for ref, (s, first, number, many) in zip(refs, layout):
        at = pl.ds(pl.multiple_of(info[2 + s] * many + first, 128 if cols else 16), number)
        if cols:
            made.append(copies.start(ref, scratch.at[pl.ds(base, ref.shape[0]), at]))
        else:
            made.append(copies.start(ref, scratch.at[at, pl.ds(base, ref.shape[1])]))
    return made


def expert_kernel(slots, in_layout, down_layout, info, *refs):
    parts = len(slots)
    refs = list(refs)
    take = lambda n: [refs.pop(0) for _ in range(n)]
    x_refs, d_refs = take(parts), take(parts)
    route_refs, (router_ref,) = take(parts), take(1)
    in_refs = [take(len(in_layout)), take(len(in_layout))]
    down_refs = [take(len(down_layout)), take(len(down_layout))]
    low_out, mixed_out = take(2)
    row_outs, gate_outs = take(parts), take(parts)
    (share_out,) = take(1)
    x_s, d_s, in_s, down_s, router_s, route_s, low_s, mixed_s, row_s, gate_s, pulled_s, sems = refs
    rows, width = x_refs[0].shape
    total = parts * rows
    ffe = in_s.shape[1] // 4
    tile = min(256, ffe)
    copies = Copies(sems)
    place = [pl.ds(p * rows, rows) for p in range(parts)]
    got_x = [copies.start(x_refs[p], x_s.at[place[p]]) for p in range(parts)]
    got_x.append(copies.start(router_ref, router_s))
    for p in range(parts):
        at, _, seen = slots[p]
        got_x.append(copies.start(route_refs[p].at[pl.ds(at, 16), pl.ds(0, seen)], route_s.at[p]))
    got_in, got_down = [], []
    for e in range(2):
        got_in.append(load_weights(copies, info, in_refs[e], in_layout, in_s, 2 * e * ffe, False))
        if e == 0:
            got_d = [copies.start(d_refs[p], d_s.at[place[p]]) for p in range(parts)]
        got_down.append(
            load_weights(copies, info, down_refs[e], down_layout, down_s, e * ffe, True)
        )
    lanes = lax.broadcasted_iota(jnp.int32, (rows, 128), 1)
    finish(got_x)
    bias = []
    for p in range(parts):
        first = slots[p][1]
        named = jnp.transpose(route_s[p].astype(F32))[first : first + rows].astype(jnp.int32)
        hit = named[:, 0:1] == lanes
        for k in range(1, 8):
            hit = hit | (named[:, k : k + 1] == lanes)
        bias.append(jnp.where(hit, 0.0, -1e30))
    logits = nn(x_s[...], router_s[...]) + jnp.concatenate(bias, axis=0)
    grown = jnp.exp(logits - jnp.max(logits, axis=-1, keepdims=True))
    shares = grown / jnp.sum(grown, axis=-1, keepdims=True)
    share_out[...] = shares
    lanes = lax.broadcasted_iota(jnp.int32, (total, 128), 1)
    gate_cols = jnp.zeros((total, 128), F32)
    sent = []
    for e in range(2):
        share = RES_SCALE * jnp.sum(
            jnp.where(lanes == info[e], shares, 0.0), axis=1, keepdims=True
        )
        gate_grad = jnp.zeros((total, 1), F32)
        finish(got_in[e])
        gate_s[...] = nn(x_s[...], in_s[:, pl.ds(2 * e * ffe, 2 * ffe)])
        finish((got_d if e == 0 else []) + got_down[e])
        pulled_s[...] = nt(d_s[...], down_s[pl.ds(e * ffe, ffe), :])
        for j in range(ffe // tile):
            gate_at = 2 * e * ffe + j * tile
            gate = gate_s[:, pl.ds(j * tile, tile)]
            up = gate_s[:, pl.ds(ffe + j * tile, tile)]
            pulled = pulled_s[:, pl.ds(j * tile, tile)]
            sigmoid = 0.5 * jnp.tanh(0.5 * gate) + 0.5
            swish = gate * sigmoid
            hidden = swish * up
            gate_grad = gate_grad + jnp.sum(hidden * pulled, axis=1, keepdims=True)
            hidden_grad = share * pulled
            low_s[:, pl.ds(gate_at, tile)] = (
                hidden_grad * up * (sigmoid * (1.0 + gate - swish))
            ).astype(BF16)
            low_s[:, pl.ds(gate_at + ffe, tile)] = (hidden_grad * swish).astype(BF16)
            mixed_s[:, pl.ds(e * ffe + j * tile, tile)] = (
                share * (1.0 / RES_SCALE) * hidden
            ).astype(BF16)
        gate_cols = gate_cols + jnp.where(lanes == e, RES_SCALE * gate_grad, 0.0)
    sent.append(copies.start(low_s, low_out))
    sent.append(copies.start(mixed_s, mixed_out))
    step = 768
    for n in range(width // step):
        at = pl.ds(n * step, step)
        row_s[:, at] = nt(low_s[...], in_s[at, :]).astype(BF16)
        for p in range(parts):
            sent.append(copies.start(row_s.at[place[p], at], row_outs[p].at[:, at]))
    for p in range(parts):
        gate_outs[p][...] = jnp.transpose(gate_cols[p * rows : (p + 1) * rows])[:8]
    finish(sent)


def run_experts(slots, info, x_list, d_list, routes, router, weights, layouts):
    parts = len(slots)
    rows, width = x_list[0].shape
    ffe = weights[0][0].shape[1] // 2
    total = parts * rows
    out_shape = [
        jax.ShapeDtypeStruct((total, 4 * ffe), BF16),
        jax.ShapeDtypeStruct((total, 2 * ffe), BF16),
    ]
    out_shape += [jax.ShapeDtypeStruct((rows, width), BF16)] * parts
    out_shape += [jax.ShapeDtypeStruct((8, rows), F32)] * parts
    out_shape += [jax.ShapeDtypeStruct((total, 128), F32)]
    operands = [*x_list, *d_list, *routes, router]
    for group in (weights[0], weights[2], weights[1], weights[3]):
        operands += list(group)
    here = pl.BlockSpec(memory_space=pltpu.VMEM)
    anywhere = pl.BlockSpec(memory_space=pltpu.HBM)
    copies = 3 * parts + 1 + sum(len(w) for w in weights) + 2 + parts * (width // 256)
    in_specs = [anywhere] * len(operands)
    outs = pl.pallas_call(
        partial(expert_kernel, slots, *layouts),
        in_specs=[pl.BlockSpec(memory_space=pltpu.SMEM)] + in_specs,
        out_specs=[anywhere] * (2 + parts) + [here] * (parts + 1),
        out_shape=out_shape,
        scratch_shapes=[
            pltpu.VMEM((total, width), BF16),
            pltpu.VMEM((total, width), BF16),
            pltpu.VMEM((width, 4 * ffe), BF16),
            pltpu.VMEM((2 * ffe, width), BF16),
            pltpu.VMEM((width, 128), BF16),
            pltpu.VMEM((parts, 16, slots[0][2]), BF16),
            pltpu.VMEM((total, 4 * ffe), BF16),
            pltpu.VMEM((total, 2 * ffe), BF16),
            pltpu.VMEM((total, width), BF16),
            pltpu.VMEM((total, 2 * ffe), F32),
            pltpu.VMEM((total, ffe), F32),
            pltpu.SemaphoreType.DMA((copies,)),
        ],
        compiler_params=pltpu.CompilerParams(vmem_limit_bytes=BIG_VMEM),
        cost_estimate=pl.CostEstimate(
            flops=20 * total * width * ffe,
            bytes_accessed=12 * ffe * width + 12 * total * width,
            transcendentals=total * ffe * 2,
        ),
    )(info, *operands)
    return outs[0], outs[1], outs[2 : 2 + parts], outs[2 + parts : 2 + 2 * parts], outs[-1]


def result_kernel(heights, out_heights, down_layout, info, *refs):
    refs = list(refs)
    take = lambda n: [refs.pop(0) for _ in range(n)]
    mixed_refs = take(len(heights))
    down_refs = [take(len(down_layout)), take(len(down_layout))]
    outs = take(len(out_heights))
    mixed_s, down_s, out_s, sems = refs
    ffe = down_s.shape[0] // 2
    copies = Copies(sems)
    got = [
        made
        for e in range(2)
        for made in load_weights(copies, info, down_refs[e], down_layout, down_s, e * ffe, True)
    ]
    start, waits = 0, []
    for ref, height in zip(mixed_refs, heights):
        waits.append(copies.start(ref, mixed_s.at[pl.ds(start, height)]))
        start += height
    finish(got)
    sent, start, place, at = [], 0, 0, 0
    for i, height in enumerate(heights):
        finish([waits[i]])
        rows = pl.ds(start, height)
        for n in range(down_s.shape[1] // 512):
            cols = pl.ds(n * 512, 512)
            out_s[rows, cols] = nn(mixed_s[rows, :], down_s[:, cols]).astype(BF16)
        start += height
        while place < len(outs) and at + out_heights[place] <= start:
            sent.append(copies.start(out_s.at[pl.ds(at, out_heights[place])], outs[place]))
            at += out_heights[place]
            place += 1
    finish(sent)


def run_results(info, mixeds, weights, layouts, out_heights):
    heights = [m.shape[0] for m in mixeds]
    total, cols = sum(heights), mixeds[0].shape[1]
    width = sum(number for _, _, number, _ in layouts[1])
    anywhere = pl.BlockSpec(memory_space=pltpu.HBM)
    operands = [*mixeds, *weights[1], *weights[3]]
    return pl.pallas_call(
        partial(result_kernel, heights, out_heights, layouts[1]),
        in_specs=[pl.BlockSpec(memory_space=pltpu.SMEM)] + [anywhere] * len(operands),
        out_specs=[anywhere] * len(out_heights),
        out_shape=[jax.ShapeDtypeStruct((h, width), BF16) for h in out_heights],
        scratch_shapes=[
            pltpu.VMEM((total, cols), BF16),
            pltpu.VMEM((cols, width), BF16),
            pltpu.VMEM((total, width), BF16),
            pltpu.SemaphoreType.DMA((len(operands) + len(out_heights),)),
        ],
        compiler_params=pltpu.CompilerParams(vmem_limit_bytes=BIG_VMEM),
        cost_estimate=pl.CostEstimate(
            flops=2 * total * cols * width,
            bytes_accessed=2 * (total * (cols + width) + cols * width),
            transcendentals=0,
        ),
    )(info, *operands)


def sort_gates_kernel(counts, info, *refs):
    out = refs[-1]
    for i, many in enumerate(counts):
        pieces = refs[sum(counts[:i]) : sum(counts[: i + 1])]
        at = 0
        for ref in pieces:
            cols = ref.shape[1]
            out[info[info.shape[0] - len(counts) + i], :, at : at + cols] = ref[0:2, :]
            at += cols


def sort_gates(info, parts, rows):
    flat = [ref for part in parts for ref in part]
    return pl.pallas_call(
        partial(sort_gates_kernel, [len(p) for p in parts]),
        in_specs=[pl.BlockSpec(memory_space=pltpu.SMEM)]
        + [pl.BlockSpec(memory_space=pltpu.VMEM)] * len(flat),
        out_specs=pl.BlockSpec(memory_space=pltpu.VMEM),
        out_shape=jax.ShapeDtypeStruct((len(parts), 2, rows), F32),
    )(info, *flat)


def spread_kernel(widths, kept, first, places, *refs):
    count = len(refs) - kept - 2 * len(widths) - 1
    blocks, refs = refs[:count], refs[count + kept :]
    outs, scratch, sems = refs[: len(widths)], refs[len(widths) : -1], refs[-1]
    copies, sent = Copies(sems), []
    for i, ref in enumerate(blocks):
        at = 0
        for out, buffer, wide in zip(outs, scratch, widths):
            buffer[i] = ref[:, at : at + wide].astype(F32)
            sent.append(copies.start(buffer.at[i], out.at[places[first + i]]))
            at += wide
    finish(sent)


def spread(places, first, blocks, widths, total, kept=()):
    count, height = len(blocks), blocks[0].shape[0]
    anywhere = pl.BlockSpec(memory_space=pltpu.HBM)
    return pl.pallas_call(
        partial(spread_kernel, widths, len(kept), first),
        in_specs=[pl.BlockSpec(memory_space=pltpu.SMEM)]
        + [pl.BlockSpec(memory_space=pltpu.VMEM)] * count
        + [anywhere] * len(kept),
        out_specs=[anywhere] * len(widths),
        out_shape=[jax.ShapeDtypeStruct((total, height, wide), F32) for wide in widths],
        scratch_shapes=[pltpu.VMEM((count, height, wide), F32) for wide in widths]
        + [pltpu.SemaphoreType.DMA((count * len(widths),))],
        input_output_aliases={1 + count + i: i for i in range(len(kept))},
        compiler_params=pltpu.CompilerParams(vmem_limit_bytes=40 * MIB),
    )(places, *blocks, *kept)


def weight_grad_kernel(heights, a_at, b_at, scale, by_rows, added, info, *refs):
    refs = list(refs)
    take = lambda n: [refs.pop(0) for _ in range(n)]
    a_refs, b_refs, more = take(len(heights[0])), take(len(heights[1])), take(added)
    a_s, b_s, sems = refs[-3:]
    outs = refs[:-3]
    step, steps = pl.program_id(0), pl.num_programs(0)
    tile = outs[0].shape[0 if by_rows else 1]

    def loads(parts, heights_of, scratch, at, tiled):
        made, start = [], 0
        for ref, height in zip(parts, heights_of):
            for t in range(steps_static if tiled else 1):
                wide = tile if tiled else scratch.shape[1]
                made.append(
                    (
                        t,
                        ref.at[:, pl.ds(at + t * wide, wide)],
                        scratch.at[pl.ds(start, height), pl.ds(t * wide, wide)],
                    )
                )
            start += height
        return made

    steps_static = (a_s if by_rows else b_s).shape[1] // tile
    first = loads(a_refs, heights[0], a_s, a_at, by_rows)
    second = loads(b_refs, heights[1], b_s, b_at, not by_rows)
    whole, tiled = (second, first) if by_rows else (first, second)
    tiled.sort(key=lambda entry: entry[0])
    copies = Copies(sems)
    made_whole = [copies.make(src, dst) for _, src, dst in whole]
    made_tiled = [(t, copies.make(src, dst)) for t, src, dst in tiled]

    @pl.when(step == 0)
    def _():
        for made in made_whole:
            made.start()
        for _, made in made_tiled:
            made.start()
        finish(made_whole)

    for t in range(steps_static):

        @pl.when(step == t)
        def _(t=t):
            finish([made for at, made in made_tiled if at == t])

    at = pl.ds(pl.multiple_of(step * tile, 128), tile)
    if by_rows:
        grad = tn(a_s[:, at], b_s[...])
    else:
        grad = tn(a_s[...], b_s[:, at])
    grad = scale * grad
    shards = len(outs) // (1 if by_rows else 2)
    place = lax.rem(step // (steps // shards) - info[2] + shards, shards)
    count = outs[0].shape[0]
    for i, out in enumerate(outs):
        value = grad if by_rows else grad[i // shards * count : (i // shards + 1) * count]

        @pl.when(place == i % shards)
        def _(i=i, out=out, value=value):
            if added:
                out[...] = (value + more[i][...].astype(F32)).astype(BF16)
            else:
                out[...] = value.astype(BF16)


def weight_grad(
    info, shards, a_list, a_at, a_cols, b_list, b_at, b_cols, scale=1.0, by_rows=True, more=()
):
    heights = ([a.shape[0] for a in a_list], [b.shape[0] for b in b_list])
    total = sum(heights[0])
    each = (a_cols if by_rows else b_cols) // shards
    tile = 256 if each % 256 == 0 else each
    tiles = each // tile
    shape = (each, b_cols) if by_rows else (a_cols // 2, each)
    many = shards if by_rows else 2 * shards
    anywhere = pl.BlockSpec(memory_space=pltpu.HBM)

    def tile_of(r):
        def index(i, info):
            at = jnp.clip(i - lax.rem(info[2] + r, shards) * tiles, 0, tiles - 1)
            return (at, 0) if by_rows else (0, at)

        block = (tile, b_cols) if by_rows else (a_cols // 2, tile)
        return pl.BlockSpec(block, index)

    parts_a = len(a_list) * (shards * tiles if by_rows else 1)
    parts_b = len(b_list) * (1 if by_rows else shards * tiles)
    return pl.pallas_call(
        partial(weight_grad_kernel, heights, a_at, b_at, scale, by_rows, len(more)),
        grid_spec=pltpu.PrefetchScalarGridSpec(
            num_scalar_prefetch=1,
            grid=(shards * tiles,),
            in_specs=[anywhere] * (len(a_list) + len(b_list))
            + [tile_of(r) for r in range(len(more))],
            out_specs=[tile_of(i % shards) for i in range(many)],
            scratch_shapes=[
                pltpu.VMEM((total, a_cols), BF16),
                pltpu.VMEM((total, b_cols), BF16),
                pltpu.SemaphoreType.DMA((parts_a + parts_b,)),
            ],
        ),
        out_shape=[jax.ShapeDtypeStruct(shape, BF16)] * many,
        compiler_params=pltpu.CompilerParams(vmem_limit_bytes=BIG_VMEM),
        cost_estimate=pl.CostEstimate(
            flops=2 * total * a_cols * b_cols,
            bytes_accessed=2 * (total * (a_cols + b_cols) + a_cols * b_cols),
            transcendentals=0,
        ),
    )(info, *a_list, *b_list, *more)


def dense_grad_kernel(unit, shards, small_too, info, places, *refs):
    sources, refs = refs[:2], refs[2:]
    extras, refs = (refs[:3], refs[3:]) if small_too else ((), refs)
    mine, theirs, a_s, b_s, scratch, sems = refs[:6]
    copies, sent = Copies(sems), []
    got = [copies.start(ref, to) for ref, to in zip(sources, (a_s, b_s))]
    flat = len(scratch.shape) == 2
    cols = b_s.shape[1]
    count = 2 * mine.shape[0]
    wide = mine.shape[2] // shards
    tile = 256 if flat else 384
    core = info[0] % 2
    if small_too:
        small, width = refs[6], a_s.shape[1]
        turned = jnp.transpose(
            jnp.concatenate([extras[0][...], extras[1][...], jnp.zeros((6, width), F32)], axis=0)
        )
        lanes = lax.broadcasted_iota(jnp.int32, (width, 128), 1)
        small[...] = jnp.where(
            lanes == count,
            turned[:, 0:1],
            jnp.where(lanes == count + 1, turned[:, 1:2], extras[2][...]),
        ).astype(BF16)
        if flat:
            scratch[:, cols:] = small[...]
    finish(got)
    ready = 0
    for t in range(a_s.shape[1] // tile):
        grad = tn(a_s[:, t * tile : (t + 1) * tile], b_s[...]).astype(BF16)
        if flat:
            scratch[t * tile : (t + 1) * tile, 0:cols] = grad
        while (ready + 1) * unit <= (t + 1) * tile:
            if flat:
                block = scratch.at[pl.ds(ready * unit, unit), :]
            else:
                first = ready * unit - t * tile
                scratch[ready, :, 0:cols] = grad[first : first + unit]
                if small_too:
                    scratch[ready, :, cols:] = small[ready * unit : (ready + 1) * unit, :]
                block = scratch.at[ready]
            name, turn = ready % count, ready // count
            place = places[name // 2]
            if shards > 1:
                turn = lax.rem(turn - info[2] + shards, shards)
            at = pl.ds(pl.multiple_of(turn * wide, 128), wide)
            to_mine = copies.make(block, mine.at[place, :, at])
            to_theirs = pltpu.make_async_copy(
                block, theirs.at[place, :, at], sems.at[copies.used - 1]
            )

            @pl.when(core == name % 2)
            def _(one=to_mine):
                one.start()

            @pl.when(core != name % 2)
            def _(one=to_theirs):
                one.start()

            sent.append(to_mine)
            ready += 1
    finish(sent)


def dense_grad(info, places, unit, shards, a, b, extras=()):
    length, rows = a.shape
    cols = b.shape[1]
    chips = places.shape[0]
    wide = cols + (128 if extras else 0)
    here = pl.BlockSpec(memory_space=pltpu.VMEM)
    anywhere = pl.BlockSpec(memory_space=pltpu.HBM)
    small = pl.BlockSpec(memory_space=pltpu.SMEM)
    flat = unit % 16 == 0
    many = rows // unit
    scratch = [
        pltpu.VMEM(a.shape, BF16),
        pltpu.VMEM(b.shape, BF16),
        pltpu.VMEM((rows, wide) if flat else (many, unit, wide), BF16),
        pltpu.SemaphoreType.DMA((2 + many,)),
    ]
    if extras:
        scratch.append(pltpu.VMEM((rows, 128), BF16))
    return pl.pallas_call(
        partial(dense_grad_kernel, unit, shards, bool(extras)),
        in_specs=[small] * 2 + [anywhere] * 2 + [here] * len(extras),
        out_specs=[anywhere] * 2,
        out_shape=[jax.ShapeDtypeStruct((chips, unit, shards * wide), BF16)] * 2,
        scratch_shapes=scratch,
        compiler_params=pltpu.CompilerParams(vmem_limit_bytes=BIG_VMEM),
        cost_estimate=pl.CostEstimate(
            flops=6 * length * rows * cols,
            bytes_accessed=2 * length * (rows + cols),
            transcendentals=0,
        ),
    )(info, places, a, b, *extras)


def normed_back_kernel(grads, weight, tokens, low_out, gain_out):
    grad = nt(grads[...], weight[...])
    rows = tokens[...].astype(F32)
    unit = rows * lax.rsqrt(jnp.mean(rows * rows, axis=-1, keepdims=True) + EPSILON)
    gain_out[...] = jnp.sum(grad * unit, axis=0, keepdims=True)
    low_out[...] = grad.astype(BF16)


def normed_back(grads, weight, tokens):
    length, width = tokens.shape
    here = pl.BlockSpec(memory_space=pltpu.VMEM)
    return pl.pallas_call(
        normed_back_kernel,
        in_specs=[here] * 3,
        out_specs=[here] * 2,
        out_shape=[
            jax.ShapeDtypeStruct((length, width), BF16),
            jax.ShapeDtypeStruct((1, width), F32),
        ],
        compiler_params=pltpu.CompilerParams(vmem_limit_bytes=40 * MIB),
        cost_estimate=pl.CostEstimate(
            flops=2 * length * width * grads.shape[1],
            bytes_accessed=2 * (grads.size + weight.size + 2 * tokens.size),
            transcendentals=0,
        ),
    )(grads, weight, tokens)


def project_kernel(shards, q_cols, k_cols, unit, info, places, own_ref, gain_ref, *refs):
    token_refs, refs = refs[:shards], refs[shards:]
    blocks, (normed_out, cols_out, out, tokens_out, w_s, t_s, sems) = refs[:-7], refs[-7:]
    count = own_ref.shape[0]
    rows = token_refs[0].shape[0]
    copies = Copies(sems)
    shard = info[2]
    key_at, value_at = q_cols * shards, (q_cols + k_cols) * shards
    made, to = [], 0
    for s in range(shards):
        at = pl.ds(pl.multiple_of(info[2 + s] * rows, 16), rows)
        made.append(copies.start(token_refs[s], t_s.at[at]))
    for at, wide in ((0, q_cols), (key_at, k_cols), (value_at, k_cols)):
        cols = pl.ds(pl.multiple_of(at + shard * wide, 128), wide)
        made.append(
            copies.start(
                own_ref.at[:, cols],
                w_s.at[pl.ds(pl.multiple_of(shard * count, 16), count), pl.ds(to, wide)],
            )
        )
        to += wide
    for i, ref in enumerate(blocks):
        at = pl.ds(pl.multiple_of(places[i] * unit, 16), unit)
        made.append(copies.start(ref.at[pl.ds(0, unit)], w_s.at[at]))
    finish(made[:shards])
    value = t_s[...].astype(F32)
    normed_out[...] = (
        value
        * lax.rsqrt(jnp.mean(value * value, axis=-1, keepdims=True) + EPSILON)
        * gain_ref[...]
    ).astype(BF16)
    finish(made[shards:])
    sent = [copies.start(w_s, cols_out), copies.start(t_s, tokens_out)]
    out[...] = nn(normed_out[...], w_s[...])
    finish(sent)


def project(info, places, own, gain, tokens, blocks, shards, q_cols, k_cols, unit):
    rows, width = tokens[0].shape
    cols = q_cols + 2 * k_cols
    anywhere = pl.BlockSpec(memory_space=pltpu.HBM)
    here = pl.BlockSpec(memory_space=pltpu.VMEM)
    small = pl.BlockSpec(memory_space=pltpu.SMEM)
    return pl.pallas_call(
        partial(project_kernel, shards, q_cols, k_cols, unit),
        in_specs=[small, small, anywhere, here] + [anywhere] * (shards + len(blocks)),
        out_specs=[here, anywhere, here, anywhere],
        out_shape=[
            jax.ShapeDtypeStruct((shards * rows, width), BF16),
            jax.ShapeDtypeStruct((width, cols), BF16),
            jax.ShapeDtypeStruct((shards * rows, cols), F32),
            jax.ShapeDtypeStruct((shards * rows, width), BF16),
        ],
        scratch_shapes=[
            pltpu.VMEM((width, cols), BF16),
            pltpu.VMEM((shards * rows, width), BF16),
            pltpu.SemaphoreType.DMA((shards + 5 + len(blocks),)),
        ],
        compiler_params=pltpu.CompilerParams(vmem_limit_bytes=BIG_VMEM),
        cost_estimate=pl.CostEstimate(
            flops=2 * shards * rows * width * cols,
            bytes_accessed=2 * (width * cols + shards * rows * (2 * width + 2 * cols)),
            transcendentals=0,
        ),
    )(info, places, own, gain, *tokens, *blocks)


def router_back_kernel(experts, info, gate_ref, share_ref, second_ref, router_ref, grad_ref, add_ref):
    core = info[0] % 2
    rows = second_ref.shape[0]
    turned = jnp.transpose(
        jnp.concatenate([gate_ref[c] for c in range(experts // 2)], axis=0)
    )
    kept = jnp.concatenate([turned, jnp.zeros((rows, 128 - experts), F32)], axis=1)
    lanes = lax.broadcasted_iota(jnp.int32, (rows, 128), 1)
    swapped = jnp.where(lanes % 2 == 0, pltpu.roll(kept, 127, 1), pltpu.roll(kept, 1, 1))
    gates = jnp.where(core == 0, kept, swapped)
    share = share_ref[...]
    dot = jnp.sum(share * gates, axis=1, keepdims=True)
    low = (share * (gates - dot)).astype(BF16)
    grad_ref[...] = tn(second_ref[...], low)
    add_ref[...] = nt(low, router_ref[...])


def router_back(info, gates, shares, second, router, experts):
    rows, width = second.shape
    here = pl.BlockSpec(memory_space=pltpu.VMEM)
    return pl.pallas_call(
        partial(router_back_kernel, experts),
        in_specs=[pl.BlockSpec(memory_space=pltpu.SMEM)] + [here] * 4,
        out_specs=[here] * 2,
        out_shape=[
            jax.ShapeDtypeStruct((width, 128), F32),
            jax.ShapeDtypeStruct((rows, width), F32),
        ],
        compiler_params=pltpu.CompilerParams(vmem_limit_bytes=16 * MIB),
    )(info, gates, shares, second, router)


def middle_back_kernel(own, right, left, add, middle, gain, upstream, low_out, grad_out, gain_out):
    grad = own[...].astype(F32) + right[...].astype(F32) + left[...].astype(F32) + add[...]
    rows = middle[...]
    scale = lax.rsqrt(jnp.mean(rows * rows, axis=-1, keepdims=True) + EPSILON)
    unit = rows * scale
    share = jnp.sum(grad * unit, axis=0, keepdims=True)
    gain_out[...] = share + jnp.where(pl.program_id(0) == 0, 0.0, gain_out[...])
    weighted = grad * gain[...]
    dot = jnp.mean(weighted * unit, axis=-1, keepdims=True)
    total = upstream[...].astype(F32) + scale * (weighted - unit * dot)
    grad_out[...] = total
    low_out[...] = (RES_SCALE * total).astype(BF16)


def middle_back(own, right, left, add, middle, gain, upstream):
    rows, width = middle.shape
    block = rows // 4
    some = pl.BlockSpec((block, width), lambda i: (i, 0))
    one = pl.BlockSpec((1, width), lambda i: (0, 0))
    return pl.pallas_call(
        middle_back_kernel,
        grid=(4,),
        in_specs=[some] * 5 + [one, some],
        out_specs=[some, some, one],
        out_shape=[
            jax.ShapeDtypeStruct((rows, width), BF16),
            jax.ShapeDtypeStruct((rows, width), F32),
            jax.ShapeDtypeStruct((1, width), F32),
        ],
        compiler_params=pltpu.CompilerParams(vmem_limit_bytes=BIG_VMEM),
    )(own, right, left, add, middle, gain, upstream)


def ring_add_kernel(right, left, front, back, *outs):
    half = right.shape[0]
    if half < front.shape[0]:
        right_out, left_out = outs
        right_out[:half] = add_low(right[...], front[:half])
        right_out[half:] = front[half:]
        left_out[:half] = back[:half]
        left_out[half:] = add_low(left[...], back[half:])
        return
    for came, own, places in ((right, front, outs[: len(outs) // 2]), (left, back, outs[len(outs) // 2 :])):
        at = 0
        for out in places:
            rows = out.shape[0]
            out[...] = add_low(came[at : at + rows], own[at : at + rows])
            at += rows


def add_both(right, left, front, back, halved=False):
    here = pl.BlockSpec(memory_space=pltpu.VMEM)
    rows, width = front.shape
    shapes = [(rows // 2, width)] * 4 if halved else [(rows, width)] * 2
    return pl.pallas_call(
        ring_add_kernel,
        in_specs=[here] * 4,
        out_specs=[here] * len(shapes),
        out_shape=[jax.ShapeDtypeStruct(shape, front.dtype) for shape in shapes],
        compiler_params=pltpu.CompilerParams(vmem_limit_bytes=16 * MIB),
        cost_estimate=pl.CostEstimate(flops=1, bytes_accessed=12 * front.size, transcendentals=0),
    )(right, left, front, back)


def sum_blocks_kernel(plan, starts, *refs):
    arrays, refs = refs[: 2 * len(starts)], refs[2 * len(starts) :]
    many = len(plan)
    total = sum(len(came) for _, _, _, came in plan)
    refs, outs, (scratch, sems) = refs[:total], refs[total : total + many], refs[-2:]
    copies = Copies(sems)
    made = []
    for i, (place, low, high, _) in enumerate(plan):
        made.append([])
        for start, pair in zip(starts, (arrays[k : k + 2] for k in range(0, len(arrays), 2))):
            first, last = max(low, start), min(high, start + pair[0].shape[2])
            if first >= last:
                continue
            for j, ref in enumerate(pair):
                made[-1].append(
                    copies.start(
                        ref.at[place, :, pl.ds(first - start, last - first)],
                        scratch.at[2 * i + j, :, pl.ds(first - low, last - first)],
                    )
                )
    at = 0
    for i, (_, low, high, came) in enumerate(plan):
        finish(made[i])
        wide = high - low
        value = scratch[2 * i, :, :wide].astype(F32) + scratch[2 * i + 1, :, :wide].astype(F32)
        outs[i][...] = value.astype(BF16)
        for start, stop in came:
            part = value[:, start - low : stop - low] + refs[at][...].astype(F32)
            at += 1
            if (start, stop) == (low, high):
                value = part
            outs[i][:, start - low : stop - low] = part.astype(BF16)


def sum_blocks(pairs, wanted):
    unit = pairs[0][0].shape[1]
    starts = [sum(p[0].shape[2] for p in pairs[:i]) for i in range(len(pairs))]
    every = sum(p[0].shape[2] for p in pairs)
    plan, flat = [], []
    for place, low, high, came in wanted:
        plan.append((place, low, high, [(at, at + c.shape[1]) for at, c in came]))
        flat += [c for _, c in came]
    anywhere = pl.BlockSpec(memory_space=pltpu.HBM)
    here = pl.BlockSpec(memory_space=pltpu.VMEM)
    arrays = [array for pair in pairs for array in pair]
    return pl.pallas_call(
        partial(sum_blocks_kernel, plan, starts),
        in_specs=[anywhere] * len(arrays) + [here] * len(flat),
        out_specs=[here] * len(plan),
        out_shape=[jax.ShapeDtypeStruct((unit, high - low), BF16) for _, low, high, _ in plan],
        scratch_shapes=[
            pltpu.VMEM((2 * len(plan), unit, every), BF16),
            pltpu.SemaphoreType.DMA((len(arrays) * len(plan),)),
        ],
        compiler_params=pltpu.CompilerParams(vmem_limit_bytes=16 * MIB),
        cost_estimate=pl.CostEstimate(
            flops=1, bytes_accessed=6 * len(plan) * unit * every, transcendentals=0
        ),
    )(*arrays, *flat)


def body(
    tokens,
    segment_ids,
    routes,
    norm1_gain,
    norm2_gain,
    qkv_weight,
    out_weight,
    route_weight,
    expert_in,
    expert_down,
    cotangent,
):
    rows, width = tokens.shape
    shards = lax.axis_size("shard")
    chips = lax.axis_size("chip")
    experts = 2 * chips
    length = rows * shards
    q_cols = QUERY_HEADS // shards * HEAD_SIZE
    k_cols = KEY_VALUE_HEADS // shards * HEAD_SIZE
    own_cols = q_cols + 2 * k_cols
    query_width = QUERY_HEADS * HEAD_SIZE
    pair_width = KEY_VALUE_HEADS * HEAD_SIZE
    ffe = expert_down.shape[1]
    cut = width // shards
    shard = lax.axis_index("shard")
    core = lax.axis_index("core")
    chip = lax.axis_index("chip")
    walk = ring_chips(chips)
    ahead = [(walk[i], walk[(i + 1) % chips]) for i in range(chips)]
    behind = [(b, a) for a, b in ahead]
    half_ring = chips // 2
    order = [0]
    for step in range(1, half_ring):
        order += [-step, step]
    order.append(half_ring)
    place_of = {c: i for i, c in enumerate(walk)}
    chip_tables = np.array([[walk[(place_of[c] + o) % chips] for o in order] for c in range(chips)])
    senders = jnp.asarray(chip_tables, jnp.int32)[chip]
    info = jnp.concatenate(
        [
            jnp.stack([2 * chip + core, 2 * chip + 1 - core]),
            (shard - jnp.arange(shards) + shards) % shards,
            senders,
        ]
    ).astype(jnp.int32)
    slot_of = lambda i: 2 + shards + i
    both_cores = jnp.concatenate([2 * senders + core, 2 * senders + 1 - core])
    rel_tables = np.array([[list(row).index(c) for c in range(chips)] for row in chip_tables])
    chip_places = jnp.asarray(rel_tables, jnp.int32)[chip]

    def to_shard(value, step):
        return lax.ppermute(value, "shard", [(i, (i + step) % shards) for i in range(shards)])

    def to_core(value):
        return lax.ppermute(value, "core", [(0, 1), (1, 0)])

    def in_order(pieces):
        out = []
        for j in range(shards):
            value = pieces[0]
            for s in range(1, shards):
                value = jnp.where((shard - j + shards) % shards == s, pieces[s], value)
            out.append(value)
        return out

    def exchange_shards(piece_for):
        got = [piece_for(shard)]
        for s in range(1, shards):
            got.append(to_shard(piece_for(lax.rem(shard + s, shards)), s))
        return got

    def sum_shards(piece_for):
        got = exchange_shards(piece_for)
        total = got[0].astype(F32)
        for piece in got[1:]:
            total = total + piece.astype(F32)
        return total

    def to_holders(parts):
        return [parts[0]] + [to_shard(parts[s], s) for s in range(1, shards)]

    def ring_step(pair, cut_far=False):
        right, left = pair
        if cut_far:
            right, left = right[: rows // 2], left[rows // 2 :]
        return lax.ppermute(right, "chip", ahead), lax.ppermute(left, "chip", behind)

    def ring_gather(value):
        out, pair = [value], (value, value)
        for step in range(1, half_ring + 1):
            pair = ring_step(pair, step == half_ring)
            out += pair
        return out

    def ring_start(parts):
        return lax.ppermute(parts[-2], "chip", ahead), lax.ppermute(parts[-1], "chip", behind)

    def ring_add(parts, step, got):
        return tuple(add_both(*got, parts[2 * step], parts[2 * step - 1]))

    def ring_send(sent):
        return lax.ppermute(sent[0], "chip", ahead), lax.ppermute(sent[1], "chip", behind)

    def ring_end(parts, got):
        return parts[0].astype(F32) + got[0].astype(F32) + got[1].astype(F32)

    def plane_gather(value, beside, use_early):
        right = left = value
        got = [value]
        half = value.shape[1] // 256 * 128
        for step in range(1, half_ring + 1):
            if step > 1:
                right, left, beside[step] = lax.optimization_barrier(
                    (right, left, beside.get(step, ()))
                )
            if step == half_ring:
                right, left = right[:, :half], left[:, half:]
            right = lax.ppermute(right, "chip", ahead)
            left = lax.ppermute(left, "chip", behind)
            if step < half_ring:
                got += [right, left]
        early = 2 * half_ring - 3
        used = use_early(got[:early] + [to_core(v) for v in got[:early]])
        right, left, used = lax.optimization_barrier((right, left, used))
        late = got[early:] + [jnp.concatenate([right, left], axis=1)]
        return used, late + [to_core(v) for v in late]

    def block_ring(values, beside):
        right = left = values
        got = [values]
        for step in range(1, half_ring + 1):
            if step > 1:
                right, left, beside = lax.optimization_barrier(
                    (right, left, beside)
                ) if step == 3 else (*lax.optimization_barrier((right, left)), beside)
            right = [lax.ppermute(v, "chip", ahead) for v in right]
            got.append(right)
            if step < half_ring:
                left = [lax.ppermute(v, "chip", behind) for v in left]
                got.append(left)
        return got + [[to_core(v) for v in values] for values in got], beside

    def own_columns(rows_at, count, target):
        return jnp.concatenate(
            [
                lax.dynamic_slice(qkv_weight, (rows_at, at + target * cols), (count, cols))
                for at, cols in (
                    (0, q_cols),
                    (query_width, k_cols),
                    (query_width + pair_width, k_cols),
                )
            ],
            axis=1,
        )

    unit = cut // experts
    name = 2 * chip + core
    units = [
        to_shard(own_columns(name * unit, unit, lax.rem(shard + s, shards)), s)
        for s in range(1, shards)
    ]
    tokens_got = [tokens] + [to_shard(tokens, s) for s in range(1, shards)]
    extras = jnp.concatenate(
        [norm1_gain, norm2_gain, segment_ids.astype(BF16), route_weight.reshape(-1)]
    ).reshape(-1, 256)
    extras = [extras] + [to_shard(extras, s) for s in range(1, shards)]
    named = jnp.pad(routes.T.astype(BF16), ((0, 16 - routes.shape[1]), (0, own_cols - rows)))
    together = unit % 16 == 0
    if together:
        units[0] = jnp.concatenate([units[0], named], axis=0)
    else:
        units.append(named)
    blocks, (tokens_got, extras) = block_ring(units, (tokens_got, extras))

    held_in, held_down = tie((expert_in[0], expert_down[0]), tokens_got)
    down_own = [held_down] + [to_shard(held_down, s) for s in range(1, shards)]
    in_own = [held_in] + [to_shard(held_in, s) for s in range(1, shards)]
    layouts = ([(s, 0, cut, cut) for s in range(shards)],) * 2
    blocks, down_own, upstream = lax.optimization_barrier((blocks, down_own, cotangent))
    dy_pair = ring_step((upstream, upstream))
    upstream_chunks = [cotangent, *dy_pair]
    named_chunks = [b[0 if together else -1] for b in blocks[:chips]]
    named_at = unit if together else 0
    block_list = [b[s] for s in range(shards - 1) for b in blocks]
    block_places = jnp.concatenate(
        [info[2 + s] * experts + both_cores for s in range(1, shards)]
    ).astype(jnp.int32)
    extras = jnp.stack(in_order(extras)).reshape(shards, -1)
    gain_one = extras[:, :cut].reshape(1, -1).astype(F32)
    gain_two = extras[:, cut : 2 * cut].reshape(1, -1).astype(F32)
    segments = extras[:, 2 * cut : 2 * cut + rows].reshape(-1).astype(F32)
    router = extras[:, 2 * cut + rows :].reshape(width, experts)
    router_wide = jnp.pad(router, ((0, 0), (0, 128 - experts)))

    inputs = tokens.astype(F32)
    if together:
        normed, qkv_cols, projected, all_tokens = project(
            info, block_places, qkv_weight, gain_one, tokens_got, block_list, shards, q_cols, k_cols, unit
        )
    else:
        placed = jnp.zeros((shards * experts, unit, own_cols), BF16)
        for i, piece in enumerate(block_list):
            placed = lax.dynamic_update_index_in_dim(placed, piece, block_places[i], 0)
        qkv_cols = lax.dynamic_update_slice(
            placed.reshape(width, own_cols), own_columns(0, cut, shard), (shard * cut, 0)
        )
        all_tokens = jnp.concatenate(in_order(tokens_got), axis=0)
        wide_tokens = all_tokens.astype(F32)
        normed = (wide_tokens * rms_scale(wide_tokens) * gain_one).astype(BF16)
        projected = nn(normed, qkv_cols)
    places = jnp.arange(length)
    inverse = jnp.power(ROPE_BASE, -(jnp.arange(HEAD_SIZE // 2) * 2.0 / HEAD_SIZE))
    angles = places.astype(F32)[:, None] * inverse[None, :]
    cosine = jnp.concatenate([jnp.cos(angles)] * 4, axis=1)
    sine = jnp.concatenate([-jnp.sin(angles), jnp.sin(angles)] * 2, axis=1)
    projected, dy_pair = lax.optimization_barrier((projected, dy_pair))
    dy_pair = ring_step(dy_pair)
    upstream_chunks += dy_pair
    qkv, probs, head_out = attend(projected, cosine, sine, segments)
    branch = nn(head_out, out_weight).astype(BF16)
    branch, in_own, dy_pair = lax.optimization_barrier((branch, in_own, dy_pair))
    dy_pair = ring_step(dy_pair)
    upstream_chunks += dy_pair
    rows_of = lambda value, j: lax.dynamic_slice(value, (j * rows, 0), (rows, value.shape[1]))
    middle = inputs + RES_SCALE * sum_shards(lambda j: rows_of(branch, j))
    middle, dy_pair = lax.optimization_barrier((middle, dy_pair))
    weights = [in_own, down_own, [to_core(w) for w in in_own], [to_core(w) for w in down_own]]
    scale_two = rms_scale(middle)
    second = (middle * scale_two * gain_two).astype(BF16)

    second_chunks, pair = [second], (second, second)
    dy_hops = 3
    row_parts, gate_parts, lows, mixeds = [], [], [], []
    for step in range(half_ring + 1):
        first = max(0, 2 * step - 1)
        picks = list(range(first, len(second_chunks)))
        if step < half_ring:
            pair = ring_step(pair, step == half_ring - 1)
            second_chunks += pair
        far = step == half_ring
        slots = [(named_at, 0, rows)] * len(picks)
        if step == half_ring:
            slots = [(named_at, 0, rows), (named_at, rows // 2, rows)]
        low, mixed, row, gate, shares = run_experts(
            slots,
            info,
            [second_chunks[i] for i in picks],
            [upstream_chunks[i] for i in picks],
            [named_chunks[min(i, chips - 1)] for i in picks],
            router_wide,
            weights,
            layouts,
        )
        if step == 0:
            own_shares = shares
        if not far:
            pair, low, dy_pair = lax.optimization_barrier((pair, low, dy_pair))
            second_chunks[-2:] = pair
            last = dy_hops == half_ring - 1
            if dy_hops < half_ring and (not last or step == half_ring - 2):
                dy_hops += 1
                dy_pair = ring_step(tie(dy_pair, pair), last)
                upstream_chunks += dy_pair
        lows.append(low)
        mixeds.append(mixed)
        row_parts += row
        gate_parts += [gate] if far else [[g] for g in gate]

    def make_in(sent, at, more=()):
        return weight_grad(
            info, shards, second_chunks, 0, width, tie(lows, sent), at, 2 * ffe, more=more
        )

    got = ring_start(row_parts)
    made = make_in((), 2 * ffe)
    got, made = lax.optimization_barrier((got, made))
    in_other = [to_core(piece) for piece in made]
    for hop, step in enumerate(range(half_ring - 1, 0, -1)):
        sent = ring_add(row_parts, step, got)
        got = ring_send(sent)
        if hop == 0:
            in_parts = make_in(sent, 0, in_other)
            got, in_parts = lax.optimization_barrier((got, in_parts))
            in_got = to_holders(in_parts)
        if hop == 1:
            out_parts = run_results(
                info, tie(mixeds, sent), weights, layouts, [p.shape[0] for p in row_parts]
            )
            gate_home = sort_gates(info, tie(gate_parts, sent), rows)
            gate_home = lax.all_to_all(
                gate_home, "chip", split_axis=0, concat_axis=0, tiled=True
            )
            got, out_parts, gate_home = lax.optimization_barrier((got, out_parts, gate_home))
        if hop == 2:
            router_add = router_back(
                info, tie(gate_home, sent), own_shares, second, router_wide, experts
            )
            down_parts = weight_grad(
                info,
                shards,
                tie(mixeds, (sent, router_add)),
                0,
                2 * ffe,
                upstream_chunks,
                0,
                width,
                RES_SCALE,
                by_rows=False,
            )
            got, down_parts = lax.optimization_barrier((got, down_parts))
    grad_route, router_add = router_add
    out_got = ring_start(tie(out_parts, got))
    attn_low, middle_grads, grad_gain_two = middle_back(
        row_parts[0], *got, router_add, middle, gain_two, cotangent
    )
    attn_low, out_got = lax.optimization_barrier((attn_low, out_got))
    attn_low, in_got = lax.optimization_barrier((attn_low, in_got))

    low = lambda value: value.astype(BF16)
    sent = ring_add(out_parts, half_ring - 1, out_got)
    got = ring_send(sent)
    attn_got = [attn_low] + [to_shard(attn_low, s) for s in range(1, shards)]
    down_other = [to_core(piece) for piece in tie(down_parts[shards:], (attn_low, sent))]
    down_parts = [add_low(a, b) for a, b in zip(down_parts[:shards], down_other)]
    attn_got, got, down_parts = lax.optimization_barrier((attn_got, got, down_parts))
    if half_ring > 2:
        got = ring_send(ring_add(out_parts, half_ring - 2, got))

    down_got = to_holders(down_parts)
    projected_grads, attn_grads = attend_back(info, qkv, probs, out_weight, cosine, sine, attn_got)
    normed_low, grad_gain_one = normed_back(projected_grads, qkv_cols, all_tokens)
    got, normed_low, grad_gain_one, down_got = lax.optimization_barrier(
        (got, normed_low, grad_gain_one, down_got)
    )
    for step in range(half_ring - 3, 0, -1):
        sent = ring_add(out_parts, step, got)
        projected_grads, sent = lax.optimization_barrier((projected_grads, sent))
        got = ring_send(sent)

    mine_out, theirs_out = dense_grad(info, chip_places, unit, 1, head_out, attn_grads)
    theirs_out = to_core(theirs_out)
    mine_qkv, theirs_qkv = dense_grad(
        info,
        chip_places,
        unit,
        shards,
        tie(normed, mine_out),
        projected_grads,
        (grad_gain_one, grad_gain_two, grad_route),
    )
    wide = own_cols + 128
    mine_qkv, theirs_qkv, theirs_out, got = lax.optimization_barrier(
        (mine_qkv, theirs_qkv, theirs_out, got)
    )
    theirs_qkv = to_core(theirs_qkv)
    pairs = ((mine_qkv, theirs_qkv), (mine_out, theirs_out))
    every = mine_qkv.shape[2] + mine_out.shape[2]
    half = every // 256 * 128
    right, left = sum_blocks(pairs, [(chips - 1, 0, half, []), (chips - 1, half, every, [])])
    right, left = lax.ppermute(right, "chip", ahead), lax.ppermute(left, "chip", behind)
    right, left, normed_low = lax.optimization_barrier((right, left, normed_low))
    normed_got = exchange_shards(lambda j: rows_of(normed_low, j))
    for hop, step in enumerate(range(half_ring - 1, 0, -1)):
        right, left = sum_blocks(
            pairs,
            [
                (2 * step, 0, every, [(0, right)]),
                (2 * step - 1, 0, every, [(every - left.shape[1], left)]),
            ],
        )
        right = lax.ppermute(right, "chip", ahead)
        left = lax.ppermute(left, "chip", behind)
        right, left = lax.optimization_barrier((right, left))
        if step == half_ring - 2:
            right, left, normed_got = lax.optimization_barrier((right, left, normed_got))
    (dense,) = sum_blocks(pairs, [(0, 0, every, [(0, right), (0, left)])])
    mixed = in_order(
        [dense[:, :wide]]
        + [to_shard(dense[:, s * wide : (s + 1) * wide], s) for s in range(1, shards)]
    )
    merged = jnp.concatenate(
        [g[:, :q_cols] for g in mixed]
        + [g[:, q_cols : q_cols + k_cols] for g in mixed]
        + [g[:, q_cols + k_cols : own_cols] for g in mixed]
        + [low(sum(g[:, own_cols:].astype(F32) for g in mixed)), dense[:, shards * wide :]],
        axis=1,
    )

    total = lambda pieces: sum(p.astype(F32) for p in pieces)
    input_grads = rms_back(inputs, rms_scale(inputs), gain_one, total(normed_got))
    grad_tokens = middle_grads + input_grads
    grad_down, grad_in = total(down_got), total(in_got)

    block_out = low(middle + RES_SCALE * ring_end(out_parts, got))
    beside = {2: block_out, half_ring - 1: grad_tokens, half_ring: (grad_down, grad_in)}
    all_cols = query_width + 2 * pair_width
    widths = [all_cols, 128, width]
    cores = jnp.split(both_cores.astype(jnp.int32), 2)
    count = 2 * half_ring - 3
    places = jnp.concatenate([c[:count] for c in cores] + [c[count:] for c in cores])
    spread_out, late = plane_gather(
        merged, beside, lambda early: spread(places, 0, early, widths, experts)
    )
    block_out, grad_tokens = beside[2], beside[half_ring - 1]
    grad_down, grad_in = beside[half_ring]
    spread_out = spread(places, 2 * count, late, widths, experts, spread_out)
    grad_qkv, small, grad_out = [out.reshape(-1, out.shape[-1]) for out in spread_out]
    return (
        block_out,
        grad_tokens,
        small[:, experts],
        small[:, experts + 1],
        grad_qkv,
        grad_out,
        small[:, :experts],
        grad_in[None],
        grad_down[None],
    )


def solution(mesh):
    chips = mesh.shape["expert"] // 2
    grid = Mesh(
        mesh.devices.reshape(chips, 2, mesh.shape["shard"]), ("chip", "core", "shard")
    )
    expert = ("chip", "core")
    every = ("chip", "core", "shard")
    in_specs = (
        P(every, None),
        P(every),
        P(every, None),
        P("shard"),
        P("shard"),
        P("shard", None),
        P("shard", None),
        P("shard", None),
        P(expert, "shard", None),
        P(expert, None, "shard"),
        P(every, None),
    )
    out_specs = (
        P(every, None),
        P(every, None),
        P("shard"),
        P("shard"),
        P("shard", None),
        P("shard", None),
        P("shard", None),
        P(expert, "shard", None),
        P(expert, None, "shard"),
    )
    return jax.shard_map(body, mesh=grid, in_specs=in_specs, out_specs=out_specs, check_vma=False)
```

```python
from functools import partial

import jax
import jax.numpy as jnp
import numpy as np
from jax import lax
from jax.experimental import pallas as pl
from jax.experimental.pallas import tpu as pltpu
from jax.sharding import Mesh, PartitionSpec as P

QUERY_HEADS = 24
KEY_VALUE_HEADS = 8
HEAD_SIZE = 64
GROUP = QUERY_HEADS // KEY_VALUE_HEADS
RES_SCALE = 0.22
ATT_SCALE = 0.015625
EPSILON = 1e-06
ROPE_BASE = 10000.0
MASKED = -1000000000.0
F32 = jnp.float32
BF16 = jnp.bfloat16
MIB = 1024 * 1024
BIG_VMEM = 60 * MIB


def mm(a, b, dims):
    return lax.dot_general(a, b, (dims, ((), ())), preferred_element_type=F32)


def nn(a, b):
    return mm(a, b, ((1,), (0,)))


def nt(a, b):
    return mm(a, b, ((1,), (1,)))


def tn(a, b):
    return mm(a, b, ((0,), (0,)))


def tie(values, after):
    return lax.optimization_barrier((values, after))[0]


def ring_chips(chips):
    depth = 4 if chips % 4 == 0 else 2
    width = max(1, chips // depth)
    walk = [(z, 0) for z in range(depth)]
    for z in reversed(range(depth)):
        line = range(1, width) if (depth - 1 - z) % 2 == 0 else reversed(range(1, width))
        walk += [(z, x) for x in line]
    return [z * width + x for z, x in walk]


def add_low(a, b):
    return (a.astype(F32) + b.astype(F32)).astype(BF16)


def rms_scale(rows):
    return lax.rsqrt(jnp.mean(rows * rows, axis=-1, keepdims=True) + EPSILON)


def rms_back(rows, scale, gain, grad):
    weighted = grad * gain
    dot = jnp.mean(weighted * rows, axis=-1, keepdims=True)
    return scale * weighted - rows * (scale * scale * scale * dot)


def turn(value, cosine, sine, first):
    swapped = jnp.where(first, pltpu.roll(value, 96, 1), pltpu.roll(value, 32, 1))
    return value * cosine + swapped * sine


def attend_kernel(
    q_ref, k_ref, v_ref, cos_ref, sin_ref, seg_col, seg_row, qkv_out, p_out, head_out, bias, turned
):
    pair, pairs = pl.program_id(0), pl.num_programs(0)
    length = q_ref.shape[0]
    block = min(256, length)
    q_cols = pairs * 2 * GROUP * HEAD_SIZE
    wide = 2 * GROUP * HEAD_SIZE
    first = lax.broadcasted_iota(jnp.int32, (length, 128), 1) % HEAD_SIZE < HEAD_SIZE // 2

    @pl.when(pair == 0)
    def _():
        keys = lax.broadcasted_iota(jnp.int32, (length, length), 0)
        rows = lax.broadcasted_iota(jnp.int32, (length, length), 1)
        allowed = (seg_col[...] == seg_row[...]) & (keys <= rows)
        bias[...] = jnp.where(allowed, 0.0, MASKED)

    cosine, sine = cos_ref[...], sin_ref[...]
    for c in range(wide // 128):
        at = pl.ds(c * 128, 128)
        turned[:, at] = turn(q_ref[:, at], cosine, sine, first).astype(BF16)
    key = turn(k_ref[...], cosine, sine, first).astype(BF16)
    value = v_ref[...].astype(BF16)
    qkv_out[:, pl.ds(pl.multiple_of(pair * wide, 128), wide)] = turned[...]
    qkv_out[:, pl.ds(pl.multiple_of(q_cols + pair * 128, 128), 128)] = key
    qkv_out[:, pl.ds(pl.multiple_of(q_cols + (pairs + pair) * 128, 128), 128)] = value
    value_t = jnp.transpose(v_ref[...]).astype(BF16)
    for r in range(length // block):
        rows = pl.ds(r * block, block)
        end = (r + 1) * block
        mask = bias[0:end, rows]
        mask = jnp.concatenate([mask] * GROUP, axis=1)
        both = []
        for g in range(2):
            query = jnp.concatenate(
                [
                    turned[rows, pl.ds((g * GROUP + j) * HEAD_SIZE, HEAD_SIZE)]
                    for j in range(GROUP)
                ],
                axis=0,
            )
            own_key = key[:end, g * HEAD_SIZE : (g + 1) * HEAD_SIZE]
            scores = nt(own_key, query) * ATT_SCALE + mask
            grown = jnp.exp(scores - jnp.max(scores, axis=0, keepdims=True))
            probs = grown * (1.0 / jnp.sum(grown, axis=0, keepdims=True))
            probs = probs.astype(BF16)
            p_out[g, 0:end, pl.ds(r * GROUP * block, GROUP * block)] = probs
            both.append(nn(value_t[g * HEAD_SIZE : (g + 1) * HEAD_SIZE, :end], probs))
        laid = jnp.transpose(jnp.concatenate(both, axis=0))
        for g in range(2):
            for j in range(GROUP):
                head_out[rows, pl.ds((g * GROUP + j) * HEAD_SIZE, HEAD_SIZE)] = laid[
                    j * block : (j + 1) * block, g * HEAD_SIZE : (g + 1) * HEAD_SIZE
                ].astype(BF16)


def attend(projected, cosine, sine, segments):
    length, cols = projected.shape
    q_cols = cols * 3 // 5
    pairs = q_cols // (2 * GROUP * HEAD_SIZE)
    wide = 2 * GROUP * HEAD_SIZE
    key_at = q_cols // 128
    return pl.pallas_call(
        attend_kernel,
        grid=(pairs,),
        in_specs=[
            pl.BlockSpec((length, wide), lambda i: (0, i)),
            pl.BlockSpec((length, 128), lambda i: (0, key_at + i)),
            pl.BlockSpec((length, 128), lambda i: (0, key_at + pairs + i)),
            pl.BlockSpec((length, 128), lambda i: (0, 0)),
            pl.BlockSpec((length, 128), lambda i: (0, 0)),
            pl.BlockSpec((length, 1), lambda i: (0, 0)),
            pl.BlockSpec((1, length), lambda i: (0, 0)),
        ],
        out_specs=[
            pl.BlockSpec((length, cols), lambda i: (0, 0)),
            pl.BlockSpec((2, length, GROUP * length), lambda i: (i, 0, 0)),
            pl.BlockSpec((length, wide), lambda i: (0, i)),
        ],
        out_shape=[
            jax.ShapeDtypeStruct((length, cols), BF16),
            jax.ShapeDtypeStruct((2 * pairs, length, GROUP * length), BF16),
            jax.ShapeDtypeStruct((length, q_cols), BF16),
        ],
        scratch_shapes=[pltpu.VMEM((length, length), F32), pltpu.VMEM((length, wide), BF16)],
        compiler_params=pltpu.CompilerParams(vmem_limit_bytes=40 * MIB),
        cost_estimate=pl.CostEstimate(
            flops=8 * pairs * GROUP * length * length * 256,
            bytes_accessed=4 * pairs * GROUP * length * length,
            transcendentals=2 * pairs * GROUP * length * length,
        ),
    )(projected, projected, projected, cosine, sine, segments[:, None], segments[None, :])


def attend_back_kernel(shards, info, q_ref, k_ref, v_ref, p_ref, w_ref, cos_ref, sin_ref, *refs):
    upstream, refs = refs[:shards], refs[shards:]
    grad_out, all_out, all_s, d_s, dq_s, dk_s, dv_s, sems = refs
    pair, pairs = pl.program_id(0), pl.num_programs(0)
    length = q_ref.shape[0]
    rows_of = length // shards

    def kept():
        return pltpu.make_async_copy(all_s, all_out, sems.at[shards])

    @pl.when(pair == 0)
    def _():
        made = [
            pltpu.make_async_copy(
                upstream[s],
                all_s.at[pl.ds(pl.multiple_of(info[2 + s] * rows_of, 16), rows_of)],
                sems.at[s],
            )
            for s in range(shards)
        ]
        for one in made:
            one.start()
        finish(made)
        kept().start()
        grads = nt(all_s[...], w_ref[...]).astype(BF16)
        for i in range(d_s.shape[0]):
            d_s[i] = grads[:, i * d_s.shape[2] : (i + 1) * d_s.shape[2]]

    @pl.when(pair == pairs - 1)
    def _():
        kept().wait()

    d_ref = d_s.at[pair]
    block = min(256, length)
    q_cols = pairs * 2 * GROUP * HEAD_SIZE
    wide = 2 * GROUP * HEAD_SIZE
    first = lax.broadcasted_iota(jnp.int32, (length, 128), 1) % HEAD_SIZE < HEAD_SIZE // 2
    key_t = jnp.transpose(k_ref[...].astype(F32)).astype(BF16)
    for r in reversed(range(length // block)):
        rows = pl.ds(r * block, block)
        end = (r + 1) * block
        both = []
        for g in range(2):
            own = pl.ds(g * HEAD_SIZE, HEAD_SIZE)
            heads = [
                pl.ds((g * GROUP + j) * HEAD_SIZE, HEAD_SIZE) for j in range(GROUP)
            ]
            query = jnp.concatenate([q_ref[rows, h] for h in heads], axis=0)
            grad = jnp.concatenate([d_ref[rows, h] for h in heads], axis=0)
            probs = p_ref[g, 0:end, pl.ds(r * GROUP * block, GROUP * block)]
            prob_grad = nt(v_ref[0:end, own], grad)
            wide_probs = probs.astype(F32)
            dots = jnp.sum(wide_probs * prob_grad, axis=0, keepdims=True)
            score_grad = (wide_probs * (prob_grad - dots)).astype(BF16)
            key_grad = nn(score_grad, query)
            value_grad = nn(probs, grad)
            if end == length:
                dk_s[0:end, own] = key_grad
                dv_s[0:end, own] = value_grad
            else:
                dk_s[0:end, own] += key_grad
                dv_s[0:end, own] += value_grad
            both.append(nn(key_t[g * HEAD_SIZE : (g + 1) * HEAD_SIZE, :end], score_grad))
        laid = jnp.transpose(jnp.concatenate(both, axis=0))
        for g in range(2):
            for j in range(GROUP):
                dq_s[rows, pl.ds((g * GROUP + j) * HEAD_SIZE, HEAD_SIZE)] = laid[
                    j * block : (j + 1) * block, g * HEAD_SIZE : (g + 1) * HEAD_SIZE
                ]
    cosine, sine = cos_ref[...] * ATT_SCALE, sin_ref[...] * -ATT_SCALE
    for c in range(wide // 128):
        at = pl.ds(c * 128, 128)
        grad_out[:, pl.ds(pl.multiple_of(pair * wide + c * 128, 128), 128)] = turn(
            dq_s[:, at], cosine, sine, first
        ).astype(BF16)
    grad_out[:, pl.ds(pl.multiple_of(q_cols + pair * 128, 128), 128)] = turn(
        dk_s[...], cosine, sine, first
    ).astype(BF16)
    grad_out[:, pl.ds(pl.multiple_of(q_cols + (pairs + pair) * 128, 128), 128)] = dv_s[
        ...
    ].astype(BF16)


def attend_back(info, qkv, probs, out_weight, cosine, sine, upstream):
    length, cols = qkv.shape
    q_cols = cols * 3 // 5
    pairs = q_cols // (2 * GROUP * HEAD_SIZE)
    wide = 2 * GROUP * HEAD_SIZE
    width = out_weight.shape[1]
    key_at = q_cols // 128
    shards = len(upstream)
    anywhere = pl.BlockSpec(memory_space=pltpu.HBM)
    return pl.pallas_call(
        partial(attend_back_kernel, shards),
        grid=(pairs,),
        in_specs=[
            pl.BlockSpec(memory_space=pltpu.SMEM),
            pl.BlockSpec((length, wide), lambda i: (0, i)),
            pl.BlockSpec((length, 128), lambda i: (0, key_at + i)),
            pl.BlockSpec((length, 128), lambda i: (0, key_at + pairs + i)),
            pl.BlockSpec((2, length, GROUP * length), lambda i: (i, 0, 0)),
            pl.BlockSpec((q_cols, width), lambda i: (0, 0)),
            pl.BlockSpec((length, 128), lambda i: (0, 0)),
            pl.BlockSpec((length, 128), lambda i: (0, 0)),
        ]
        + [anywhere] * shards,
        out_specs=[pl.BlockSpec((length, cols), lambda i: (0, 0)), anywhere],
        out_shape=[
            jax.ShapeDtypeStruct((length, cols), BF16),
            jax.ShapeDtypeStruct((length, width), BF16),
        ],
        scratch_shapes=[
            pltpu.VMEM((length, width), BF16),
            pltpu.VMEM((pairs, length, wide), BF16),
            pltpu.VMEM((length, wide), F32),
            pltpu.VMEM((length, 128), F32),
            pltpu.VMEM((length, 128), F32),
            pltpu.SemaphoreType.DMA((shards + 1,)),
        ],
        compiler_params=pltpu.CompilerParams(vmem_limit_bytes=40 * MIB),
        cost_estimate=pl.CostEstimate(
            flops=16 * pairs * GROUP * length * length * 256 + 2 * length * q_cols * width,
            bytes_accessed=4 * pairs * GROUP * length * length,
            transcendentals=0,
        ),
    )(info, qkv, qkv, qkv, probs, out_weight, cosine, sine, *upstream)


class Copies:
    def __init__(self, sems):
        self.sems, self.used = sems, 0

    def make(self, src, dst):
        made = pltpu.make_async_copy(src, dst, self.sems.at[self.used])
        self.used += 1
        return made

    def start(self, src, dst):
        made = self.make(src, dst)
        made.start()
        return made


def finish(copies):
    for made in copies:
        made.wait()


def load_weights(copies, info, refs, layout, scratch, base, cols):
    made = []
    for ref, (s, first, number, many) in zip(refs, layout):
        at = pl.ds(pl.multiple_of(info[2 + s] * many + first, 128 if cols else 16), number)
        if cols:
            made.append(copies.start(ref, scratch.at[pl.ds(base, ref.shape[0]), at]))
        else:
            made.append(copies.start(ref, scratch.at[at, pl.ds(base, ref.shape[1])]))
    return made


def expert_kernel(slots, in_layout, down_layout, info, *refs):
    parts = len(slots)
    refs = list(refs)
    take = lambda n: [refs.pop(0) for _ in range(n)]
    x_refs, d_refs = take(parts), take(parts)
    route_refs, (router_ref,) = take(parts), take(1)
    in_refs = [take(len(in_layout)), take(len(in_layout))]
    down_refs = [take(len(down_layout)), take(len(down_layout))]
    low_out, mixed_out = take(2)
    row_outs, gate_outs = take(parts), take(parts)
    (share_out,) = take(1)
    x_s, d_s, in_s, down_s, router_s, route_s, low_s, mixed_s, row_s, gate_s, pulled_s, sems = refs
    rows, width = x_refs[0].shape
    total = parts * rows
    ffe = in_s.shape[1] // 4
    tile = min(256, ffe)
    copies = Copies(sems)
    place = [pl.ds(p * rows, rows) for p in range(parts)]
    got_x = [copies.start(x_refs[p], x_s.at[place[p]]) for p in range(parts)]
    got_x.append(copies.start(router_ref, router_s))
    for p in range(parts):
        at, _, seen = slots[p]
        got_x.append(copies.start(route_refs[p].at[pl.ds(at, 16), pl.ds(0, seen)], route_s.at[p]))
    got_in, got_down = [], []
    for e in range(2):
        got_in.append(load_weights(copies, info, in_refs[e], in_layout, in_s, 2 * e * ffe, False))
        if e == 0:
            got_d = [copies.start(d_refs[p], d_s.at[place[p]]) for p in range(parts)]
        got_down.append(
            load_weights(copies, info, down_refs[e], down_layout, down_s, e * ffe, True)
        )
    lanes = lax.broadcasted_iota(jnp.int32, (rows, 128), 1)
    finish(got_x)
    bias = []
    for p in range(parts):
        first = slots[p][1]
        named = jnp.transpose(route_s[p].astype(F32))[first : first + rows].astype(jnp.int32)
        hit = named[:, 0:1] == lanes
        for k in range(1, 8):
            hit = hit | (named[:, k : k + 1] == lanes)
        bias.append(jnp.where(hit, 0.0, -1e30))
    logits = nn(x_s[...], router_s[...]) + jnp.concatenate(bias, axis=0)
    grown = jnp.exp(logits - jnp.max(logits, axis=-1, keepdims=True))
    shares = grown / jnp.sum(grown, axis=-1, keepdims=True)
    share_out[...] = shares
    lanes = lax.broadcasted_iota(jnp.int32, (total, 128), 1)
    gate_cols = jnp.zeros((total, 128), F32)
    sent = []
    for e in range(2):
        share = RES_SCALE * jnp.sum(
            jnp.where(lanes == info[e], shares, 0.0), axis=1, keepdims=True
        )
        gate_grad = jnp.zeros((total, 1), F32)
        finish(got_in[e])
        gate_s[...] = nn(x_s[...], in_s[:, pl.ds(2 * e * ffe, 2 * ffe)])
        finish((got_d if e == 0 else []) + got_down[e])
        pulled_s[...] = nt(d_s[...], down_s[pl.ds(e * ffe, ffe), :])
        for j in range(ffe // tile):
            gate_at = 2 * e * ffe + j * tile
            gate = gate_s[:, pl.ds(j * tile, tile)]
            up = gate_s[:, pl.ds(ffe + j * tile, tile)]
            pulled = pulled_s[:, pl.ds(j * tile, tile)]
            sigmoid = 0.5 * jnp.tanh(0.5 * gate) + 0.5
            swish = gate * sigmoid
            hidden = swish * up
            gate_grad = gate_grad + jnp.sum(hidden * pulled, axis=1, keepdims=True)
            hidden_grad = share * pulled
            low_s[:, pl.ds(gate_at, tile)] = (
                hidden_grad * up * (sigmoid * (1.0 + gate - swish))
            ).astype(BF16)
            low_s[:, pl.ds(gate_at + ffe, tile)] = (hidden_grad * swish).astype(BF16)
            mixed_s[:, pl.ds(e * ffe + j * tile, tile)] = (
                share * (1.0 / RES_SCALE) * hidden
            ).astype(BF16)
        gate_cols = gate_cols + jnp.where(lanes == e, RES_SCALE * gate_grad, 0.0)
    sent.append(copies.start(low_s, low_out))
    sent.append(copies.start(mixed_s, mixed_out))
    step = 768
    for n in range(width // step):
        at = pl.ds(n * step, step)
        row_s[:, at] = nt(low_s[...], in_s[at, :]).astype(BF16)
        for p in range(parts):
            sent.append(copies.start(row_s.at[place[p], at], row_outs[p].at[:, at]))
    for p in range(parts):
        gate_outs[p][...] = jnp.transpose(gate_cols[p * rows : (p + 1) * rows])[:8]
    finish(sent)


def run_experts(slots, info, x_list, d_list, routes, router, weights, layouts):
    parts = len(slots)
    rows, width = x_list[0].shape
    ffe = weights[0][0].shape[1] // 2
    total = parts * rows
    out_shape = [
        jax.ShapeDtypeStruct((total, 4 * ffe), BF16),
        jax.ShapeDtypeStruct((total, 2 * ffe), BF16),
    ]
    out_shape += [jax.ShapeDtypeStruct((rows, width), BF16)] * parts
    out_shape += [jax.ShapeDtypeStruct((8, rows), F32)] * parts
    out_shape += [jax.ShapeDtypeStruct((total, 128), F32)]
    operands = [*x_list, *d_list, *routes, router]
    for group in (weights[0], weights[2], weights[1], weights[3]):
        operands += list(group)
    here = pl.BlockSpec(memory_space=pltpu.VMEM)
    anywhere = pl.BlockSpec(memory_space=pltpu.HBM)
    copies = 3 * parts + 1 + sum(len(w) for w in weights) + 2 + parts * (width // 256)
    in_specs = [anywhere] * len(operands)
    outs = pl.pallas_call(
        partial(expert_kernel, slots, *layouts),
        in_specs=[pl.BlockSpec(memory_space=pltpu.SMEM)] + in_specs,
        out_specs=[anywhere] * (2 + parts) + [here] * (parts + 1),
        out_shape=out_shape,
        scratch_shapes=[
            pltpu.VMEM((total, width), BF16),
            pltpu.VMEM((total, width), BF16),
            pltpu.VMEM((width, 4 * ffe), BF16),
            pltpu.VMEM((2 * ffe, width), BF16),
            pltpu.VMEM((width, 128), BF16),
            pltpu.VMEM((parts, 16, slots[0][2]), BF16),
            pltpu.VMEM((total, 4 * ffe), BF16),
            pltpu.VMEM((total, 2 * ffe), BF16),
            pltpu.VMEM((total, width), BF16),
            pltpu.VMEM((total, 2 * ffe), F32),
            pltpu.VMEM((total, ffe), F32),
            pltpu.SemaphoreType.DMA((copies,)),
        ],
        compiler_params=pltpu.CompilerParams(vmem_limit_bytes=BIG_VMEM),
        cost_estimate=pl.CostEstimate(
            flops=20 * total * width * ffe,
            bytes_accessed=12 * ffe * width + 12 * total * width,
            transcendentals=total * ffe * 2,
        ),
    )(info, *operands)
    return outs[0], outs[1], outs[2 : 2 + parts], outs[2 + parts : 2 + 2 * parts], outs[-1]


def result_kernel(heights, out_heights, down_layout, info, *refs):
    refs = list(refs)
    take = lambda n: [refs.pop(0) for _ in range(n)]
    mixed_refs = take(len(heights))
    down_refs = [take(len(down_layout)), take(len(down_layout))]
    outs = take(len(out_heights))
    mixed_s, down_s, out_s, sems = refs
    ffe = down_s.shape[0] // 2
    copies = Copies(sems)
    got = [
        made
        for e in range(2)
        for made in load_weights(copies, info, down_refs[e], down_layout, down_s, e * ffe, True)
    ]
    start, waits = 0, []
    for ref, height in zip(mixed_refs, heights):
        waits.append(copies.start(ref, mixed_s.at[pl.ds(start, height)]))
        start += height
    finish(got)
    sent, start, place, at = [], 0, 0, 0
    for i, height in enumerate(heights):
        finish([waits[i]])
        rows = pl.ds(start, height)
        for n in range(down_s.shape[1] // 512):
            cols = pl.ds(n * 512, 512)
            out_s[rows, cols] = nn(mixed_s[rows, :], down_s[:, cols]).astype(BF16)
        start += height
        while place < len(outs) and at + out_heights[place] <= start:
            sent.append(copies.start(out_s.at[pl.ds(at, out_heights[place])], outs[place]))
            at += out_heights[place]
            place += 1
    finish(sent)


def run_results(info, mixeds, weights, layouts, out_heights):
    heights = [m.shape[0] for m in mixeds]
    total, cols = sum(heights), mixeds[0].shape[1]
    width = sum(number for _, _, number, _ in layouts[1])
    anywhere = pl.BlockSpec(memory_space=pltpu.HBM)
    operands = [*mixeds, *weights[1], *weights[3]]
    return pl.pallas_call(
        partial(result_kernel, heights, out_heights, layouts[1]),
        in_specs=[pl.BlockSpec(memory_space=pltpu.SMEM)] + [anywhere] * len(operands),
        out_specs=[anywhere] * len(out_heights),
        out_shape=[jax.ShapeDtypeStruct((h, width), BF16) for h in out_heights],
        scratch_shapes=[
            pltpu.VMEM((total, cols), BF16),
            pltpu.VMEM((cols, width), BF16),
            pltpu.VMEM((total, width), BF16),
            pltpu.SemaphoreType.DMA((len(operands) + len(out_heights),)),
        ],
        compiler_params=pltpu.CompilerParams(vmem_limit_bytes=BIG_VMEM),
        cost_estimate=pl.CostEstimate(
            flops=2 * total * cols * width,
            bytes_accessed=2 * (total * (cols + width) + cols * width),
            transcendentals=0,
        ),
    )(info, *operands)


def sort_gates_kernel(counts, info, *refs):
    out = refs[-1]
    for i, many in enumerate(counts):
        pieces = refs[sum(counts[:i]) : sum(counts[: i + 1])]
        at = 0
        for ref in pieces:
            cols = ref.shape[1]
            out[info[info.shape[0] - len(counts) + i], :, at : at + cols] = ref[0:2, :]
            at += cols


def sort_gates(info, parts, rows):
    flat = [ref for part in parts for ref in part]
    return pl.pallas_call(
        partial(sort_gates_kernel, [len(p) for p in parts]),
        in_specs=[pl.BlockSpec(memory_space=pltpu.SMEM)]
        + [pl.BlockSpec(memory_space=pltpu.VMEM)] * len(flat),
        out_specs=pl.BlockSpec(memory_space=pltpu.VMEM),
        out_shape=jax.ShapeDtypeStruct((len(parts), 2, rows), F32),
    )(info, *flat)


def spread_kernel(widths, kept, first, places, *refs):
    count = len(refs) - kept - 2 * len(widths) - 1
    blocks, refs = refs[:count], refs[count + kept :]
    outs, scratch, sems = refs[: len(widths)], refs[len(widths) : -1], refs[-1]
    copies, sent = Copies(sems), []
    for i, ref in enumerate(blocks):
        at = 0
        for out, buffer, wide in zip(outs, scratch, widths):
            buffer[i] = ref[:, at : at + wide].astype(F32)
            sent.append(copies.start(buffer.at[i], out.at[places[first + i]]))
            at += wide
    finish(sent)


def spread(places, first, blocks, widths, total, kept=()):
    count, height = len(blocks), blocks[0].shape[0]
    anywhere = pl.BlockSpec(memory_space=pltpu.HBM)
    return pl.pallas_call(
        partial(spread_kernel, widths, len(kept), first),
        in_specs=[pl.BlockSpec(memory_space=pltpu.SMEM)]
        + [pl.BlockSpec(memory_space=pltpu.VMEM)] * count
        + [anywhere] * len(kept),
        out_specs=[anywhere] * len(widths),
        out_shape=[jax.ShapeDtypeStruct((total, height, wide), F32) for wide in widths],
        scratch_shapes=[pltpu.VMEM((count, height, wide), F32) for wide in widths]
        + [pltpu.SemaphoreType.DMA((count * len(widths),))],
        input_output_aliases={1 + count + i: i for i in range(len(kept))},
        compiler_params=pltpu.CompilerParams(vmem_limit_bytes=40 * MIB),
    )(places, *blocks, *kept)


def weight_grad_kernel(heights, a_at, b_at, scale, by_rows, added, info, *refs):
    refs = list(refs)
    take = lambda n: [refs.pop(0) for _ in range(n)]
    a_refs, b_refs, more = take(len(heights[0])), take(len(heights[1])), take(added)
    a_s, b_s, sems = refs[-3:]
    outs = refs[:-3]
    step, steps = pl.program_id(0), pl.num_programs(0)
    tile = outs[0].shape[0 if by_rows else 1]

    def loads(parts, heights_of, scratch, at, tiled):
        made, start = [], 0
        for ref, height in zip(parts, heights_of):
            for t in range(steps_static if tiled else 1):
                wide = tile if tiled else scratch.shape[1]
                made.append(
                    (
                        t,
                        ref.at[:, pl.ds(at + t * wide, wide)],
                        scratch.at[pl.ds(start, height), pl.ds(t * wide, wide)],
                    )
                )
            start += height
        return made

    steps_static = (a_s if by_rows else b_s).shape[1] // tile
    first = loads(a_refs, heights[0], a_s, a_at, by_rows)
    second = loads(b_refs, heights[1], b_s, b_at, not by_rows)
    whole, tiled = (second, first) if by_rows else (first, second)
    tiled.sort(key=lambda entry: entry[0])
    copies = Copies(sems)
    made_whole = [copies.make(src, dst) for _, src, dst in whole]
    made_tiled = [(t, copies.make(src, dst)) for t, src, dst in tiled]

    @pl.when(step == 0)
    def _():
        for made in made_whole:
            made.start()
        for _, made in made_tiled:
            made.start()
        finish(made_whole)

    for t in range(steps_static):

        @pl.when(step == t)
        def _(t=t):
            finish([made for at, made in made_tiled if at == t])

    at = pl.ds(pl.multiple_of(step * tile, 128), tile)
    if by_rows:
        grad = tn(a_s[:, at], b_s[...])
    else:
        grad = tn(a_s[...], b_s[:, at])
    grad = scale * grad
    shards = len(outs) // (1 if by_rows else 2)
    place = lax.rem(step // (steps // shards) - info[2] + shards, shards)
    count = outs[0].shape[0]
    for i, out in enumerate(outs):
        value = grad if by_rows else grad[i // shards * count : (i // shards + 1) * count]

        @pl.when(place == i % shards)
        def _(i=i, out=out, value=value):
            if added:
                out[...] = (value + more[i][...].astype(F32)).astype(BF16)
            else:
                out[...] = value.astype(BF16)


def weight_grad(
    info, shards, a_list, a_at, a_cols, b_list, b_at, b_cols, scale=1.0, by_rows=True, more=()
):
    heights = ([a.shape[0] for a in a_list], [b.shape[0] for b in b_list])
    total = sum(heights[0])
    each = (a_cols if by_rows else b_cols) // shards
    tile = 256 if each % 256 == 0 else each
    tiles = each // tile
    shape = (each, b_cols) if by_rows else (a_cols // 2, each)
    many = shards if by_rows else 2 * shards
    anywhere = pl.BlockSpec(memory_space=pltpu.HBM)

    def tile_of(r):
        def index(i, info):
            at = jnp.clip(i - lax.rem(info[2] + r, shards) * tiles, 0, tiles - 1)
            return (at, 0) if by_rows else (0, at)

        block = (tile, b_cols) if by_rows else (a_cols // 2, tile)
        return pl.BlockSpec(block, index)

    parts_a = len(a_list) * (shards * tiles if by_rows else 1)
    parts_b = len(b_list) * (1 if by_rows else shards * tiles)
    return pl.pallas_call(
        partial(weight_grad_kernel, heights, a_at, b_at, scale, by_rows, len(more)),
        grid_spec=pltpu.PrefetchScalarGridSpec(
            num_scalar_prefetch=1,
            grid=(shards * tiles,),
            in_specs=[anywhere] * (len(a_list) + len(b_list))
            + [tile_of(r) for r in range(len(more))],
            out_specs=[tile_of(i % shards) for i in range(many)],
            scratch_shapes=[
                pltpu.VMEM((total, a_cols), BF16),
                pltpu.VMEM((total, b_cols), BF16),
                pltpu.SemaphoreType.DMA((parts_a + parts_b,)),
            ],
        ),
        out_shape=[jax.ShapeDtypeStruct(shape, BF16)] * many,
        compiler_params=pltpu.CompilerParams(vmem_limit_bytes=BIG_VMEM),
        cost_estimate=pl.CostEstimate(
            flops=2 * total * a_cols * b_cols,
            bytes_accessed=2 * (total * (a_cols + b_cols) + a_cols * b_cols),
            transcendentals=0,
        ),
    )(info, *a_list, *b_list, *more)


def dense_grad_kernel(unit, shards, small_too, info, places, *refs):
    sources, refs = refs[:2], refs[2:]
    extras, refs = (refs[:3], refs[3:]) if small_too else ((), refs)
    mine, theirs, a_s, b_s, scratch, sems = refs[:6]
    copies, sent = Copies(sems), []
    got = [copies.start(ref, to) for ref, to in zip(sources, (a_s, b_s))]
    flat = len(scratch.shape) == 2
    cols = b_s.shape[1]
    count = 2 * mine.shape[0]
    wide = mine.shape[2] // shards
    tile = 256 if flat else 384
    core = info[0] % 2
    if small_too:
        small, width = refs[6], a_s.shape[1]
        turned = jnp.transpose(
            jnp.concatenate([extras[0][...], extras[1][...], jnp.zeros((6, width), F32)], axis=0)
        )
        lanes = lax.broadcasted_iota(jnp.int32, (width, 128), 1)
        small[...] = jnp.where(
            lanes == count,
            turned[:, 0:1],
            jnp.where(lanes == count + 1, turned[:, 1:2], extras[2][...]),
        ).astype(BF16)
        if flat:
            scratch[:, cols:] = small[...]
    finish(got)
    ready = 0
    for t in range(a_s.shape[1] // tile):
        grad = tn(a_s[:, t * tile : (t + 1) * tile], b_s[...]).astype(BF16)
        if flat:
            scratch[t * tile : (t + 1) * tile, 0:cols] = grad
        while (ready + 1) * unit <= (t + 1) * tile:
            if flat:
                block = scratch.at[pl.ds(ready * unit, unit), :]
            else:
                first = ready * unit - t * tile
                scratch[ready, :, 0:cols] = grad[first : first + unit]
                if small_too:
                    scratch[ready, :, cols:] = small[ready * unit : (ready + 1) * unit, :]
                block = scratch.at[ready]
            name, turn = ready % count, ready // count
            place = places[name // 2]
            if shards > 1:
                turn = lax.rem(turn - info[2] + shards, shards)
            at = pl.ds(pl.multiple_of(turn * wide, 128), wide)
            to_mine = copies.make(block, mine.at[place, :, at])
            to_theirs = pltpu.make_async_copy(
                block, theirs.at[place, :, at], sems.at[copies.used - 1]
            )

            @pl.when(core == name % 2)
            def _(one=to_mine):
                one.start()

            @pl.when(core != name % 2)
            def _(one=to_theirs):
                one.start()

            sent.append(to_mine)
            ready += 1
    finish(sent)


def dense_grad(info, places, unit, shards, a, b, extras=()):
    length, rows = a.shape
    cols = b.shape[1]
    chips = places.shape[0]
    wide = cols + (128 if extras else 0)
    here = pl.BlockSpec(memory_space=pltpu.VMEM)
    anywhere = pl.BlockSpec(memory_space=pltpu.HBM)
    small = pl.BlockSpec(memory_space=pltpu.SMEM)
    flat = unit % 16 == 0
    many = rows // unit
    scratch = [
        pltpu.VMEM(a.shape, BF16),
        pltpu.VMEM(b.shape, BF16),
        pltpu.VMEM((rows, wide) if flat else (many, unit, wide), BF16),
        pltpu.SemaphoreType.DMA((2 + many,)),
    ]
    if extras:
        scratch.append(pltpu.VMEM((rows, 128), BF16))
    return pl.pallas_call(
        partial(dense_grad_kernel, unit, shards, bool(extras)),
        in_specs=[small] * 2 + [anywhere] * 2 + [here] * len(extras),
        out_specs=[anywhere] * 2,
        out_shape=[jax.ShapeDtypeStruct((chips, unit, shards * wide), BF16)] * 2,
        scratch_shapes=scratch,
        compiler_params=pltpu.CompilerParams(vmem_limit_bytes=BIG_VMEM),
        cost_estimate=pl.CostEstimate(
            flops=6 * length * rows * cols,
            bytes_accessed=2 * length * (rows + cols),
            transcendentals=0,
        ),
    )(info, places, a, b, *extras)


def normed_back_kernel(grads, weight, tokens, low_out, gain_out):
    grad = nt(grads[...], weight[...])
    rows = tokens[...].astype(F32)
    unit = rows * lax.rsqrt(jnp.mean(rows * rows, axis=-1, keepdims=True) + EPSILON)
    gain_out[...] = jnp.sum(grad * unit, axis=0, keepdims=True)
    low_out[...] = grad.astype(BF16)


def normed_back(grads, weight, tokens):
    length, width = tokens.shape
    here = pl.BlockSpec(memory_space=pltpu.VMEM)
    return pl.pallas_call(
        normed_back_kernel,
        in_specs=[here] * 3,
        out_specs=[here] * 2,
        out_shape=[
            jax.ShapeDtypeStruct((length, width), BF16),
            jax.ShapeDtypeStruct((1, width), F32),
        ],
        compiler_params=pltpu.CompilerParams(vmem_limit_bytes=40 * MIB),
        cost_estimate=pl.CostEstimate(
            flops=2 * length * width * grads.shape[1],
            bytes_accessed=2 * (grads.size + weight.size + 2 * tokens.size),
            transcendentals=0,
        ),
    )(grads, weight, tokens)


def project_kernel(shards, q_cols, k_cols, unit, info, places, own_ref, gain_ref, *refs):
    token_refs, refs = refs[:shards], refs[shards:]
    blocks, (normed_out, cols_out, out, tokens_out, w_s, t_s, sems) = refs[:-7], refs[-7:]
    count = own_ref.shape[0]
    rows = token_refs[0].shape[0]
    copies = Copies(sems)
    shard = info[2]
    key_at, value_at = q_cols * shards, (q_cols + k_cols) * shards
    made, to = [], 0
    for s in range(shards):
        at = pl.ds(pl.multiple_of(info[2 + s] * rows, 16), rows)
        made.append(copies.start(token_refs[s], t_s.at[at]))
    for at, wide in ((0, q_cols), (key_at, k_cols), (value_at, k_cols)):
        cols = pl.ds(pl.multiple_of(at + shard * wide, 128), wide)
        made.append(
            copies.start(
                own_ref.at[:, cols],
                w_s.at[pl.ds(pl.multiple_of(shard * count, 16), count), pl.ds(to, wide)],
            )
        )
        to += wide
    for i, ref in enumerate(blocks):
        at = pl.ds(pl.multiple_of(places[i] * unit, 16), unit)
        made.append(copies.start(ref.at[pl.ds(0, unit)], w_s.at[at]))
    finish(made[:shards])
    value = t_s[...].astype(F32)
    normed_out[...] = (
        value
        * lax.rsqrt(jnp.mean(value * value, axis=-1, keepdims=True) + EPSILON)
        * gain_ref[...]
    ).astype(BF16)
    finish(made[shards:])
    sent = [copies.start(w_s, cols_out), copies.start(t_s, tokens_out)]
    out[...] = nn(normed_out[...], w_s[...])
    finish(sent)


def project(info, places, own, gain, tokens, blocks, shards, q_cols, k_cols, unit):
    rows, width = tokens[0].shape
    cols = q_cols + 2 * k_cols
    anywhere = pl.BlockSpec(memory_space=pltpu.HBM)
    here = pl.BlockSpec(memory_space=pltpu.VMEM)
    small = pl.BlockSpec(memory_space=pltpu.SMEM)
    return pl.pallas_call(
        partial(project_kernel, shards, q_cols, k_cols, unit),
        in_specs=[small, small, anywhere, here] + [anywhere] * (shards + len(blocks)),
        out_specs=[here, anywhere, here, anywhere],
        out_shape=[
            jax.ShapeDtypeStruct((shards * rows, width), BF16),
            jax.ShapeDtypeStruct((width, cols), BF16),
            jax.ShapeDtypeStruct((shards * rows, cols), F32),
            jax.ShapeDtypeStruct((shards * rows, width), BF16),
        ],
        scratch_shapes=[
            pltpu.VMEM((width, cols), BF16),
            pltpu.VMEM((shards * rows, width), BF16),
            pltpu.SemaphoreType.DMA((shards + 5 + len(blocks),)),
        ],
        compiler_params=pltpu.CompilerParams(vmem_limit_bytes=BIG_VMEM),
        cost_estimate=pl.CostEstimate(
            flops=2 * shards * rows * width * cols,
            bytes_accessed=2 * (width * cols + shards * rows * (2 * width + 2 * cols)),
            transcendentals=0,
        ),
    )(info, places, own, gain, *tokens, *blocks)


def router_back_kernel(experts, info, gate_ref, share_ref, second_ref, router_ref, grad_ref, add_ref):
    core = info[0] % 2
    rows = second_ref.shape[0]
    turned = jnp.transpose(
        jnp.concatenate([gate_ref[c] for c in range(experts // 2)], axis=0)
    )
    kept = jnp.concatenate([turned, jnp.zeros((rows, 128 - experts), F32)], axis=1)
    lanes = lax.broadcasted_iota(jnp.int32, (rows, 128), 1)
    swapped = jnp.where(lanes % 2 == 0, pltpu.roll(kept, 127, 1), pltpu.roll(kept, 1, 1))
    gates = jnp.where(core == 0, kept, swapped)
    share = share_ref[...]
    dot = jnp.sum(share * gates, axis=1, keepdims=True)
    low = (share * (gates - dot)).astype(BF16)
    grad_ref[...] = tn(second_ref[...], low)
    add_ref[...] = nt(low, router_ref[...])


def router_back(info, gates, shares, second, router, experts):
    rows, width = second.shape
    here = pl.BlockSpec(memory_space=pltpu.VMEM)
    return pl.pallas_call(
        partial(router_back_kernel, experts),
        in_specs=[pl.BlockSpec(memory_space=pltpu.SMEM)] + [here] * 4,
        out_specs=[here] * 2,
        out_shape=[
            jax.ShapeDtypeStruct((width, 128), F32),
            jax.ShapeDtypeStruct((rows, width), F32),
        ],
        compiler_params=pltpu.CompilerParams(vmem_limit_bytes=16 * MIB),
    )(info, gates, shares, second, router)


def middle_back_kernel(own, right, left, add, middle, gain, upstream, low_out, grad_out, gain_out):
    grad = own[...].astype(F32) + right[...].astype(F32) + left[...].astype(F32) + add[...]
    rows = middle[...]
    scale = lax.rsqrt(jnp.mean(rows * rows, axis=-1, keepdims=True) + EPSILON)
    unit = rows * scale
    share = jnp.sum(grad * unit, axis=0, keepdims=True)
    gain_out[...] = share + jnp.where(pl.program_id(0) == 0, 0.0, gain_out[...])
    weighted = grad * gain[...]
    dot = jnp.mean(weighted * unit, axis=-1, keepdims=True)
    total = upstream[...].astype(F32) + scale * (weighted - unit * dot)
    grad_out[...] = total
    low_out[...] = (RES_SCALE * total).astype(BF16)


def middle_back(own, right, left, add, middle, gain, upstream):
    rows, width = middle.shape
    block = rows // 4
    some = pl.BlockSpec((block, width), lambda i: (i, 0))
    one = pl.BlockSpec((1, width), lambda i: (0, 0))
    return pl.pallas_call(
        middle_back_kernel,
        grid=(4,),
        in_specs=[some] * 5 + [one, some],
        out_specs=[some, some, one],
        out_shape=[
            jax.ShapeDtypeStruct((rows, width), BF16),
            jax.ShapeDtypeStruct((rows, width), F32),
            jax.ShapeDtypeStruct((1, width), F32),
        ],
        compiler_params=pltpu.CompilerParams(vmem_limit_bytes=BIG_VMEM),
    )(own, right, left, add, middle, gain, upstream)


def ring_add_kernel(right, left, front, back, *outs):
    half = right.shape[0]
    if half < front.shape[0]:
        right_out, left_out = outs
        right_out[:half] = add_low(right[...], front[:half])
        right_out[half:] = front[half:]
        left_out[:half] = back[:half]
        left_out[half:] = add_low(left[...], back[half:])
        return
    for came, own, places in ((right, front, outs[: len(outs) // 2]), (left, back, outs[len(outs) // 2 :])):
        at = 0
        for out in places:
            rows = out.shape[0]
            out[...] = add_low(came[at : at + rows], own[at : at + rows])
            at += rows


def add_both(right, left, front, back, halved=False):
    here = pl.BlockSpec(memory_space=pltpu.VMEM)
    rows, width = front.shape
    shapes = [(rows // 2, width)] * 4 if halved else [(rows, width)] * 2
    return pl.pallas_call(
        ring_add_kernel,
        in_specs=[here] * 4,
        out_specs=[here] * len(shapes),
        out_shape=[jax.ShapeDtypeStruct(shape, front.dtype) for shape in shapes],
        compiler_params=pltpu.CompilerParams(vmem_limit_bytes=16 * MIB),
        cost_estimate=pl.CostEstimate(flops=1, bytes_accessed=12 * front.size, transcendentals=0),
    )(right, left, front, back)


def sum_blocks_kernel(plan, starts, *refs):
    arrays, refs = refs[: 2 * len(starts)], refs[2 * len(starts) :]
    many = len(plan)
    total = sum(len(came) for _, _, _, came in plan)
    refs, outs, (scratch, sems) = refs[:total], refs[total : total + many], refs[-2:]
    copies = Copies(sems)
    made = []
    for i, (place, low, high, _) in enumerate(plan):
        made.append([])
        for start, pair in zip(starts, (arrays[k : k + 2] for k in range(0, len(arrays), 2))):
            first, last = max(low, start), min(high, start + pair[0].shape[2])
            if first >= last:
                continue
            for j, ref in enumerate(pair):
                made[-1].append(
                    copies.start(
                        ref.at[place, :, pl.ds(first - start, last - first)],
                        scratch.at[2 * i + j, :, pl.ds(first - low, last - first)],
                    )
                )
    at = 0
    for i, (_, low, high, came) in enumerate(plan):
        finish(made[i])
        wide = high - low
        value = scratch[2 * i, :, :wide].astype(F32) + scratch[2 * i + 1, :, :wide].astype(F32)
        outs[i][...] = value.astype(BF16)
        for start, stop in came:
            part = value[:, start - low : stop - low] + refs[at][...].astype(F32)
            at += 1
            if (start, stop) == (low, high):
                value = part
            outs[i][:, start - low : stop - low] = part.astype(BF16)


def sum_blocks(pairs, wanted):
    unit = pairs[0][0].shape[1]
    starts = [sum(p[0].shape[2] for p in pairs[:i]) for i in range(len(pairs))]
    every = sum(p[0].shape[2] for p in pairs)
    plan, flat = [], []
    for place, low, high, came in wanted:
        plan.append((place, low, high, [(at, at + c.shape[1]) for at, c in came]))
        flat += [c for _, c in came]
    anywhere = pl.BlockSpec(memory_space=pltpu.HBM)
    here = pl.BlockSpec(memory_space=pltpu.VMEM)
    arrays = [array for pair in pairs for array in pair]
    return pl.pallas_call(
        partial(sum_blocks_kernel, plan, starts),
        in_specs=[anywhere] * len(arrays) + [here] * len(flat),
        out_specs=[here] * len(plan),
        out_shape=[jax.ShapeDtypeStruct((unit, high - low), BF16) for _, low, high, _ in plan],
        scratch_shapes=[
            pltpu.VMEM((2 * len(plan), unit, every), BF16),
            pltpu.SemaphoreType.DMA((len(arrays) * len(plan),)),
        ],
        compiler_params=pltpu.CompilerParams(vmem_limit_bytes=16 * MIB),
        cost_estimate=pl.CostEstimate(
            flops=1, bytes_accessed=6 * len(plan) * unit * every, transcendentals=0
        ),
    )(*arrays, *flat)


def body(
    tokens,
    segment_ids,
    routes,
    norm1_gain,
    norm2_gain,
    qkv_weight,
    out_weight,
    route_weight,
    expert_in,
    expert_down,
    cotangent,
):
    rows, width = tokens.shape
    shards = lax.axis_size("shard")
    chips = lax.axis_size("chip")
    experts = 2 * chips
    length = rows * shards
    q_cols = QUERY_HEADS // shards * HEAD_SIZE
    k_cols = KEY_VALUE_HEADS // shards * HEAD_SIZE
    own_cols = q_cols + 2 * k_cols
    query_width = QUERY_HEADS * HEAD_SIZE
    pair_width = KEY_VALUE_HEADS * HEAD_SIZE
    ffe = expert_down.shape[1]
    cut = width // shards
    shard = lax.axis_index("shard")
    core = lax.axis_index("core")
    chip = lax.axis_index("chip")
    walk = ring_chips(chips)
    ahead = [(walk[i], walk[(i + 1) % chips]) for i in range(chips)]
    behind = [(b, a) for a, b in ahead]
    half_ring = chips // 2
    order = [0]
    for step in range(1, half_ring):
        order += [-step, step]
    order.append(half_ring)
    place_of = {c: i for i, c in enumerate(walk)}
    chip_tables = np.array([[walk[(place_of[c] + o) % chips] for o in order] for c in range(chips)])
    senders = jnp.asarray(chip_tables, jnp.int32)[chip]
    info = jnp.concatenate(
        [
            jnp.stack([2 * chip + core, 2 * chip + 1 - core]),
            (shard - jnp.arange(shards) + shards) % shards,
            senders,
        ]
    ).astype(jnp.int32)
    slot_of = lambda i: 2 + shards + i
    both_cores = jnp.concatenate([2 * senders + core, 2 * senders + 1 - core])
    rel_tables = np.array([[list(row).index(c) for c in range(chips)] for row in chip_tables])
    chip_places = jnp.asarray(rel_tables, jnp.int32)[chip]

    def to_shard(value, step):
        return lax.ppermute(value, "shard", [(i, (i + step) % shards) for i in range(shards)])

    def to_core(value):
        return lax.ppermute(value, "core", [(0, 1), (1, 0)])

    def in_order(pieces):
        out = []
        for j in range(shards):
            value = pieces[0]
            for s in range(1, shards):
                value = jnp.where((shard - j + shards) % shards == s, pieces[s], value)
            out.append(value)
        return out

    def exchange_shards(piece_for):
        got = [piece_for(shard)]
        for s in range(1, shards):
            got.append(to_shard(piece_for(lax.rem(shard + s, shards)), s))
        return got

    def sum_shards(piece_for):
        got = exchange_shards(piece_for)
        total = got[0].astype(F32)
        for piece in got[1:]:
            total = total + piece.astype(F32)
        return total

    def to_holders(parts):
        return [parts[0]] + [to_shard(parts[s], s) for s in range(1, shards)]

    def ring_step(pair, cut_far=False):
        right, left = pair
        if cut_far:
            right, left = right[: rows // 2], left[rows // 2 :]
        return lax.ppermute(right, "chip", ahead), lax.ppermute(left, "chip", behind)

    def ring_gather(value):
        out, pair = [value], (value, value)
        for step in range(1, half_ring + 1):
            pair = ring_step(pair, step == half_ring)
            out += pair
        return out

    def ring_start(parts):
        return lax.ppermute(parts[-2], "chip", ahead), lax.ppermute(parts[-1], "chip", behind)

    def ring_add(parts, step, got):
        return tuple(add_both(*got, parts[2 * step], parts[2 * step - 1]))

    def ring_send(sent):
        return lax.ppermute(sent[0], "chip", ahead), lax.ppermute(sent[1], "chip", behind)

    def ring_end(parts, got):
        return parts[0].astype(F32) + got[0].astype(F32) + got[1].astype(F32)

    def plane_gather(value, beside, use_early):
        right = left = value
        got = [value]
        half = value.shape[1] // 256 * 128
        for step in range(1, half_ring + 1):
            if step > 1:
                right, left, beside[step] = lax.optimization_barrier(
                    (right, left, beside.get(step, ()))
                )
            if step == half_ring:
                right, left = right[:, :half], left[:, half:]
            right = lax.ppermute(right, "chip", ahead)
            left = lax.ppermute(left, "chip", behind)
            if step < half_ring:
                got += [right, left]
        early = 2 * half_ring - 3
        used = use_early(got[:early] + [to_core(v) for v in got[:early]])
        right, left, used = lax.optimization_barrier((right, left, used))
        late = got[early:] + [jnp.concatenate([right, left], axis=1)]
        return used, late + [to_core(v) for v in late]

    def block_ring(values, beside):
        right = left = values
        got = [values]
        for step in range(1, half_ring + 1):
            if step > 1:
                right, left, beside = lax.optimization_barrier(
                    (right, left, beside)
                ) if step == 3 else (*lax.optimization_barrier((right, left)), beside)
            right = [lax.ppermute(v, "chip", ahead) for v in right]
            got.append(right)
            if step < half_ring:
                left = [lax.ppermute(v, "chip", behind) for v in left]
                got.append(left)
        return got + [[to_core(v) for v in values] for values in got], beside

    def own_columns(rows_at, count, target):
        return jnp.concatenate(
            [
                lax.dynamic_slice(qkv_weight, (rows_at, at + target * cols), (count, cols))
                for at, cols in (
                    (0, q_cols),
                    (query_width, k_cols),
                    (query_width + pair_width, k_cols),
                )
            ],
            axis=1,
        )

    unit = cut // experts
    name = 2 * chip + core
    units = [
        to_shard(own_columns(name * unit, unit, lax.rem(shard + s, shards)), s)
        for s in range(1, shards)
    ]
    tokens_got = [tokens] + [to_shard(tokens, s) for s in range(1, shards)]
    extras = jnp.concatenate(
        [norm1_gain, norm2_gain, segment_ids.astype(BF16), route_weight.reshape(-1)]
    ).reshape(-1, 256)
    extras = [extras] + [to_shard(extras, s) for s in range(1, shards)]
    named = jnp.pad(routes.T.astype(BF16), ((0, 16 - routes.shape[1]), (0, own_cols - rows)))
    together = unit % 16 == 0
    if together:
        units[0] = jnp.concatenate([units[0], named], axis=0)
    else:
        units.append(named)
    blocks, (tokens_got, extras) = block_ring(units, (tokens_got, extras))

    held_in, held_down = tie((expert_in[0], expert_down[0]), tokens_got)
    down_own = [held_down] + [to_shard(held_down, s) for s in range(1, shards)]
    in_own = [held_in] + [to_shard(held_in, s) for s in range(1, shards)]
    layouts = ([(s, 0, cut, cut) for s in range(shards)],) * 2
    blocks, down_own, upstream = lax.optimization_barrier((blocks, down_own, cotangent))
    dy_pair = ring_step((upstream, upstream))
    upstream_chunks = [cotangent, *dy_pair]
    named_chunks = [b[0 if together else -1] for b in blocks[:chips]]
    named_at = unit if together else 0
    block_list = [b[s] for s in range(shards - 1) for b in blocks]
    block_places = jnp.concatenate(
        [info[2 + s] * experts + both_cores for s in range(1, shards)]
    ).astype(jnp.int32)
    extras = jnp.stack(in_order(extras)).reshape(shards, -1)
    gain_one = extras[:, :cut].reshape(1, -1).astype(F32)
    gain_two = extras[:, cut : 2 * cut].reshape(1, -1).astype(F32)
    segments = extras[:, 2 * cut : 2 * cut + rows].reshape(-1).astype(F32)
    router = extras[:, 2 * cut + rows :].reshape(width, experts)
    router_wide = jnp.pad(router, ((0, 0), (0, 128 - experts)))

    inputs = tokens.astype(F32)
    if together:
        normed, qkv_cols, projected, all_tokens = project(
            info, block_places, qkv_weight, gain_one, tokens_got, block_list, shards, q_cols, k_cols, unit
        )
    else:
        placed = jnp.zeros((shards * experts, unit, own_cols), BF16)
        for i, piece in enumerate(block_list):
            placed = lax.dynamic_update_index_in_dim(placed, piece, block_places[i], 0)
        qkv_cols = lax.dynamic_update_slice(
            placed.reshape(width, own_cols), own_columns(0, cut, shard), (shard * cut, 0)
        )
        all_tokens = jnp.concatenate(in_order(tokens_got), axis=0)
        wide_tokens = all_tokens.astype(F32)
        normed = (wide_tokens * rms_scale(wide_tokens) * gain_one).astype(BF16)
        projected = nn(normed, qkv_cols)
    places = jnp.arange(length)
    inverse = jnp.power(ROPE_BASE, -(jnp.arange(HEAD_SIZE // 2) * 2.0 / HEAD_SIZE))
    angles = places.astype(F32)[:, None] * inverse[None, :]
    cosine = jnp.concatenate([jnp.cos(angles)] * 4, axis=1)
    sine = jnp.concatenate([-jnp.sin(angles), jnp.sin(angles)] * 2, axis=1)
    projected, dy_pair = lax.optimization_barrier((projected, dy_pair))
    dy_pair = ring_step(dy_pair)
    upstream_chunks += dy_pair
    qkv, probs, head_out = attend(projected, cosine, sine, segments)
    branch = nn(head_out, out_weight).astype(BF16)
    branch, in_own, dy_pair = lax.optimization_barrier((branch, in_own, dy_pair))
    dy_pair = ring_step(dy_pair)
    upstream_chunks += dy_pair
    rows_of = lambda value, j: lax.dynamic_slice(value, (j * rows, 0), (rows, value.shape[1]))
    middle = inputs + RES_SCALE * sum_shards(lambda j: rows_of(branch, j))
    middle, dy_pair = lax.optimization_barrier((middle, dy_pair))
    weights = [in_own, down_own, [to_core(w) for w in in_own], [to_core(w) for w in down_own]]
    scale_two = rms_scale(middle)
    second = (middle * scale_two * gain_two).astype(BF16)

    second_chunks, pair = [second], (second, second)
    dy_hops = 3
    row_parts, gate_parts, lows, mixeds = [], [], [], []
    for step in range(half_ring + 1):
        first = max(0, 2 * step - 1)
        picks = list(range(first, len(second_chunks)))
        if step < half_ring:
            pair = ring_step(pair, step == half_ring - 1)
            second_chunks += pair
        far = step == half_ring
        slots = [(named_at, 0, rows)] * len(picks)
        if step == half_ring:
            slots = [(named_at, 0, rows), (named_at, rows // 2, rows)]
        low, mixed, row, gate, shares = run_experts(
            slots,
            info,
            [second_chunks[i] for i in picks],
            [upstream_chunks[i] for i in picks],
            [named_chunks[min(i, chips - 1)] for i in picks],
            router_wide,
            weights,
            layouts,
        )
        if step == 0:
            own_shares = shares
        if not far:
            pair, low, dy_pair = lax.optimization_barrier((pair, low, dy_pair))
            second_chunks[-2:] = pair
            last = dy_hops == half_ring - 1
            if dy_hops < half_ring and (not last or step == half_ring - 2):
                dy_hops += 1
                dy_pair = ring_step(tie(dy_pair, pair), last)
                upstream_chunks += dy_pair
        lows.append(low)
        mixeds.append(mixed)
        row_parts += row
        gate_parts += [gate] if far else [[g] for g in gate]

    def make_in(sent, at, more=()):
        return weight_grad(
            info, shards, second_chunks, 0, width, tie(lows, sent), at, 2 * ffe, more=more
        )

    got = ring_start(row_parts)
    made = make_in((), 2 * ffe)
    got, made = lax.optimization_barrier((got, made))
    in_other = [to_core(piece) for piece in made]
    for hop, step in enumerate(range(half_ring - 1, 0, -1)):
        sent = ring_add(row_parts, step, got)
        got = ring_send(sent)
        if hop == 0:
            in_parts = make_in(sent, 0, in_other)
            got, in_parts = lax.optimization_barrier((got, in_parts))
            in_got = to_holders(in_parts)
        if hop == 1:
            out_parts = run_results(
                info, tie(mixeds, sent), weights, layouts, [p.shape[0] for p in row_parts]
            )
            gate_home = sort_gates(info, tie(gate_parts, sent), rows)
            gate_home = lax.all_to_all(
                gate_home, "chip", split_axis=0, concat_axis=0, tiled=True
            )
            got, out_parts, gate_home = lax.optimization_barrier((got, out_parts, gate_home))
        if hop == 2:
            router_add = router_back(
                info, tie(gate_home, sent), own_shares, second, router_wide, experts
            )
            down_parts = weight_grad(
                info,
                shards,
                tie(mixeds, (sent, router_add)),
                0,
                2 * ffe,
                upstream_chunks,
                0,
                width,
                RES_SCALE,
                by_rows=False,
            )
            got, down_parts = lax.optimization_barrier((got, down_parts))
    grad_route, router_add = router_add
    out_got = ring_start(tie(out_parts, got))
    attn_low, middle_grads, grad_gain_two = middle_back(
        row_parts[0], *got, router_add, middle, gain_two, cotangent
    )
    attn_low, out_got = lax.optimization_barrier((attn_low, out_got))
    attn_low, in_got = lax.optimization_barrier((attn_low, in_got))

    low = lambda value: value.astype(BF16)
    sent = ring_add(out_parts, half_ring - 1, out_got)
    got = ring_send(sent)
    attn_got = [attn_low] + [to_shard(attn_low, s) for s in range(1, shards)]
    down_other = [to_core(piece) for piece in tie(down_parts[shards:], (attn_low, sent))]
    down_parts = [add_low(a, b) for a, b in zip(down_parts[:shards], down_other)]
    attn_got, got, down_parts = lax.optimization_barrier((attn_got, got, down_parts))
    if half_ring > 2:
        got = ring_send(ring_add(out_parts, half_ring - 2, got))

    down_got = to_holders(down_parts)
    projected_grads, attn_grads = attend_back(info, qkv, probs, out_weight, cosine, sine, attn_got)
    normed_low, grad_gain_one = normed_back(projected_grads, qkv_cols, all_tokens)
    got, normed_low, grad_gain_one, down_got = lax.optimization_barrier(
        (got, normed_low, grad_gain_one, down_got)
    )
    for step in range(half_ring - 3, 0, -1):
        sent = ring_add(out_parts, step, got)
        projected_grads, attn_grads, sent = lax.optimization_barrier(
            (projected_grads, attn_grads, sent)
        )
        got = ring_send(sent)

    mine_out, theirs_out = dense_grad(info, chip_places, unit, 1, head_out, attn_grads)
    theirs_out = to_core(theirs_out)
    mine_qkv, theirs_qkv = dense_grad(
        info,
        chip_places,
        unit,
        shards,
        tie(normed, mine_out),
        projected_grads,
        (grad_gain_one, grad_gain_two, grad_route),
    )
    wide = own_cols + 128
    mine_qkv, theirs_qkv, got = lax.optimization_barrier((mine_qkv, theirs_qkv, got))
    theirs_qkv = to_core(theirs_qkv)
    pairs = ((mine_qkv, theirs_qkv), (mine_out, theirs_out))
    every = mine_qkv.shape[2] + mine_out.shape[2]
    half = every // 256 * 128
    right, left = sum_blocks(pairs, [(chips - 1, 0, half, []), (chips - 1, half, every, [])])
    right, left = lax.ppermute(right, "chip", ahead), lax.ppermute(left, "chip", behind)
    right, left, normed_low = lax.optimization_barrier((right, left, normed_low))
    normed_got = exchange_shards(lambda j: rows_of(normed_low, j))
    for hop, step in enumerate(range(half_ring - 1, 0, -1)):
        right, left = sum_blocks(
            pairs,
            [
                (2 * step, 0, every, [(0, right)]),
                (2 * step - 1, 0, every, [(every - left.shape[1], left)]),
            ],
        )
        right = lax.ppermute(right, "chip", ahead)
        left = lax.ppermute(left, "chip", behind)
        right, left = lax.optimization_barrier((right, left))
        if step == half_ring - 2:
            right, left, normed_got = lax.optimization_barrier((right, left, normed_got))
    (dense,) = sum_blocks(pairs, [(0, 0, every, [(0, right), (0, left)])])
    mixed = in_order(
        [dense[:, :wide]]
        + [to_shard(dense[:, s * wide : (s + 1) * wide], s) for s in range(1, shards)]
    )
    merged = jnp.concatenate(
        [g[:, :q_cols] for g in mixed]
        + [g[:, q_cols : q_cols + k_cols] for g in mixed]
        + [g[:, q_cols + k_cols : own_cols] for g in mixed]
        + [low(sum(g[:, own_cols:].astype(F32) for g in mixed)), dense[:, shards * wide :]],
        axis=1,
    )

    total = lambda pieces: sum(p.astype(F32) for p in pieces)
    input_grads = rms_back(inputs, rms_scale(inputs), gain_one, total(normed_got))
    grad_tokens = middle_grads + input_grads
    grad_down, grad_in = total(down_got), total(in_got)

    block_out = low(middle + RES_SCALE * ring_end(out_parts, got))
    beside = {2: block_out, half_ring - 1: grad_tokens, half_ring: (grad_down, grad_in)}
    all_cols = query_width + 2 * pair_width
    widths = [all_cols, 128, width]
    cores = jnp.split(both_cores.astype(jnp.int32), 2)
    count = 2 * half_ring - 3
    places = jnp.concatenate([c[:count] for c in cores] + [c[count:] for c in cores])
    spread_out, late = plane_gather(
        merged, beside, lambda early: spread(places, 0, early, widths, experts)
    )
    block_out, grad_tokens = beside[2], beside[half_ring - 1]
    grad_down, grad_in = beside[half_ring]
    spread_out = spread(places, 2 * count, late, widths, experts, spread_out)
    grad_qkv, small, grad_out = [out.reshape(-1, out.shape[-1]) for out in spread_out]
    return (
        block_out,
        grad_tokens,
        small[:, experts],
        small[:, experts + 1],
        grad_qkv,
        grad_out,
        small[:, :experts],
        grad_in[None],
        grad_down[None],
    )


def solution(mesh):
    chips = mesh.shape["expert"] // 2
    grid = Mesh(
        mesh.devices.reshape(chips, 2, mesh.shape["shard"]), ("chip", "core", "shard")
    )
    expert = ("chip", "core")
    every = ("chip", "core", "shard")
    in_specs = (
        P(every, None),
        P(every),
        P(every, None),
        P("shard"),
        P("shard"),
        P("shard", None),
        P("shard", None),
        P("shard", None),
        P(expert, "shard", None),
        P(expert, None, "shard"),
        P(every, None),
    )
    out_specs = (
        P(every, None),
        P(every, None),
        P("shard"),
        P("shard"),
        P("shard", None),
        P("shard", None),
        P("shard", None),
        P(expert, "shard", None),
        P(expert, None, "shard"),
    )
    return jax.shard_map(body, mesh=grid, in_specs=in_specs, out_specs=out_specs, check_vma=False)
```

```python
from functools import partial

import jax
import jax.numpy as jnp
import numpy as np
from jax import lax
from jax.experimental import pallas as pl
from jax.experimental.pallas import tpu as pltpu
from jax.sharding import Mesh, PartitionSpec as P

QUERY_HEADS = 24
KEY_VALUE_HEADS = 8
HEAD_SIZE = 64
GROUP = QUERY_HEADS // KEY_VALUE_HEADS
RES_SCALE = 0.22
ATT_SCALE = 0.015625
EPSILON = 1e-06
ROPE_BASE = 10000.0
MASKED = -1000000000.0
F32 = jnp.float32
BF16 = jnp.bfloat16
MIB = 1024 * 1024
BIG_VMEM = 60 * MIB


def mm(a, b, dims):
    return lax.dot_general(a, b, (dims, ((), ())), preferred_element_type=F32)


def nn(a, b):
    return mm(a, b, ((1,), (0,)))


def nt(a, b):
    return mm(a, b, ((1,), (1,)))


def tn(a, b):
    return mm(a, b, ((0,), (0,)))


def tie(values, after):
    return lax.optimization_barrier((values, after))[0]


def ring_chips(chips):
    depth = 4 if chips % 4 == 0 else 2
    width = max(1, chips // depth)
    walk = [(z, 0) for z in range(depth)]
    for z in reversed(range(depth)):
        line = range(1, width) if (depth - 1 - z) % 2 == 0 else reversed(range(1, width))
        walk += [(z, x) for x in line]
    return [z * width + x for z, x in walk]


def add_low(a, b):
    return (a.astype(F32) + b.astype(F32)).astype(BF16)


def rms_scale(rows):
    return lax.rsqrt(jnp.mean(rows * rows, axis=-1, keepdims=True) + EPSILON)


def rms_back(rows, scale, gain, grad):
    weighted = grad * gain
    dot = jnp.mean(weighted * rows, axis=-1, keepdims=True)
    return scale * weighted - rows * (scale * scale * scale * dot)


def turn(value, cosine, sine, first):
    swapped = jnp.where(first, pltpu.roll(value, 96, 1), pltpu.roll(value, 32, 1))
    return value * cosine + swapped * sine


def attend_kernel(
    q_ref, k_ref, v_ref, cos_ref, sin_ref, seg_col, seg_row, qkv_out, p_out, head_out, bias, turned
):
    pair, pairs = pl.program_id(0), pl.num_programs(0)
    length = q_ref.shape[0]
    block = min(256, length)
    q_cols = pairs * 2 * GROUP * HEAD_SIZE
    wide = 2 * GROUP * HEAD_SIZE
    first = lax.broadcasted_iota(jnp.int32, (length, 128), 1) % HEAD_SIZE < HEAD_SIZE // 2

    @pl.when(pair == 0)
    def _():
        keys = lax.broadcasted_iota(jnp.int32, (length, length), 0)
        rows = lax.broadcasted_iota(jnp.int32, (length, length), 1)
        allowed = (seg_col[...] == seg_row[...]) & (keys <= rows)
        bias[...] = jnp.where(allowed, 0.0, MASKED)

    cosine, sine = cos_ref[...], sin_ref[...]
    for c in range(wide // 128):
        at = pl.ds(c * 128, 128)
        turned[:, at] = turn(q_ref[:, at], cosine, sine, first).astype(BF16)
    key = turn(k_ref[...], cosine, sine, first).astype(BF16)
    value = v_ref[...].astype(BF16)
    qkv_out[:, pl.ds(pl.multiple_of(pair * wide, 128), wide)] = turned[...]
    qkv_out[:, pl.ds(pl.multiple_of(q_cols + pair * 128, 128), 128)] = key
    qkv_out[:, pl.ds(pl.multiple_of(q_cols + (pairs + pair) * 128, 128), 128)] = value
    value_t = jnp.transpose(v_ref[...]).astype(BF16)
    for r in range(length // block):
        rows = pl.ds(r * block, block)
        end = (r + 1) * block
        mask = bias[0:end, rows]
        mask = jnp.concatenate([mask] * GROUP, axis=1)
        both = []
        for g in range(2):
            query = jnp.concatenate(
                [
                    turned[rows, pl.ds((g * GROUP + j) * HEAD_SIZE, HEAD_SIZE)]
                    for j in range(GROUP)
                ],
                axis=0,
            )
            own_key = key[:end, g * HEAD_SIZE : (g + 1) * HEAD_SIZE]
            scores = nt(own_key, query) * ATT_SCALE + mask
            grown = jnp.exp(scores - jnp.max(scores, axis=0, keepdims=True))
            probs = grown * (1.0 / jnp.sum(grown, axis=0, keepdims=True))
            probs = probs.astype(BF16)
            p_out[g, 0:end, pl.ds(r * GROUP * block, GROUP * block)] = probs
            both.append(nn(value_t[g * HEAD_SIZE : (g + 1) * HEAD_SIZE, :end], probs))
        laid = jnp.transpose(jnp.concatenate(both, axis=0))
        for g in range(2):
            for j in range(GROUP):
                head_out[rows, pl.ds((g * GROUP + j) * HEAD_SIZE, HEAD_SIZE)] = laid[
                    j * block : (j + 1) * block, g * HEAD_SIZE : (g + 1) * HEAD_SIZE
                ].astype(BF16)


def attend(projected, cosine, sine, segments):
    length, cols = projected.shape
    q_cols = cols * 3 // 5
    pairs = q_cols // (2 * GROUP * HEAD_SIZE)
    wide = 2 * GROUP * HEAD_SIZE
    key_at = q_cols // 128
    return pl.pallas_call(
        attend_kernel,
        grid=(pairs,),
        in_specs=[
            pl.BlockSpec((length, wide), lambda i: (0, i)),
            pl.BlockSpec((length, 128), lambda i: (0, key_at + i)),
            pl.BlockSpec((length, 128), lambda i: (0, key_at + pairs + i)),
            pl.BlockSpec((length, 128), lambda i: (0, 0)),
            pl.BlockSpec((length, 128), lambda i: (0, 0)),
            pl.BlockSpec((length, 1), lambda i: (0, 0)),
            pl.BlockSpec((1, length), lambda i: (0, 0)),
        ],
        out_specs=[
            pl.BlockSpec((length, cols), lambda i: (0, 0)),
            pl.BlockSpec((2, length, GROUP * length), lambda i: (i, 0, 0)),
            pl.BlockSpec((length, wide), lambda i: (0, i)),
        ],
        out_shape=[
            jax.ShapeDtypeStruct((length, cols), BF16),
            jax.ShapeDtypeStruct((2 * pairs, length, GROUP * length), BF16),
            jax.ShapeDtypeStruct((length, q_cols), BF16),
        ],
        scratch_shapes=[pltpu.VMEM((length, length), F32), pltpu.VMEM((length, wide), BF16)],
        compiler_params=pltpu.CompilerParams(vmem_limit_bytes=40 * MIB),
        cost_estimate=pl.CostEstimate(
            flops=8 * pairs * GROUP * length * length * 256,
            bytes_accessed=4 * pairs * GROUP * length * length,
            transcendentals=2 * pairs * GROUP * length * length,
        ),
    )(projected, projected, projected, cosine, sine, segments[:, None], segments[None, :])


def attend_back_kernel(shards, info, q_ref, k_ref, v_ref, p_ref, w_ref, cos_ref, sin_ref, *refs):
    upstream, refs = refs[:shards], refs[shards:]
    grad_out, all_out, all_s, d_s, dq_s, dk_s, dv_s, sems = refs
    pair, pairs = pl.program_id(0), pl.num_programs(0)
    length = q_ref.shape[0]
    rows_of = length // shards

    def kept():
        return pltpu.make_async_copy(all_s, all_out, sems.at[shards])

    @pl.when(pair == 0)
    def _():
        made = [
            pltpu.make_async_copy(
                upstream[s],
                all_s.at[pl.ds(pl.multiple_of(info[2 + s] * rows_of, 16), rows_of)],
                sems.at[s],
            )
            for s in range(shards)
        ]
        for one in made:
            one.start()
        finish(made)
        kept().start()
        grads = nt(all_s[...], w_ref[...]).astype(BF16)
        for i in range(d_s.shape[0]):
            d_s[i] = grads[:, i * d_s.shape[2] : (i + 1) * d_s.shape[2]]

    @pl.when(pair == pairs - 1)
    def _():
        kept().wait()

    d_ref = d_s.at[pair]
    block = min(256, length)
    q_cols = pairs * 2 * GROUP * HEAD_SIZE
    wide = 2 * GROUP * HEAD_SIZE
    first = lax.broadcasted_iota(jnp.int32, (length, 128), 1) % HEAD_SIZE < HEAD_SIZE // 2
    key_t = jnp.transpose(k_ref[...].astype(F32)).astype(BF16)
    for r in reversed(range(length // block)):
        rows = pl.ds(r * block, block)
        end = (r + 1) * block
        both = []
        for g in range(2):
            own = pl.ds(g * HEAD_SIZE, HEAD_SIZE)
            heads = [
                pl.ds((g * GROUP + j) * HEAD_SIZE, HEAD_SIZE) for j in range(GROUP)
            ]
            query = jnp.concatenate([q_ref[rows, h] for h in heads], axis=0)
            grad = jnp.concatenate([d_ref[rows, h] for h in heads], axis=0)
            probs = p_ref[g, 0:end, pl.ds(r * GROUP * block, GROUP * block)]
            prob_grad = nt(v_ref[0:end, own], grad)
            wide_probs = probs.astype(F32)
            dots = jnp.sum(wide_probs * prob_grad, axis=0, keepdims=True)
            score_grad = (wide_probs * (prob_grad - dots)).astype(BF16)
            key_grad = nn(score_grad, query)
            value_grad = nn(probs, grad)
            if end == length:
                dk_s[0:end, own] = key_grad
                dv_s[0:end, own] = value_grad
            else:
                dk_s[0:end, own] += key_grad
                dv_s[0:end, own] += value_grad
            both.append(nn(key_t[g * HEAD_SIZE : (g + 1) * HEAD_SIZE, :end], score_grad))
        laid = jnp.transpose(jnp.concatenate(both, axis=0))
        for g in range(2):
            for j in range(GROUP):
                dq_s[rows, pl.ds((g * GROUP + j) * HEAD_SIZE, HEAD_SIZE)] = laid[
                    j * block : (j + 1) * block, g * HEAD_SIZE : (g + 1) * HEAD_SIZE
                ]
    cosine, sine = cos_ref[...] * ATT_SCALE, sin_ref[...] * -ATT_SCALE
    for c in range(wide // 128):
        at = pl.ds(c * 128, 128)
        grad_out[:, pl.ds(pl.multiple_of(pair * wide + c * 128, 128), 128)] = turn(
            dq_s[:, at], cosine, sine, first
        ).astype(BF16)
    grad_out[:, pl.ds(pl.multiple_of(q_cols + pair * 128, 128), 128)] = turn(
        dk_s[...], cosine, sine, first
    ).astype(BF16)
    grad_out[:, pl.ds(pl.multiple_of(q_cols + (pairs + pair) * 128, 128), 128)] = dv_s[
        ...
    ].astype(BF16)


def attend_back(info, qkv, probs, out_weight, cosine, sine, upstream):
    length, cols = qkv.shape
    q_cols = cols * 3 // 5
    pairs = q_cols // (2 * GROUP * HEAD_SIZE)
    wide = 2 * GROUP * HEAD_SIZE
    width = out_weight.shape[1]
    key_at = q_cols // 128
    shards = len(upstream)
    anywhere = pl.BlockSpec(memory_space=pltpu.HBM)
    return pl.pallas_call(
        partial(attend_back_kernel, shards),
        grid=(pairs,),
        in_specs=[
            pl.BlockSpec(memory_space=pltpu.SMEM),
            pl.BlockSpec((length, wide), lambda i: (0, i)),
            pl.BlockSpec((length, 128), lambda i: (0, key_at + i)),
            pl.BlockSpec((length, 128), lambda i: (0, key_at + pairs + i)),
            pl.BlockSpec((2, length, GROUP * length), lambda i: (i, 0, 0)),
            pl.BlockSpec((q_cols, width), lambda i: (0, 0)),
            pl.BlockSpec((length, 128), lambda i: (0, 0)),
            pl.BlockSpec((length, 128), lambda i: (0, 0)),
        ]
        + [anywhere] * shards,
        out_specs=[pl.BlockSpec((length, cols), lambda i: (0, 0)), anywhere],
        out_shape=[
            jax.ShapeDtypeStruct((length, cols), BF16),
            jax.ShapeDtypeStruct((length, width), BF16),
        ],
        scratch_shapes=[
            pltpu.VMEM((length, width), BF16),
            pltpu.VMEM((pairs, length, wide), BF16),
            pltpu.VMEM((length, wide), F32),
            pltpu.VMEM((length, 128), F32),
            pltpu.VMEM((length, 128), F32),
            pltpu.SemaphoreType.DMA((shards + 1,)),
        ],
        compiler_params=pltpu.CompilerParams(vmem_limit_bytes=40 * MIB),
        cost_estimate=pl.CostEstimate(
            flops=16 * pairs * GROUP * length * length * 256 + 2 * length * q_cols * width,
            bytes_accessed=4 * pairs * GROUP * length * length,
            transcendentals=0,
        ),
    )(info, qkv, qkv, qkv, probs, out_weight, cosine, sine, *upstream)


class Copies:
    def __init__(self, sems):
        self.sems, self.used = sems, 0

    def make(self, src, dst):
        made = pltpu.make_async_copy(src, dst, self.sems.at[self.used])
        self.used += 1
        return made

    def start(self, src, dst):
        made = self.make(src, dst)
        made.start()
        return made


def finish(copies):
    for made in copies:
        made.wait()


def load_weights(copies, info, refs, layout, scratch, base, cols):
    made = []
    for ref, (s, first, number, many) in zip(refs, layout):
        at = pl.ds(pl.multiple_of(info[2 + s] * many + first, 128 if cols else 16), number)
        if cols:
            made.append(copies.start(ref, scratch.at[pl.ds(base, ref.shape[0]), at]))
        else:
            made.append(copies.start(ref, scratch.at[at, pl.ds(base, ref.shape[1])]))
    return made


def expert_kernel(slots, in_layout, down_layout, info, *refs):
    parts = len(slots)
    refs = list(refs)
    take = lambda n: [refs.pop(0) for _ in range(n)]
    x_refs, d_refs = take(parts), take(parts)
    route_refs, (router_ref,) = take(parts), take(1)
    in_refs = [take(len(in_layout)), take(len(in_layout))]
    down_refs = [take(len(down_layout)), take(len(down_layout))]
    low_out, mixed_out = take(2)
    row_outs, gate_outs = take(parts), take(parts)
    (share_out,) = take(1)
    x_s, d_s, in_s, down_s, router_s, route_s, low_s, mixed_s, row_s, gate_s, pulled_s, sems = refs
    rows, width = x_refs[0].shape
    total = parts * rows
    ffe = in_s.shape[1] // 4
    tile = min(256, ffe)
    copies = Copies(sems)
    place = [pl.ds(p * rows, rows) for p in range(parts)]
    got_x = [copies.start(x_refs[p], x_s.at[place[p]]) for p in range(parts)]
    got_x.append(copies.start(router_ref, router_s))
    for p in range(parts):
        at, _, seen = slots[p]
        got_x.append(copies.start(route_refs[p].at[pl.ds(at, 16), pl.ds(0, seen)], route_s.at[p]))
    got_in, got_down = [], []
    for e in range(2):
        got_in.append(load_weights(copies, info, in_refs[e], in_layout, in_s, 2 * e * ffe, False))
        if e == 0:
            got_d = [copies.start(d_refs[p], d_s.at[place[p]]) for p in range(parts)]
        got_down.append(
            load_weights(copies, info, down_refs[e], down_layout, down_s, e * ffe, True)
        )
    lanes = lax.broadcasted_iota(jnp.int32, (rows, 128), 1)
    finish(got_x)
    bias = []
    for p in range(parts):
        first = slots[p][1]
        named = jnp.transpose(route_s[p].astype(F32))[first : first + rows].astype(jnp.int32)
        hit = named[:, 0:1] == lanes
        for k in range(1, 8):
            hit = hit | (named[:, k : k + 1] == lanes)
        bias.append(jnp.where(hit, 0.0, -1e30))
    logits = nn(x_s[...], router_s[...]) + jnp.concatenate(bias, axis=0)
    grown = jnp.exp(logits - jnp.max(logits, axis=-1, keepdims=True))
    shares = grown / jnp.sum(grown, axis=-1, keepdims=True)
    share_out[...] = shares
    lanes = lax.broadcasted_iota(jnp.int32, (total, 128), 1)
    gate_cols = jnp.zeros((total, 128), F32)
    sent = []
    for e in range(2):
        share = RES_SCALE * jnp.sum(
            jnp.where(lanes == info[e], shares, 0.0), axis=1, keepdims=True
        )
        gate_grad = jnp.zeros((total, 1), F32)
        finish(got_in[e])
        gate_s[...] = nn(x_s[...], in_s[:, pl.ds(2 * e * ffe, 2 * ffe)])
        finish((got_d if e == 0 else []) + got_down[e])
        pulled_s[...] = nt(d_s[...], down_s[pl.ds(e * ffe, ffe), :])
        for j in range(ffe // tile):
            gate_at = 2 * e * ffe + j * tile
            gate = gate_s[:, pl.ds(j * tile, tile)]
            up = gate_s[:, pl.ds(ffe + j * tile, tile)]
            pulled = pulled_s[:, pl.ds(j * tile, tile)]
            sigmoid = 0.5 * jnp.tanh(0.5 * gate) + 0.5
            swish = gate * sigmoid
            hidden = swish * up
            gate_grad = gate_grad + jnp.sum(hidden * pulled, axis=1, keepdims=True)
            hidden_grad = share * pulled
            low_s[:, pl.ds(gate_at, tile)] = (
                hidden_grad * up * (sigmoid * (1.0 + gate - swish))
            ).astype(BF16)
            low_s[:, pl.ds(gate_at + ffe, tile)] = (hidden_grad * swish).astype(BF16)
            mixed_s[:, pl.ds(e * ffe + j * tile, tile)] = (
                share * (1.0 / RES_SCALE) * hidden
            ).astype(BF16)
        gate_cols = gate_cols + jnp.where(lanes == e, RES_SCALE * gate_grad, 0.0)
    sent.append(copies.start(low_s, low_out))
    sent.append(copies.start(mixed_s, mixed_out))
    step = 768
    for n in range(width // step):
        at = pl.ds(n * step, step)
        row_s[:, at] = nt(low_s[...], in_s[at, :]).astype(BF16)
        for p in range(parts):
            sent.append(copies.start(row_s.at[place[p], at], row_outs[p].at[:, at]))
    for p in range(parts):
        gate_outs[p][...] = jnp.transpose(gate_cols[p * rows : (p + 1) * rows])[:8]
    finish(sent)


def run_experts(slots, info, x_list, d_list, routes, router, weights, layouts):
    parts = len(slots)
    rows, width = x_list[0].shape
    ffe = weights[0][0].shape[1] // 2
    total = parts * rows
    out_shape = [
        jax.ShapeDtypeStruct((total, 4 * ffe), BF16),
        jax.ShapeDtypeStruct((total, 2 * ffe), BF16),
    ]
    out_shape += [jax.ShapeDtypeStruct((rows, width), BF16)] * parts
    out_shape += [jax.ShapeDtypeStruct((8, rows), F32)] * parts
    out_shape += [jax.ShapeDtypeStruct((total, 128), F32)]
    operands = [*x_list, *d_list, *routes, router]
    for group in (weights[0], weights[2], weights[1], weights[3]):
        operands += list(group)
    here = pl.BlockSpec(memory_space=pltpu.VMEM)
    anywhere = pl.BlockSpec(memory_space=pltpu.HBM)
    copies = 3 * parts + 1 + sum(len(w) for w in weights) + 2 + parts * (width // 256)
    in_specs = [anywhere] * len(operands)
    outs = pl.pallas_call(
        partial(expert_kernel, slots, *layouts),
        in_specs=[pl.BlockSpec(memory_space=pltpu.SMEM)] + in_specs,
        out_specs=[anywhere] * (2 + parts) + [here] * (parts + 1),
        out_shape=out_shape,
        scratch_shapes=[
            pltpu.VMEM((total, width), BF16),
            pltpu.VMEM((total, width), BF16),
            pltpu.VMEM((width, 4 * ffe), BF16),
            pltpu.VMEM((2 * ffe, width), BF16),
            pltpu.VMEM((width, 128), BF16),
            pltpu.VMEM((parts, 16, slots[0][2]), BF16),
            pltpu.VMEM((total, 4 * ffe), BF16),
            pltpu.VMEM((total, 2 * ffe), BF16),
            pltpu.VMEM((total, width), BF16),
            pltpu.VMEM((total, 2 * ffe), F32),
            pltpu.VMEM((total, ffe), F32),
            pltpu.SemaphoreType.DMA((copies,)),
        ],
        compiler_params=pltpu.CompilerParams(vmem_limit_bytes=BIG_VMEM),
        cost_estimate=pl.CostEstimate(
            flops=20 * total * width * ffe,
            bytes_accessed=12 * ffe * width + 12 * total * width,
            transcendentals=total * ffe * 2,
        ),
    )(info, *operands)
    return outs[0], outs[1], outs[2 : 2 + parts], outs[2 + parts : 2 + 2 * parts], outs[-1]


def result_kernel(heights, out_heights, down_layout, info, *refs):
    refs = list(refs)
    take = lambda n: [refs.pop(0) for _ in range(n)]
    mixed_refs = take(len(heights))
    down_refs = [take(len(down_layout)), take(len(down_layout))]
    outs = take(len(out_heights))
    mixed_s, down_s, out_s, sems = refs
    ffe = down_s.shape[0] // 2
    copies = Copies(sems)
    got = [
        made
        for e in range(2)
        for made in load_weights(copies, info, down_refs[e], down_layout, down_s, e * ffe, True)
    ]
    start, waits = 0, []
    for ref, height in zip(mixed_refs, heights):
        waits.append(copies.start(ref, mixed_s.at[pl.ds(start, height)]))
        start += height
    finish(got)
    sent, start, place, at = [], 0, 0, 0
    for i, height in enumerate(heights):
        finish([waits[i]])
        rows = pl.ds(start, height)
        for n in range(down_s.shape[1] // 512):
            cols = pl.ds(n * 512, 512)
            out_s[rows, cols] = nn(mixed_s[rows, :], down_s[:, cols]).astype(BF16)
        start += height
        while place < len(outs) and at + out_heights[place] <= start:
            sent.append(copies.start(out_s.at[pl.ds(at, out_heights[place])], outs[place]))
            at += out_heights[place]
            place += 1
    finish(sent)


def run_results(info, mixeds, weights, layouts, out_heights):
    heights = [m.shape[0] for m in mixeds]
    total, cols = sum(heights), mixeds[0].shape[1]
    width = sum(number for _, _, number, _ in layouts[1])
    anywhere = pl.BlockSpec(memory_space=pltpu.HBM)
    operands = [*mixeds, *weights[1], *weights[3]]
    return pl.pallas_call(
        partial(result_kernel, heights, out_heights, layouts[1]),
        in_specs=[pl.BlockSpec(memory_space=pltpu.SMEM)] + [anywhere] * len(operands),
        out_specs=[anywhere] * len(out_heights),
        out_shape=[jax.ShapeDtypeStruct((h, width), BF16) for h in out_heights],
        scratch_shapes=[
            pltpu.VMEM((total, cols), BF16),
            pltpu.VMEM((cols, width), BF16),
            pltpu.VMEM((total, width), BF16),
            pltpu.SemaphoreType.DMA((len(operands) + len(out_heights),)),
        ],
        compiler_params=pltpu.CompilerParams(vmem_limit_bytes=BIG_VMEM),
        cost_estimate=pl.CostEstimate(
            flops=2 * total * cols * width,
            bytes_accessed=2 * (total * (cols + width) + cols * width),
            transcendentals=0,
        ),
    )(info, *operands)


def sort_gates_kernel(counts, info, *refs):
    out = refs[-1]
    for i, many in enumerate(counts):
        pieces = refs[sum(counts[:i]) : sum(counts[: i + 1])]
        at = 0
        for ref in pieces:
            cols = ref.shape[1]
            out[info[info.shape[0] - len(counts) + i], :, at : at + cols] = ref[0:2, :]
            at += cols


def sort_gates(info, parts, rows):
    flat = [ref for part in parts for ref in part]
    return pl.pallas_call(
        partial(sort_gates_kernel, [len(p) for p in parts]),
        in_specs=[pl.BlockSpec(memory_space=pltpu.SMEM)]
        + [pl.BlockSpec(memory_space=pltpu.VMEM)] * len(flat),
        out_specs=pl.BlockSpec(memory_space=pltpu.VMEM),
        out_shape=jax.ShapeDtypeStruct((len(parts), 2, rows), F32),
    )(info, *flat)


def spread_kernel(widths, kept, first, places, *refs):
    count = len(refs) - kept - 2 * len(widths) - 1
    blocks, refs = refs[:count], refs[count + kept :]
    outs, scratch, sems = refs[: len(widths)], refs[len(widths) : -1], refs[-1]
    copies, sent = Copies(sems), []
    for i, ref in enumerate(blocks):
        at = 0
        for out, buffer, wide in zip(outs, scratch, widths):
            buffer[i] = ref[:, at : at + wide].astype(F32)
            sent.append(copies.start(buffer.at[i], out.at[places[first + i]]))
            at += wide
    finish(sent)


def spread(places, first, blocks, widths, total, kept=()):
    count, height = len(blocks), blocks[0].shape[0]
    anywhere = pl.BlockSpec(memory_space=pltpu.HBM)
    return pl.pallas_call(
        partial(spread_kernel, widths, len(kept), first),
        in_specs=[pl.BlockSpec(memory_space=pltpu.SMEM)]
        + [pl.BlockSpec(memory_space=pltpu.VMEM)] * count
        + [anywhere] * len(kept),
        out_specs=[anywhere] * len(widths),
        out_shape=[jax.ShapeDtypeStruct((total, height, wide), F32) for wide in widths],
        scratch_shapes=[pltpu.VMEM((count, height, wide), F32) for wide in widths]
        + [pltpu.SemaphoreType.DMA((count * len(widths),))],
        input_output_aliases={1 + count + i: i for i in range(len(kept))},
        compiler_params=pltpu.CompilerParams(vmem_limit_bytes=40 * MIB),
    )(places, *blocks, *kept)


def weight_grad_kernel(heights, a_at, b_at, scale, by_rows, added, info, *refs):
    refs = list(refs)
    take = lambda n: [refs.pop(0) for _ in range(n)]
    a_refs, b_refs, more = take(len(heights[0])), take(len(heights[1])), take(added)
    a_s, b_s, sems = refs[-3:]
    outs = refs[:-3]
    step, steps = pl.program_id(0), pl.num_programs(0)
    tile = outs[0].shape[0 if by_rows else 1]

    def loads(parts, heights_of, scratch, at, tiled):
        made, start = [], 0
        for ref, height in zip(parts, heights_of):
            for t in range(steps_static if tiled else 1):
                wide = tile if tiled else scratch.shape[1]
                made.append(
                    (
                        t,
                        ref.at[:, pl.ds(at + t * wide, wide)],
                        scratch.at[pl.ds(start, height), pl.ds(t * wide, wide)],
                    )
                )
            start += height
        return made

    steps_static = (a_s if by_rows else b_s).shape[1] // tile
    first = loads(a_refs, heights[0], a_s, a_at, by_rows)
    second = loads(b_refs, heights[1], b_s, b_at, not by_rows)
    whole, tiled = (second, first) if by_rows else (first, second)
    tiled.sort(key=lambda entry: entry[0])
    copies = Copies(sems)
    made_whole = [copies.make(src, dst) for _, src, dst in whole]
    made_tiled = [(t, copies.make(src, dst)) for t, src, dst in tiled]

    @pl.when(step == 0)
    def _():
        for made in made_whole:
            made.start()
        for _, made in made_tiled:
            made.start()
        finish(made_whole)

    for t in range(steps_static):

        @pl.when(step == t)
        def _(t=t):
            finish([made for at, made in made_tiled if at == t])

    at = pl.ds(pl.multiple_of(step * tile, 128), tile)
    if by_rows:
        grad = tn(a_s[:, at], b_s[...])
    else:
        grad = tn(a_s[...], b_s[:, at])
    grad = scale * grad
    shards = len(outs) // (1 if by_rows else 2)
    place = lax.rem(step // (steps // shards) - info[2] + shards, shards)
    count = outs[0].shape[0]
    for i, out in enumerate(outs):
        value = grad if by_rows else grad[i // shards * count : (i // shards + 1) * count]

        @pl.when(place == i % shards)
        def _(i=i, out=out, value=value):
            if added:
                out[...] = (value + more[i][...].astype(F32)).astype(BF16)
            else:
                out[...] = value.astype(BF16)


def weight_grad(
    info, shards, a_list, a_at, a_cols, b_list, b_at, b_cols, scale=1.0, by_rows=True, more=()
):
    heights = ([a.shape[0] for a in a_list], [b.shape[0] for b in b_list])
    total = sum(heights[0])
    each = (a_cols if by_rows else b_cols) // shards
    tile = 256 if each % 256 == 0 else each
    tiles = each // tile
    shape = (each, b_cols) if by_rows else (a_cols // 2, each)
    many = shards if by_rows else 2 * shards
    anywhere = pl.BlockSpec(memory_space=pltpu.HBM)

    def tile_of(r):
        def index(i, info):
            at = jnp.clip(i - lax.rem(info[2] + r, shards) * tiles, 0, tiles - 1)
            return (at, 0) if by_rows else (0, at)

        block = (tile, b_cols) if by_rows else (a_cols // 2, tile)
        return pl.BlockSpec(block, index)

    parts_a = len(a_list) * (shards * tiles if by_rows else 1)
    parts_b = len(b_list) * (1 if by_rows else shards * tiles)
    return pl.pallas_call(
        partial(weight_grad_kernel, heights, a_at, b_at, scale, by_rows, len(more)),
        grid_spec=pltpu.PrefetchScalarGridSpec(
            num_scalar_prefetch=1,
            grid=(shards * tiles,),
            in_specs=[anywhere] * (len(a_list) + len(b_list))
            + [tile_of(r) for r in range(len(more))],
            out_specs=[tile_of(i % shards) for i in range(many)],
            scratch_shapes=[
                pltpu.VMEM((total, a_cols), BF16),
                pltpu.VMEM((total, b_cols), BF16),
                pltpu.SemaphoreType.DMA((parts_a + parts_b,)),
            ],
        ),
        out_shape=[jax.ShapeDtypeStruct(shape, BF16)] * many,
        compiler_params=pltpu.CompilerParams(vmem_limit_bytes=BIG_VMEM),
        cost_estimate=pl.CostEstimate(
            flops=2 * total * a_cols * b_cols,
            bytes_accessed=2 * (total * (a_cols + b_cols) + a_cols * b_cols),
            transcendentals=0,
        ),
    )(info, *a_list, *b_list, *more)


def dense_grad_kernel(unit, shards, small_too, info, places, *refs):
    sources, refs = refs[:2], refs[2:]
    extras, refs = (refs[:3], refs[3:]) if small_too else ((), refs)
    mine, theirs, a_s, b_s, scratch, sems = refs[:6]
    copies, sent = Copies(sems), []
    got = [copies.start(ref, to) for ref, to in zip(sources, (a_s, b_s))]
    flat = len(scratch.shape) == 2
    cols = b_s.shape[1]
    count = 2 * mine.shape[0]
    wide = mine.shape[2] // shards
    tile = 256 if flat else 384
    core = info[0] % 2
    if small_too:
        small, width = refs[6], a_s.shape[1]
        turned = jnp.transpose(
            jnp.concatenate([extras[0][...], extras[1][...], jnp.zeros((6, width), F32)], axis=0)
        )
        lanes = lax.broadcasted_iota(jnp.int32, (width, 128), 1)
        small[...] = jnp.where(
            lanes == count,
            turned[:, 0:1],
            jnp.where(lanes == count + 1, turned[:, 1:2], extras[2][...]),
        ).astype(BF16)
        if flat:
            scratch[:, cols:] = small[...]
    finish(got)
    ready = 0
    for t in range(a_s.shape[1] // tile):
        grad = tn(a_s[:, t * tile : (t + 1) * tile], b_s[...]).astype(BF16)
        if flat:
            scratch[t * tile : (t + 1) * tile, 0:cols] = grad
        while (ready + 1) * unit <= (t + 1) * tile:
            if flat:
                block = scratch.at[pl.ds(ready * unit, unit), :]
            else:
                first = ready * unit - t * tile
                scratch[ready, :, 0:cols] = grad[first : first + unit]
                if small_too:
                    scratch[ready, :, cols:] = small[ready * unit : (ready + 1) * unit, :]
                block = scratch.at[ready]
            name, turn = ready % count, ready // count
            place = places[name // 2]
            if shards > 1:
                turn = lax.rem(turn - info[2] + shards, shards)
            at = pl.ds(pl.multiple_of(turn * wide, 128), wide)
            to_mine = copies.make(block, mine.at[place, :, at])
            to_theirs = pltpu.make_async_copy(
                block, theirs.at[place, :, at], sems.at[copies.used - 1]
            )

            @pl.when(core == name % 2)
            def _(one=to_mine):
                one.start()

            @pl.when(core != name % 2)
            def _(one=to_theirs):
                one.start()

            sent.append(to_mine)
            ready += 1
    finish(sent)


def dense_grad(info, places, unit, shards, a, b, extras=()):
    length, rows = a.shape
    cols = b.shape[1]
    chips = places.shape[0]
    wide = cols + (128 if extras else 0)
    here = pl.BlockSpec(memory_space=pltpu.VMEM)
    anywhere = pl.BlockSpec(memory_space=pltpu.HBM)
    small = pl.BlockSpec(memory_space=pltpu.SMEM)
    flat = unit % 16 == 0
    many = rows // unit
    scratch = [
        pltpu.VMEM(a.shape, BF16),
        pltpu.VMEM(b.shape, BF16),
        pltpu.VMEM((rows, wide) if flat else (many, unit, wide), BF16),
        pltpu.SemaphoreType.DMA((2 + many,)),
    ]
    if extras:
        scratch.append(pltpu.VMEM((rows, 128), BF16))
    return pl.pallas_call(
        partial(dense_grad_kernel, unit, shards, bool(extras)),
        in_specs=[small] * 2 + [anywhere] * 2 + [here] * len(extras),
        out_specs=[anywhere] * 2,
        out_shape=[jax.ShapeDtypeStruct((chips, unit, shards * wide), BF16)] * 2,
        scratch_shapes=scratch,
        compiler_params=pltpu.CompilerParams(vmem_limit_bytes=BIG_VMEM),
        cost_estimate=pl.CostEstimate(
            flops=6 * length * rows * cols,
            bytes_accessed=2 * length * (rows + cols),
            transcendentals=0,
        ),
    )(info, places, a, b, *extras)


def normed_back_kernel(grads, weight, tokens, low_out, gain_out):
    grad = nt(grads[...], weight[...])
    rows = tokens[...].astype(F32)
    unit = rows * lax.rsqrt(jnp.mean(rows * rows, axis=-1, keepdims=True) + EPSILON)
    gain_out[...] = jnp.sum(grad * unit, axis=0, keepdims=True)
    low_out[...] = grad.astype(BF16)


def normed_back(grads, weight, tokens):
    length, width = tokens.shape
    here = pl.BlockSpec(memory_space=pltpu.VMEM)
    return pl.pallas_call(
        normed_back_kernel,
        in_specs=[here] * 3,
        out_specs=[here] * 2,
        out_shape=[
            jax.ShapeDtypeStruct((length, width), BF16),
            jax.ShapeDtypeStruct((1, width), F32),
        ],
        compiler_params=pltpu.CompilerParams(vmem_limit_bytes=40 * MIB),
        cost_estimate=pl.CostEstimate(
            flops=2 * length * width * grads.shape[1],
            bytes_accessed=2 * (grads.size + weight.size + 2 * tokens.size),
            transcendentals=0,
        ),
    )(grads, weight, tokens)


def project_kernel(shards, q_cols, k_cols, unit, info, places, own_ref, gain_ref, *refs):
    token_refs, refs = refs[:shards], refs[shards:]
    blocks, (normed_out, cols_out, out, tokens_out, w_s, t_s, sems) = refs[:-7], refs[-7:]
    count = own_ref.shape[0]
    rows = token_refs[0].shape[0]
    copies = Copies(sems)
    shard = info[2]
    key_at, value_at = q_cols * shards, (q_cols + k_cols) * shards
    made, to = [], 0
    for s in range(shards):
        at = pl.ds(pl.multiple_of(info[2 + s] * rows, 16), rows)
        made.append(copies.start(token_refs[s], t_s.at[at]))
    for at, wide in ((0, q_cols), (key_at, k_cols), (value_at, k_cols)):
        cols = pl.ds(pl.multiple_of(at + shard * wide, 128), wide)
        made.append(
            copies.start(
                own_ref.at[:, cols],
                w_s.at[pl.ds(pl.multiple_of(shard * count, 16), count), pl.ds(to, wide)],
            )
        )
        to += wide
    for i, ref in enumerate(blocks):
        at = pl.ds(pl.multiple_of(places[i] * unit, 16), unit)
        made.append(copies.start(ref.at[pl.ds(0, unit)], w_s.at[at]))
    finish(made[:shards])
    value = t_s[...].astype(F32)
    normed_out[...] = (
        value
        * lax.rsqrt(jnp.mean(value * value, axis=-1, keepdims=True) + EPSILON)
        * gain_ref[...]
    ).astype(BF16)
    finish(made[shards:])
    sent = [copies.start(w_s, cols_out), copies.start(t_s, tokens_out)]
    out[...] = nn(normed_out[...], w_s[...])
    finish(sent)


def project(info, places, own, gain, tokens, blocks, shards, q_cols, k_cols, unit):
    rows, width = tokens[0].shape
    cols = q_cols + 2 * k_cols
    anywhere = pl.BlockSpec(memory_space=pltpu.HBM)
    here = pl.BlockSpec(memory_space=pltpu.VMEM)
    small = pl.BlockSpec(memory_space=pltpu.SMEM)
    return pl.pallas_call(
        partial(project_kernel, shards, q_cols, k_cols, unit),
        in_specs=[small, small, anywhere, here] + [anywhere] * (shards + len(blocks)),
        out_specs=[here, anywhere, here, anywhere],
        out_shape=[
            jax.ShapeDtypeStruct((shards * rows, width), BF16),
            jax.ShapeDtypeStruct((width, cols), BF16),
            jax.ShapeDtypeStruct((shards * rows, cols), F32),
            jax.ShapeDtypeStruct((shards * rows, width), BF16),
        ],
        scratch_shapes=[
            pltpu.VMEM((width, cols), BF16),
            pltpu.VMEM((shards * rows, width), BF16),
            pltpu.SemaphoreType.DMA((shards + 5 + len(blocks),)),
        ],
        compiler_params=pltpu.CompilerParams(vmem_limit_bytes=BIG_VMEM),
        cost_estimate=pl.CostEstimate(
            flops=2 * shards * rows * width * cols,
            bytes_accessed=2 * (width * cols + shards * rows * (2 * width + 2 * cols)),
            transcendentals=0,
        ),
    )(info, places, own, gain, *tokens, *blocks)


def router_back_kernel(experts, info, gate_ref, share_ref, second_ref, router_ref, grad_ref, add_ref):
    core = info[0] % 2
    rows = second_ref.shape[0]
    turned = jnp.transpose(
        jnp.concatenate([gate_ref[c] for c in range(experts // 2)], axis=0)
    )
    kept = jnp.concatenate([turned, jnp.zeros((rows, 128 - experts), F32)], axis=1)
    lanes = lax.broadcasted_iota(jnp.int32, (rows, 128), 1)
    swapped = jnp.where(lanes % 2 == 0, pltpu.roll(kept, 127, 1), pltpu.roll(kept, 1, 1))
    gates = jnp.where(core == 0, kept, swapped)
    share = share_ref[...]
    dot = jnp.sum(share * gates, axis=1, keepdims=True)
    low = (share * (gates - dot)).astype(BF16)
    grad_ref[...] = tn(second_ref[...], low)
    add_ref[...] = nt(low, router_ref[...])


def router_back(info, gates, shares, second, router, experts):
    rows, width = second.shape
    here = pl.BlockSpec(memory_space=pltpu.VMEM)
    return pl.pallas_call(
        partial(router_back_kernel, experts),
        in_specs=[pl.BlockSpec(memory_space=pltpu.SMEM)] + [here] * 4,
        out_specs=[here] * 2,
        out_shape=[
            jax.ShapeDtypeStruct((width, 128), F32),
            jax.ShapeDtypeStruct((rows, width), F32),
        ],
        compiler_params=pltpu.CompilerParams(vmem_limit_bytes=16 * MIB),
    )(info, gates, shares, second, router)


def middle_back_kernel(own, right, left, add, middle, gain, upstream, low_out, grad_out, gain_out):
    grad = own[...].astype(F32) + right[...].astype(F32) + left[...].astype(F32) + add[...]
    rows = middle[...]
    scale = lax.rsqrt(jnp.mean(rows * rows, axis=-1, keepdims=True) + EPSILON)
    unit = rows * scale
    share = jnp.sum(grad * unit, axis=0, keepdims=True)
    gain_out[...] = share + jnp.where(pl.program_id(0) == 0, 0.0, gain_out[...])
    weighted = grad * gain[...]
    dot = jnp.mean(weighted * unit, axis=-1, keepdims=True)
    total = upstream[...].astype(F32) + scale * (weighted - unit * dot)
    grad_out[...] = total
    low_out[...] = (RES_SCALE * total).astype(BF16)


def middle_back(own, right, left, add, middle, gain, upstream):
    rows, width = middle.shape
    block = rows // 4
    some = pl.BlockSpec((block, width), lambda i: (i, 0))
    one = pl.BlockSpec((1, width), lambda i: (0, 0))
    return pl.pallas_call(
        middle_back_kernel,
        grid=(4,),
        in_specs=[some] * 5 + [one, some],
        out_specs=[some, some, one],
        out_shape=[
            jax.ShapeDtypeStruct((rows, width), BF16),
            jax.ShapeDtypeStruct((rows, width), F32),
            jax.ShapeDtypeStruct((1, width), F32),
        ],
        compiler_params=pltpu.CompilerParams(vmem_limit_bytes=BIG_VMEM),
    )(own, right, left, add, middle, gain, upstream)


def ring_add_kernel(right, left, front, back, *outs):
    half = right.shape[0]
    if half < front.shape[0]:
        right_out, left_out = outs
        right_out[:half] = add_low(right[...], front[:half])
        right_out[half:] = front[half:]
        left_out[:half] = back[:half]
        left_out[half:] = add_low(left[...], back[half:])
        return
    for came, own, places in ((right, front, outs[: len(outs) // 2]), (left, back, outs[len(outs) // 2 :])):
        at = 0
        for out in places:
            rows = out.shape[0]
            out[...] = add_low(came[at : at + rows], own[at : at + rows])
            at += rows


def add_both(right, left, front, back, halved=False):
    here = pl.BlockSpec(memory_space=pltpu.VMEM)
    rows, width = front.shape
    shapes = [(rows // 2, width)] * 4 if halved else [(rows, width)] * 2
    return pl.pallas_call(
        ring_add_kernel,
        in_specs=[here] * 4,
        out_specs=[here] * len(shapes),
        out_shape=[jax.ShapeDtypeStruct(shape, front.dtype) for shape in shapes],
        compiler_params=pltpu.CompilerParams(vmem_limit_bytes=16 * MIB),
        cost_estimate=pl.CostEstimate(flops=1, bytes_accessed=12 * front.size, transcendentals=0),
    )(right, left, front, back)


def sum_blocks_kernel(plan, starts, *refs):
    arrays, refs = refs[: 2 * len(starts)], refs[2 * len(starts) :]
    many = len(plan)
    total = sum(len(came) for _, _, _, came in plan)
    refs, outs, (scratch, sems) = refs[:total], refs[total : total + many], refs[-2:]
    copies = Copies(sems)
    made = []
    for i, (place, low, high, _) in enumerate(plan):
        made.append([])
        for start, pair in zip(starts, (arrays[k : k + 2] for k in range(0, len(arrays), 2))):
            first, last = max(low, start), min(high, start + pair[0].shape[2])
            if first >= last:
                continue
            for j, ref in enumerate(pair):
                made[-1].append(
                    copies.start(
                        ref.at[place, :, pl.ds(first - start, last - first)],
                        scratch.at[2 * i + j, :, pl.ds(first - low, last - first)],
                    )
                )
    at = 0
    for i, (_, low, high, came) in enumerate(plan):
        finish(made[i])
        wide = high - low
        value = scratch[2 * i, :, :wide].astype(F32) + scratch[2 * i + 1, :, :wide].astype(F32)
        outs[i][...] = value.astype(BF16)
        for start, stop in came:
            part = value[:, start - low : stop - low] + refs[at][...].astype(F32)
            at += 1
            if (start, stop) == (low, high):
                value = part
            outs[i][:, start - low : stop - low] = part.astype(BF16)


def sum_blocks(pairs, wanted):
    unit = pairs[0][0].shape[1]
    starts = [sum(p[0].shape[2] for p in pairs[:i]) for i in range(len(pairs))]
    every = sum(p[0].shape[2] for p in pairs)
    plan, flat = [], []
    for place, low, high, came in wanted:
        plan.append((place, low, high, [(at, at + c.shape[1]) for at, c in came]))
        flat += [c for _, c in came]
    anywhere = pl.BlockSpec(memory_space=pltpu.HBM)
    here = pl.BlockSpec(memory_space=pltpu.VMEM)
    arrays = [array for pair in pairs for array in pair]
    return pl.pallas_call(
        partial(sum_blocks_kernel, plan, starts),
        in_specs=[anywhere] * len(arrays) + [here] * len(flat),
        out_specs=[here] * len(plan),
        out_shape=[jax.ShapeDtypeStruct((unit, high - low), BF16) for _, low, high, _ in plan],
        scratch_shapes=[
            pltpu.VMEM((2 * len(plan), unit, every), BF16),
            pltpu.SemaphoreType.DMA((len(arrays) * len(plan),)),
        ],
        compiler_params=pltpu.CompilerParams(vmem_limit_bytes=16 * MIB),
        cost_estimate=pl.CostEstimate(
            flops=1, bytes_accessed=6 * len(plan) * unit * every, transcendentals=0
        ),
    )(*arrays, *flat)


def body(
    tokens,
    segment_ids,
    routes,
    norm1_gain,
    norm2_gain,
    qkv_weight,
    out_weight,
    route_weight,
    expert_in,
    expert_down,
    cotangent,
):
    rows, width = tokens.shape
    shards = lax.axis_size("shard")
    chips = lax.axis_size("chip")
    experts = 2 * chips
    length = rows * shards
    q_cols = QUERY_HEADS // shards * HEAD_SIZE
    k_cols = KEY_VALUE_HEADS // shards * HEAD_SIZE
    own_cols = q_cols + 2 * k_cols
    query_width = QUERY_HEADS * HEAD_SIZE
    pair_width = KEY_VALUE_HEADS * HEAD_SIZE
    ffe = expert_down.shape[1]
    cut = width // shards
    shard = lax.axis_index("shard")
    core = lax.axis_index("core")
    chip = lax.axis_index("chip")
    walk = ring_chips(chips)
    ahead = [(walk[i], walk[(i + 1) % chips]) for i in range(chips)]
    behind = [(b, a) for a, b in ahead]
    half_ring = chips // 2
    order = [0]
    for step in range(1, half_ring):
        order += [-step, step]
    order.append(half_ring)
    place_of = {c: i for i, c in enumerate(walk)}
    chip_tables = np.array([[walk[(place_of[c] + o) % chips] for o in order] for c in range(chips)])
    senders = jnp.asarray(chip_tables, jnp.int32)[chip]
    info = jnp.concatenate(
        [
            jnp.stack([2 * chip + core, 2 * chip + 1 - core]),
            (shard - jnp.arange(shards) + shards) % shards,
            senders,
        ]
    ).astype(jnp.int32)
    slot_of = lambda i: 2 + shards + i
    both_cores = jnp.concatenate([2 * senders + core, 2 * senders + 1 - core])
    rel_tables = np.array([[list(row).index(c) for c in range(chips)] for row in chip_tables])
    chip_places = jnp.asarray(rel_tables, jnp.int32)[chip]

    def to_shard(value, step):
        return lax.ppermute(value, "shard", [(i, (i + step) % shards) for i in range(shards)])

    def to_core(value):
        return lax.ppermute(value, "core", [(0, 1), (1, 0)])

    def in_order(pieces):
        out = []
        for j in range(shards):
            value = pieces[0]
            for s in range(1, shards):
                value = jnp.where((shard - j + shards) % shards == s, pieces[s], value)
            out.append(value)
        return out

    def exchange_shards(piece_for):
        got = [piece_for(shard)]
        for s in range(1, shards):
            got.append(to_shard(piece_for(lax.rem(shard + s, shards)), s))
        return got

    def sum_shards(piece_for):
        got = exchange_shards(piece_for)
        total = got[0].astype(F32)
        for piece in got[1:]:
            total = total + piece.astype(F32)
        return total

    def to_holders(parts):
        return [parts[0]] + [to_shard(parts[s], s) for s in range(1, shards)]

    def ring_step(pair, cut_far=False):
        right, left = pair
        if cut_far:
            right, left = right[: rows // 2], left[rows // 2 :]
        return lax.ppermute(right, "chip", ahead), lax.ppermute(left, "chip", behind)

    def ring_gather(value):
        out, pair = [value], (value, value)
        for step in range(1, half_ring + 1):
            pair = ring_step(pair, step == half_ring)
            out += pair
        return out

    def ring_start(parts):
        return lax.ppermute(parts[-2], "chip", ahead), lax.ppermute(parts[-1], "chip", behind)

    def ring_add(parts, step, got):
        return tuple(add_both(*got, parts[2 * step], parts[2 * step - 1]))

    def ring_send(sent):
        return lax.ppermute(sent[0], "chip", ahead), lax.ppermute(sent[1], "chip", behind)

    def ring_end(parts, got):
        return parts[0].astype(F32) + got[0].astype(F32) + got[1].astype(F32)

    def plane_gather(value, beside, use_early):
        right = left = value
        got = [value]
        half = value.shape[1] // 256 * 128
        for step in range(1, half_ring + 1):
            if step > 1:
                right, left, beside[step] = lax.optimization_barrier(
                    (right, left, beside.get(step, ()))
                )
            if step == half_ring:
                right, left = right[:, :half], left[:, half:]
            right = lax.ppermute(right, "chip", ahead)
            left = lax.ppermute(left, "chip", behind)
            if step < half_ring:
                got += [right, left]
        early = 2 * half_ring - 3
        used = use_early(got[:early] + [to_core(v) for v in got[:early]])
        right, left, used = lax.optimization_barrier((right, left, used))
        late = got[early:] + [jnp.concatenate([right, left], axis=1)]
        return used, late + [to_core(v) for v in late]

    def block_ring(values, beside):
        right = left = values
        got = [values]
        for step in range(1, half_ring + 1):
            if step > 1:
                right, left, beside = lax.optimization_barrier(
                    (right, left, beside)
                ) if step == 3 else (*lax.optimization_barrier((right, left)), beside)
            right = [lax.ppermute(v, "chip", ahead) for v in right]
            got.append(right)
            if step < half_ring:
                left = [lax.ppermute(v, "chip", behind) for v in left]
                got.append(left)
        return got + [[to_core(v) for v in values] for values in got], beside

    def own_columns(rows_at, count, target):
        return jnp.concatenate(
            [
                lax.dynamic_slice(qkv_weight, (rows_at, at + target * cols), (count, cols))
                for at, cols in (
                    (0, q_cols),
                    (query_width, k_cols),
                    (query_width + pair_width, k_cols),
                )
            ],
            axis=1,
        )

    unit = cut // experts
    name = 2 * chip + core
    units = [
        to_shard(own_columns(name * unit, unit, lax.rem(shard + s, shards)), s)
        for s in range(1, shards)
    ]
    tokens_got = [tokens] + [to_shard(tokens, s) for s in range(1, shards)]
    extras = jnp.concatenate(
        [norm1_gain, norm2_gain, segment_ids.astype(BF16), route_weight.reshape(-1)]
    ).reshape(-1, 256)
    extras = [extras] + [to_shard(extras, s) for s in range(1, shards)]
    named = jnp.pad(routes.T.astype(BF16), ((0, 16 - routes.shape[1]), (0, own_cols - rows)))
    together = unit % 16 == 0
    if together:
        units[0] = jnp.concatenate([units[0], named], axis=0)
    else:
        units.append(named)
    blocks, (tokens_got, extras) = block_ring(units, (tokens_got, extras))

    held_in, held_down = tie((expert_in[0], expert_down[0]), tokens_got)
    down_own = [held_down] + [to_shard(held_down, s) for s in range(1, shards)]
    in_own = [held_in] + [to_shard(held_in, s) for s in range(1, shards)]
    layouts = ([(s, 0, cut, cut) for s in range(shards)],) * 2
    blocks, down_own, upstream = lax.optimization_barrier((blocks, down_own, cotangent))
    dy_pair = ring_step((upstream, upstream))
    upstream_chunks = [cotangent, *dy_pair]
    named_chunks = [b[0 if together else -1] for b in blocks[:chips]]
    named_at = unit if together else 0
    block_list = [b[s] for s in range(shards - 1) for b in blocks]
    block_places = jnp.concatenate(
        [info[2 + s] * experts + both_cores for s in range(1, shards)]
    ).astype(jnp.int32)
    extras = jnp.stack(in_order(extras)).reshape(shards, -1)
    gain_one = extras[:, :cut].reshape(1, -1).astype(F32)
    gain_two = extras[:, cut : 2 * cut].reshape(1, -1).astype(F32)
    segments = extras[:, 2 * cut : 2 * cut + rows].reshape(-1).astype(F32)
    router = extras[:, 2 * cut + rows :].reshape(width, experts)
    router_wide = jnp.pad(router, ((0, 0), (0, 128 - experts)))

    inputs = tokens.astype(F32)
    if together:
        normed, qkv_cols, projected, all_tokens = project(
            info, block_places, qkv_weight, gain_one, tokens_got, block_list, shards, q_cols, k_cols, unit
        )
    else:
        placed = jnp.zeros((shards * experts, unit, own_cols), BF16)
        for i, piece in enumerate(block_list):
            placed = lax.dynamic_update_index_in_dim(placed, piece, block_places[i], 0)
        qkv_cols = lax.dynamic_update_slice(
            placed.reshape(width, own_cols), own_columns(0, cut, shard), (shard * cut, 0)
        )
        all_tokens = jnp.concatenate(in_order(tokens_got), axis=0)
        wide_tokens = all_tokens.astype(F32)
        normed = (wide_tokens * rms_scale(wide_tokens) * gain_one).astype(BF16)
        projected = nn(normed, qkv_cols)
    places = jnp.arange(length)
    inverse = jnp.power(ROPE_BASE, -(jnp.arange(HEAD_SIZE // 2) * 2.0 / HEAD_SIZE))
    angles = places.astype(F32)[:, None] * inverse[None, :]
    cosine = jnp.concatenate([jnp.cos(angles)] * 4, axis=1)
    sine = jnp.concatenate([-jnp.sin(angles), jnp.sin(angles)] * 2, axis=1)
    projected, dy_pair = lax.optimization_barrier((projected, dy_pair))
    dy_pair = ring_step(dy_pair)
    upstream_chunks += dy_pair
    qkv, probs, head_out = attend(projected, cosine, sine, segments)
    branch = nn(head_out, out_weight).astype(BF16)
    branch, in_own, dy_pair = lax.optimization_barrier((branch, in_own, dy_pair))
    dy_pair = ring_step(dy_pair)
    upstream_chunks += dy_pair
    rows_of = lambda value, j: lax.dynamic_slice(value, (j * rows, 0), (rows, value.shape[1]))
    middle = inputs + RES_SCALE * sum_shards(lambda j: rows_of(branch, j))
    middle, dy_pair = lax.optimization_barrier((middle, dy_pair))
    weights = [in_own, down_own, [to_core(w) for w in in_own], [to_core(w) for w in down_own]]
    scale_two = rms_scale(middle)
    second = (middle * scale_two * gain_two).astype(BF16)

    second_chunks, pair = [second], (second, second)
    dy_hops = 3
    row_parts, gate_parts, lows, mixeds = [], [], [], []
    for step in range(half_ring + 1):
        first = max(0, 2 * step - 1)
        picks = list(range(first, len(second_chunks)))
        if step < half_ring:
            pair = ring_step(pair, step == half_ring - 1)
            second_chunks += pair
        far = step == half_ring
        slots = [(named_at, 0, rows)] * len(picks)
        if step == half_ring:
            slots = [(named_at, 0, rows), (named_at, rows // 2, rows)]
        low, mixed, row, gate, shares = run_experts(
            slots,
            info,
            [second_chunks[i] for i in picks],
            [upstream_chunks[i] for i in picks],
            [named_chunks[min(i, chips - 1)] for i in picks],
            router_wide,
            weights,
            layouts,
        )
        if step == 0:
            own_shares = shares
        if not far:
            pair, low, dy_pair = lax.optimization_barrier((pair, low, dy_pair))
            second_chunks[-2:] = pair
            last = dy_hops == half_ring - 1
            if dy_hops < half_ring and (not last or step == half_ring - 2):
                dy_hops += 1
                dy_pair = ring_step(tie(dy_pair, pair), last)
                upstream_chunks += dy_pair
        lows.append(low)
        mixeds.append(mixed)
        row_parts += row
        gate_parts += [gate] if far else [[g] for g in gate]

    def make_in(sent, at, more=()):
        return weight_grad(
            info, shards, second_chunks, 0, width, tie(lows, sent), at, 2 * ffe, more=more
        )

    got = ring_start(row_parts)
    made = make_in((), 2 * ffe)
    got, made = lax.optimization_barrier((got, made))
    in_other = [to_core(piece) for piece in made]
    for hop, step in enumerate(range(half_ring - 1, 0, -1)):
        sent = ring_add(row_parts, step, got)
        got = ring_send(sent)
        if hop == 0:
            in_parts = make_in(sent, 0, in_other)
            got, in_parts = lax.optimization_barrier((got, in_parts))
            in_got = to_holders(in_parts)
        if hop == 1:
            out_parts = run_results(
                info, tie(mixeds, sent), weights, layouts, [p.shape[0] for p in row_parts]
            )
            gate_home = sort_gates(info, tie(gate_parts, sent), rows)
            gate_home = lax.all_to_all(
                gate_home, "chip", split_axis=0, concat_axis=0, tiled=True
            )
            got, out_parts, gate_home = lax.optimization_barrier((got, out_parts, gate_home))
        if hop == 2:
            router_add = router_back(
                info, tie(gate_home, sent), own_shares, second, router_wide, experts
            )
            down_parts = weight_grad(
                info,
                shards,
                tie(mixeds, (sent, router_add)),
                0,
                2 * ffe,
                upstream_chunks,
                0,
                width,
                RES_SCALE,
                by_rows=False,
            )
            got, down_parts = lax.optimization_barrier((got, down_parts))
    grad_route, router_add = router_add
    out_got = ring_start(tie(out_parts, got))
    attn_low, middle_grads, grad_gain_two = middle_back(
        row_parts[0], *got, router_add, middle, gain_two, cotangent
    )
    attn_low, out_got = lax.optimization_barrier((attn_low, out_got))
    attn_low, in_got = lax.optimization_barrier((attn_low, in_got))

    low = lambda value: value.astype(BF16)
    sent = ring_add(out_parts, half_ring - 1, out_got)
    got = ring_send(sent)
    attn_got = [attn_low] + [to_shard(attn_low, s) for s in range(1, shards)]
    down_other = [to_core(piece) for piece in tie(down_parts[shards:], (attn_low, sent))]
    down_parts = [add_low(a, b) for a, b in zip(down_parts[:shards], down_other)]
    attn_got, got, down_parts = lax.optimization_barrier((attn_got, got, down_parts))
    if half_ring > 2:
        got = ring_send(ring_add(out_parts, half_ring - 2, got))

    down_got = to_holders(down_parts)
    projected_grads, attn_grads = attend_back(info, qkv, probs, out_weight, cosine, sine, attn_got)
    normed_low, grad_gain_one = normed_back(projected_grads, qkv_cols, all_tokens)
    got, normed_low, grad_gain_one, down_got = lax.optimization_barrier(
        (got, normed_low, grad_gain_one, down_got)
    )
    for step in range(half_ring - 3, 0, -1):
        sent = ring_add(out_parts, step, got)
        projected_grads, attn_grads, sent = lax.optimization_barrier(
            (projected_grads, attn_grads, sent)
        )
        got = ring_send(sent)

    mine_out, theirs_out = dense_grad(info, chip_places, unit, 1, head_out, attn_grads)
    theirs_out = to_core(theirs_out)
    mine_qkv, theirs_qkv = dense_grad(
        info,
        chip_places,
        unit,
        shards,
        tie(normed, mine_out),
        projected_grads,
        (grad_gain_one, grad_gain_two, grad_route),
    )
    wide = own_cols + 128
    mine_qkv, theirs_qkv, got = lax.optimization_barrier((mine_qkv, theirs_qkv, got))
    theirs_qkv = to_core(theirs_qkv)
    pairs = ((mine_qkv, theirs_qkv), (mine_out, theirs_out))
    every = mine_qkv.shape[2] + mine_out.shape[2]
    half = every // 256 * 128
    right, left = sum_blocks(pairs, [(chips - 1, 0, half, []), (chips - 1, half, every, [])])
    right, left = lax.ppermute(right, "chip", ahead), lax.ppermute(left, "chip", behind)
    right, left, normed_low = lax.optimization_barrier((right, left, normed_low))
    normed_got = exchange_shards(lambda j: rows_of(normed_low, j))
    for step in range(half_ring - 1, 0, -1):
        wanted = [
            (2 * step, 0, every, [(0, right)]),
            (2 * step - 1, 0, every, [(every - left.shape[1], left)]),
        ]
        if step == 1:
            wanted.append((0, 0, every, []))
        right, left, *own = sum_blocks(pairs, wanted)
        right = lax.ppermute(right, "chip", ahead)
        left = lax.ppermute(left, "chip", behind)
        right, left = lax.optimization_barrier((right, left))
        if step == half_ring - 2:
            right, left, normed_got = lax.optimization_barrier((right, left, normed_got))
    dense = low(own[0].astype(F32) + right.astype(F32) + left.astype(F32))
    mixed = in_order(
        [dense[:, :wide]]
        + [to_shard(dense[:, s * wide : (s + 1) * wide], s) for s in range(1, shards)]
    )
    merged = jnp.concatenate(
        [g[:, :q_cols] for g in mixed]
        + [g[:, q_cols : q_cols + k_cols] for g in mixed]
        + [g[:, q_cols + k_cols : own_cols] for g in mixed]
        + [low(sum(g[:, own_cols:].astype(F32) for g in mixed)), dense[:, shards * wide :]],
        axis=1,
    )

    total = lambda pieces: sum(p.astype(F32) for p in pieces)
    input_grads = rms_back(inputs, rms_scale(inputs), gain_one, total(normed_got))
    grad_tokens = middle_grads + input_grads
    grad_down, grad_in = total(down_got), total(in_got)

    block_out = low(middle + RES_SCALE * ring_end(out_parts, got))
    beside = {2: block_out, half_ring - 1: grad_tokens, half_ring: (grad_down, grad_in)}
    all_cols = query_width + 2 * pair_width
    widths = [all_cols, 128, width]
    cores = jnp.split(both_cores.astype(jnp.int32), 2)
    count = 2 * half_ring - 3
    places = jnp.concatenate([c[:count] for c in cores] + [c[count:] for c in cores])
    spread_out, late = plane_gather(
        merged, beside, lambda early: spread(places, 0, early, widths, experts)
    )
    block_out, grad_tokens = beside[2], beside[half_ring - 1]
    grad_down, grad_in = beside[half_ring]
    spread_out = spread(places, 2 * count, late, widths, experts, spread_out)
    grad_qkv, small, grad_out = [out.reshape(-1, out.shape[-1]) for out in spread_out]
    return (
        block_out,
        grad_tokens,
        small[:, experts],
        small[:, experts + 1],
        grad_qkv,
        grad_out,
        small[:, :experts],
        grad_in[None],
        grad_down[None],
    )


def solution(mesh):
    chips = mesh.shape["expert"] // 2
    grid = Mesh(
        mesh.devices.reshape(chips, 2, mesh.shape["shard"]), ("chip", "core", "shard")
    )
    expert = ("chip", "core")
    every = ("chip", "core", "shard")
    in_specs = (
        P(every, None),
        P(every),
        P(every, None),
        P("shard"),
        P("shard"),
        P("shard", None),
        P("shard", None),
        P("shard", None),
        P(expert, "shard", None),
        P(expert, None, "shard"),
        P(every, None),
    )
    out_specs = (
        P(every, None),
        P(every, None),
        P("shard"),
        P("shard"),
        P("shard", None),
        P("shard", None),
        P("shard", None),
        P(expert, "shard", None),
        P(expert, None, "shard"),
    )
    return jax.shard_map(body, mesh=grid, in_specs=in_specs, out_specs=out_specs, check_vma=False)
```

```python
from functools import partial

import jax
import jax.numpy as jnp
import numpy as np
from jax import lax
from jax.experimental import pallas as pl
from jax.experimental.pallas import tpu as pltpu
from jax.sharding import Mesh, PartitionSpec as P

QUERY_HEADS = 24
KEY_VALUE_HEADS = 8
HEAD_SIZE = 64
GROUP = QUERY_HEADS // KEY_VALUE_HEADS
RES_SCALE = 0.22
ATT_SCALE = 0.015625
EPSILON = 1e-06
ROPE_BASE = 10000.0
MASKED = -1000000000.0
F32 = jnp.float32
BF16 = jnp.bfloat16
MIB = 1024 * 1024
BIG_VMEM = 60 * MIB


def mm(a, b, dims):
    return lax.dot_general(a, b, (dims, ((), ())), preferred_element_type=F32)


def nn(a, b):
    return mm(a, b, ((1,), (0,)))


def nt(a, b):
    return mm(a, b, ((1,), (1,)))


def tn(a, b):
    return mm(a, b, ((0,), (0,)))


def tie(values, after):
    return lax.optimization_barrier((values, after))[0]


def ring_chips(chips):
    depth = 4 if chips % 4 == 0 else 2
    width = max(1, chips // depth)
    walk = [(z, 0) for z in range(depth)]
    for z in reversed(range(depth)):
        line = range(1, width) if (depth - 1 - z) % 2 == 0 else reversed(range(1, width))
        walk += [(z, x) for x in line]
    return [z * width + x for z, x in walk]


def add_low(a, b):
    return (a.astype(F32) + b.astype(F32)).astype(BF16)


def rms_scale(rows):
    return lax.rsqrt(jnp.mean(rows * rows, axis=-1, keepdims=True) + EPSILON)


def rms_back(rows, scale, gain, grad):
    weighted = grad * gain
    dot = jnp.mean(weighted * rows, axis=-1, keepdims=True)
    return scale * weighted - rows * (scale * scale * scale * dot)


def turn(value, cosine, sine, first):
    swapped = jnp.where(first, pltpu.roll(value, 96, 1), pltpu.roll(value, 32, 1))
    return value * cosine + swapped * sine


def attend_kernel(
    q_ref, k_ref, v_ref, cos_ref, sin_ref, seg_col, seg_row, qkv_out, p_out, head_out, bias, turned
):
    pair, pairs = pl.program_id(0), pl.num_programs(0)
    length = q_ref.shape[0]
    block = min(256, length)
    q_cols = pairs * 2 * GROUP * HEAD_SIZE
    wide = 2 * GROUP * HEAD_SIZE
    first = lax.broadcasted_iota(jnp.int32, (length, 128), 1) % HEAD_SIZE < HEAD_SIZE // 2

    @pl.when(pair == 0)
    def _():
        keys = lax.broadcasted_iota(jnp.int32, (length, length), 0)
        rows = lax.broadcasted_iota(jnp.int32, (length, length), 1)
        allowed = (seg_col[...] == seg_row[...]) & (keys <= rows)
        bias[...] = jnp.where(allowed, 0.0, MASKED)

    cosine, sine = cos_ref[...], sin_ref[...]
    for c in range(wide // 128):
        at = pl.ds(c * 128, 128)
        turned[:, at] = turn(q_ref[:, at], cosine, sine, first).astype(BF16)
    key = turn(k_ref[...], cosine, sine, first).astype(BF16)
    value = v_ref[...].astype(BF16)
    qkv_out[:, pl.ds(pl.multiple_of(pair * wide, 128), wide)] = turned[...]
    qkv_out[:, pl.ds(pl.multiple_of(q_cols + pair * 128, 128), 128)] = key
    qkv_out[:, pl.ds(pl.multiple_of(q_cols + (pairs + pair) * 128, 128), 128)] = value
    value_t = jnp.transpose(v_ref[...]).astype(BF16)
    for r in range(length // block):
        rows = pl.ds(r * block, block)
        end = (r + 1) * block
        mask = bias[0:end, rows]
        mask = jnp.concatenate([mask] * GROUP, axis=1)
        both = []
        for g in range(2):
            query = jnp.concatenate(
                [
                    turned[rows, pl.ds((g * GROUP + j) * HEAD_SIZE, HEAD_SIZE)]
                    for j in range(GROUP)
                ],
                axis=0,
            )
            own_key = key[:end, g * HEAD_SIZE : (g + 1) * HEAD_SIZE]
            scores = nt(own_key, query) * ATT_SCALE + mask
            grown = jnp.exp(scores - jnp.max(scores, axis=0, keepdims=True))
            probs = grown * (1.0 / jnp.sum(grown, axis=0, keepdims=True))
            probs = probs.astype(BF16)
            p_out[g, 0:end, pl.ds(r * GROUP * block, GROUP * block)] = probs
            both.append(nn(value_t[g * HEAD_SIZE : (g + 1) * HEAD_SIZE, :end], probs))
        laid = jnp.transpose(jnp.concatenate(both, axis=0))
        for g in range(2):
            for j in range(GROUP):
                head_out[rows, pl.ds((g * GROUP + j) * HEAD_SIZE, HEAD_SIZE)] = laid[
                    j * block : (j + 1) * block, g * HEAD_SIZE : (g + 1) * HEAD_SIZE
                ].astype(BF16)


def attend(projected, cosine, sine, segments):
    length, cols = projected.shape
    q_cols = cols * 3 // 5
    pairs = q_cols // (2 * GROUP * HEAD_SIZE)
    wide = 2 * GROUP * HEAD_SIZE
    key_at = q_cols // 128
    return pl.pallas_call(
        attend_kernel,
        grid=(pairs,),
        in_specs=[
            pl.BlockSpec((length, wide), lambda i: (0, i)),
            pl.BlockSpec((length, 128), lambda i: (0, key_at + i)),
            pl.BlockSpec((length, 128), lambda i: (0, key_at + pairs + i)),
            pl.BlockSpec((length, 128), lambda i: (0, 0)),
            pl.BlockSpec((length, 128), lambda i: (0, 0)),
            pl.BlockSpec((length, 1), lambda i: (0, 0)),
            pl.BlockSpec((1, length), lambda i: (0, 0)),
        ],
        out_specs=[
            pl.BlockSpec((length, cols), lambda i: (0, 0)),
            pl.BlockSpec((2, length, GROUP * length), lambda i: (i, 0, 0)),
            pl.BlockSpec((length, wide), lambda i: (0, i)),
        ],
        out_shape=[
            jax.ShapeDtypeStruct((length, cols), BF16),
            jax.ShapeDtypeStruct((2 * pairs, length, GROUP * length), BF16),
            jax.ShapeDtypeStruct((length, q_cols), BF16),
        ],
        scratch_shapes=[pltpu.VMEM((length, length), F32), pltpu.VMEM((length, wide), BF16)],
        compiler_params=pltpu.CompilerParams(vmem_limit_bytes=40 * MIB),
        cost_estimate=pl.CostEstimate(
            flops=8 * pairs * GROUP * length * length * 256,
            bytes_accessed=4 * pairs * GROUP * length * length,
            transcendentals=2 * pairs * GROUP * length * length,
        ),
    )(projected, projected, projected, cosine, sine, segments[:, None], segments[None, :])


def attend_back_kernel(shards, info, q_ref, k_ref, v_ref, p_ref, w_ref, cos_ref, sin_ref, *refs):
    upstream, refs = refs[:shards], refs[shards:]
    grad_out, all_out, all_s, d_s, dq_s, dk_s, dv_s, sems = refs
    pair, pairs = pl.program_id(0), pl.num_programs(0)
    length = q_ref.shape[0]
    rows_of = length // shards

    def kept():
        return pltpu.make_async_copy(all_s, all_out, sems.at[shards])

    @pl.when(pair == 0)
    def _():
        made = [
            pltpu.make_async_copy(
                upstream[s],
                all_s.at[pl.ds(pl.multiple_of(info[2 + s] * rows_of, 16), rows_of)],
                sems.at[s],
            )
            for s in range(shards)
        ]
        for one in made:
            one.start()
        finish(made)
        kept().start()
        grads = nt(all_s[...], w_ref[...]).astype(BF16)
        for i in range(d_s.shape[0]):
            d_s[i] = grads[:, i * d_s.shape[2] : (i + 1) * d_s.shape[2]]

    @pl.when(pair == pairs - 1)
    def _():
        kept().wait()

    d_ref = d_s.at[pair]
    block = min(256, length)
    q_cols = pairs * 2 * GROUP * HEAD_SIZE
    wide = 2 * GROUP * HEAD_SIZE
    first = lax.broadcasted_iota(jnp.int32, (length, 128), 1) % HEAD_SIZE < HEAD_SIZE // 2
    key_t = jnp.transpose(k_ref[...].astype(F32)).astype(BF16)
    for r in reversed(range(length // block)):
        rows = pl.ds(r * block, block)
        end = (r + 1) * block
        both = []
        for g in range(2):
            own = pl.ds(g * HEAD_SIZE, HEAD_SIZE)
            heads = [
                pl.ds((g * GROUP + j) * HEAD_SIZE, HEAD_SIZE) for j in range(GROUP)
            ]
            query = jnp.concatenate([q_ref[rows, h] for h in heads], axis=0)
            grad = jnp.concatenate([d_ref[rows, h] for h in heads], axis=0)
            probs = p_ref[g, 0:end, pl.ds(r * GROUP * block, GROUP * block)]
            prob_grad = nt(v_ref[0:end, own], grad)
            wide_probs = probs.astype(F32)
            dots = jnp.sum(wide_probs * prob_grad, axis=0, keepdims=True)
            score_grad = (wide_probs * (prob_grad - dots)).astype(BF16)
            key_grad = nn(score_grad, query)
            value_grad = nn(probs, grad)
            if end == length:
                dk_s[0:end, own] = key_grad
                dv_s[0:end, own] = value_grad
            else:
                dk_s[0:end, own] += key_grad
                dv_s[0:end, own] += value_grad
            both.append(nn(key_t[g * HEAD_SIZE : (g + 1) * HEAD_SIZE, :end], score_grad))
        laid = jnp.transpose(jnp.concatenate(both, axis=0))
        for g in range(2):
            for j in range(GROUP):
                dq_s[rows, pl.ds((g * GROUP + j) * HEAD_SIZE, HEAD_SIZE)] = laid[
                    j * block : (j + 1) * block, g * HEAD_SIZE : (g + 1) * HEAD_SIZE
                ]
    cosine, sine = cos_ref[...] * ATT_SCALE, sin_ref[...] * -ATT_SCALE
    for c in range(wide // 128):
        at = pl.ds(c * 128, 128)
        grad_out[:, pl.ds(pl.multiple_of(pair * wide + c * 128, 128), 128)] = turn(
            dq_s[:, at], cosine, sine, first
        ).astype(BF16)
    grad_out[:, pl.ds(pl.multiple_of(q_cols + pair * 128, 128), 128)] = turn(
        dk_s[...], cosine, sine, first
    ).astype(BF16)
    grad_out[:, pl.ds(pl.multiple_of(q_cols + (pairs + pair) * 128, 128), 128)] = dv_s[
        ...
    ].astype(BF16)


def attend_back(info, qkv, probs, out_weight, cosine, sine, upstream):
    length, cols = qkv.shape
    q_cols = cols * 3 // 5
    pairs = q_cols // (2 * GROUP * HEAD_SIZE)
    wide = 2 * GROUP * HEAD_SIZE
    width = out_weight.shape[1]
    key_at = q_cols // 128
    shards = len(upstream)
    anywhere = pl.BlockSpec(memory_space=pltpu.HBM)
    return pl.pallas_call(
        partial(attend_back_kernel, shards),
        grid=(pairs,),
        in_specs=[
            pl.BlockSpec(memory_space=pltpu.SMEM),
            pl.BlockSpec((length, wide), lambda i: (0, i)),
            pl.BlockSpec((length, 128), lambda i: (0, key_at + i)),
            pl.BlockSpec((length, 128), lambda i: (0, key_at + pairs + i)),
            pl.BlockSpec((2, length, GROUP * length), lambda i: (i, 0, 0)),
            pl.BlockSpec((q_cols, width), lambda i: (0, 0)),
            pl.BlockSpec((length, 128), lambda i: (0, 0)),
            pl.BlockSpec((length, 128), lambda i: (0, 0)),
        ]
        + [anywhere] * shards,
        out_specs=[pl.BlockSpec((length, cols), lambda i: (0, 0)), anywhere],
        out_shape=[
            jax.ShapeDtypeStruct((length, cols), BF16),
            jax.ShapeDtypeStruct((length, width), BF16),
        ],
        scratch_shapes=[
            pltpu.VMEM((length, width), BF16),
            pltpu.VMEM((pairs, length, wide), BF16),
            pltpu.VMEM((length, wide), F32),
            pltpu.VMEM((length, 128), F32),
            pltpu.VMEM((length, 128), F32),
            pltpu.SemaphoreType.DMA((shards + 1,)),
        ],
        compiler_params=pltpu.CompilerParams(vmem_limit_bytes=40 * MIB),
        cost_estimate=pl.CostEstimate(
            flops=16 * pairs * GROUP * length * length * 256 + 2 * length * q_cols * width,
            bytes_accessed=4 * pairs * GROUP * length * length,
            transcendentals=0,
        ),
    )(info, qkv, qkv, qkv, probs, out_weight, cosine, sine, *upstream)


class Copies:
    def __init__(self, sems):
        self.sems, self.used = sems, 0

    def make(self, src, dst):
        made = pltpu.make_async_copy(src, dst, self.sems.at[self.used])
        self.used += 1
        return made

    def start(self, src, dst):
        made = self.make(src, dst)
        made.start()
        return made


def finish(copies):
    for made in copies:
        made.wait()


def load_weights(copies, info, refs, layout, scratch, base, cols):
    made = []
    for ref, (s, first, number, many) in zip(refs, layout):
        at = pl.ds(pl.multiple_of(info[2 + s] * many + first, 128 if cols else 16), number)
        if cols:
            made.append(copies.start(ref, scratch.at[pl.ds(base, ref.shape[0]), at]))
        else:
            made.append(copies.start(ref, scratch.at[at, pl.ds(base, ref.shape[1])]))
    return made


def expert_kernel(slots, in_layout, down_layout, info, *refs):
    parts = len(slots)
    refs = list(refs)
    take = lambda n: [refs.pop(0) for _ in range(n)]
    x_refs, d_refs = take(parts), take(parts)
    route_refs, (router_ref,) = take(parts), take(1)
    in_refs = [take(len(in_layout)), take(len(in_layout))]
    down_refs = [take(len(down_layout)), take(len(down_layout))]
    low_out, mixed_out = take(2)
    row_outs, gate_outs = take(parts), take(parts)
    (share_out,) = take(1)
    x_s, d_s, in_s, down_s, router_s, route_s, low_s, mixed_s, row_s, gate_s, pulled_s, sems = refs
    rows, width = x_refs[0].shape
    total = parts * rows
    ffe = in_s.shape[1] // 4
    tile = min(256, ffe)
    copies = Copies(sems)
    place = [pl.ds(p * rows, rows) for p in range(parts)]
    got_x = [copies.start(x_refs[p], x_s.at[place[p]]) for p in range(parts)]
    got_x.append(copies.start(router_ref, router_s))
    for p in range(parts):
        at, _, seen = slots[p]
        got_x.append(copies.start(route_refs[p].at[pl.ds(at, 16), pl.ds(0, seen)], route_s.at[p]))
    got_in, got_down = [], []
    for e in range(2):
        got_in.append(load_weights(copies, info, in_refs[e], in_layout, in_s, 2 * e * ffe, False))
        if e == 0:
            got_d = [copies.start(d_refs[p], d_s.at[place[p]]) for p in range(parts)]
        got_down.append(
            load_weights(copies, info, down_refs[e], down_layout, down_s, e * ffe, True)
        )
    lanes = lax.broadcasted_iota(jnp.int32, (rows, 128), 1)
    finish(got_x)
    bias = []
    for p in range(parts):
        first = slots[p][1]
        named = jnp.transpose(route_s[p].astype(F32))[first : first + rows].astype(jnp.int32)
        hit = named[:, 0:1] == lanes
        for k in range(1, 8):
            hit = hit | (named[:, k : k + 1] == lanes)
        bias.append(jnp.where(hit, 0.0, -1e30))
    logits = nn(x_s[...], router_s[...]) + jnp.concatenate(bias, axis=0)
    grown = jnp.exp(logits - jnp.max(logits, axis=-1, keepdims=True))
    shares = grown / jnp.sum(grown, axis=-1, keepdims=True)
    share_out[...] = shares
    lanes = lax.broadcasted_iota(jnp.int32, (total, 128), 1)
    gate_cols = jnp.zeros((total, 128), F32)
    sent = []
    for e in range(2):
        share = RES_SCALE * jnp.sum(
            jnp.where(lanes == info[e], shares, 0.0), axis=1, keepdims=True
        )
        gate_grad = jnp.zeros((total, 1), F32)
        finish(got_in[e])
        gate_s[...] = nn(x_s[...], in_s[:, pl.ds(2 * e * ffe, 2 * ffe)])
        finish((got_d if e == 0 else []) + got_down[e])
        pulled_s[...] = nt(d_s[...], down_s[pl.ds(e * ffe, ffe), :])
        for j in range(ffe // tile):
            gate_at = 2 * e * ffe + j * tile
            gate = gate_s[:, pl.ds(j * tile, tile)]
            up = gate_s[:, pl.ds(ffe + j * tile, tile)]
            pulled = pulled_s[:, pl.ds(j * tile, tile)]
            sigmoid = 0.5 * jnp.tanh(0.5 * gate) + 0.5
            swish = gate * sigmoid
            hidden = swish * up
            gate_grad = gate_grad + jnp.sum(hidden * pulled, axis=1, keepdims=True)
            hidden_grad = share * pulled
            low_s[:, pl.ds(gate_at, tile)] = (
                hidden_grad * up * (sigmoid * (1.0 + gate - swish))
            ).astype(BF16)
            low_s[:, pl.ds(gate_at + ffe, tile)] = (hidden_grad * swish).astype(BF16)
            mixed_s[:, pl.ds(e * ffe + j * tile, tile)] = (
                share * (1.0 / RES_SCALE) * hidden
            ).astype(BF16)
        gate_cols = gate_cols + jnp.where(lanes == e, RES_SCALE * gate_grad, 0.0)
    sent.append(copies.start(low_s, low_out))
    sent.append(copies.start(mixed_s, mixed_out))
    step = 768
    for n in range(width // step):
        at = pl.ds(n * step, step)
        row_s[:, at] = nt(low_s[...], in_s[at, :]).astype(BF16)
        for p in range(parts):
            sent.append(copies.start(row_s.at[place[p], at], row_outs[p].at[:, at]))
    for p in range(parts):
        gate_outs[p][...] = jnp.transpose(gate_cols[p * rows : (p + 1) * rows])[:8]
    finish(sent)


def run_experts(slots, info, x_list, d_list, routes, router, weights, layouts):
    parts = len(slots)
    rows, width = x_list[0].shape
    ffe = weights[0][0].shape[1] // 2
    total = parts * rows
    out_shape = [
        jax.ShapeDtypeStruct((total, 4 * ffe), BF16),
        jax.ShapeDtypeStruct((total, 2 * ffe), BF16),
    ]
    out_shape += [jax.ShapeDtypeStruct((rows, width), BF16)] * parts
    out_shape += [jax.ShapeDtypeStruct((8, rows), F32)] * parts
    out_shape += [jax.ShapeDtypeStruct((total, 128), F32)]
    operands = [*x_list, *d_list, *routes, router]
    for group in (weights[0], weights[2], weights[1], weights[3]):
        operands += list(group)
    here = pl.BlockSpec(memory_space=pltpu.VMEM)
    anywhere = pl.BlockSpec(memory_space=pltpu.HBM)
    copies = 3 * parts + 1 + sum(len(w) for w in weights) + 2 + parts * (width // 256)
    in_specs = [anywhere] * len(operands)
    outs = pl.pallas_call(
        partial(expert_kernel, slots, *layouts),
        in_specs=[pl.BlockSpec(memory_space=pltpu.SMEM)] + in_specs,
        out_specs=[anywhere] * (2 + parts) + [here] * (parts + 1),
        out_shape=out_shape,
        scratch_shapes=[
            pltpu.VMEM((total, width), BF16),
            pltpu.VMEM((total, width), BF16),
            pltpu.VMEM((width, 4 * ffe), BF16),
            pltpu.VMEM((2 * ffe, width), BF16),
            pltpu.VMEM((width, 128), BF16),
            pltpu.VMEM((parts, 16, slots[0][2]), BF16),
            pltpu.VMEM((total, 4 * ffe), BF16),
            pltpu.VMEM((total, 2 * ffe), BF16),
            pltpu.VMEM((total, width), BF16),
            pltpu.VMEM((total, 2 * ffe), F32),
            pltpu.VMEM((total, ffe), F32),
            pltpu.SemaphoreType.DMA((copies,)),
        ],
        compiler_params=pltpu.CompilerParams(vmem_limit_bytes=BIG_VMEM),
        cost_estimate=pl.CostEstimate(
            flops=20 * total * width * ffe,
            bytes_accessed=12 * ffe * width + 12 * total * width,
            transcendentals=total * ffe * 2,
        ),
    )(info, *operands)
    return outs[0], outs[1], outs[2 : 2 + parts], outs[2 + parts : 2 + 2 * parts], outs[-1]


def result_kernel(heights, out_heights, down_layout, info, *refs):
    refs = list(refs)
    take = lambda n: [refs.pop(0) for _ in range(n)]
    mixed_refs = take(len(heights))
    down_refs = [take(len(down_layout)), take(len(down_layout))]
    outs = take(len(out_heights))
    mixed_s, down_s, out_s, sems = refs
    ffe = down_s.shape[0] // 2
    copies = Copies(sems)
    got = [
        made
        for e in range(2)
        for made in load_weights(copies, info, down_refs[e], down_layout, down_s, e * ffe, True)
    ]
    start, waits = 0, []
    for ref, height in zip(mixed_refs, heights):
        waits.append(copies.start(ref, mixed_s.at[pl.ds(start, height)]))
        start += height
    finish(got)
    sent, start, place, at = [], 0, 0, 0
    for i, height in enumerate(heights):
        finish([waits[i]])
        rows = pl.ds(start, height)
        for n in range(down_s.shape[1] // 512):
            cols = pl.ds(n * 512, 512)
            out_s[rows, cols] = nn(mixed_s[rows, :], down_s[:, cols]).astype(BF16)
        start += height
        while place < len(outs) and at + out_heights[place] <= start:
            sent.append(copies.start(out_s.at[pl.ds(at, out_heights[place])], outs[place]))
            at += out_heights[place]
            place += 1
    finish(sent)


def run_results(info, mixeds, weights, layouts, out_heights):
    heights = [m.shape[0] for m in mixeds]
    total, cols = sum(heights), mixeds[0].shape[1]
    width = sum(number for _, _, number, _ in layouts[1])
    anywhere = pl.BlockSpec(memory_space=pltpu.HBM)
    operands = [*mixeds, *weights[1], *weights[3]]
    return pl.pallas_call(
        partial(result_kernel, heights, out_heights, layouts[1]),
        in_specs=[pl.BlockSpec(memory_space=pltpu.SMEM)] + [anywhere] * len(operands),
        out_specs=[anywhere] * len(out_heights),
        out_shape=[jax.ShapeDtypeStruct((h, width), BF16) for h in out_heights],
        scratch_shapes=[
            pltpu.VMEM((total, cols), BF16),
            pltpu.VMEM((cols, width), BF16),
            pltpu.VMEM((total, width), BF16),
            pltpu.SemaphoreType.DMA((len(operands) + len(out_heights),)),
        ],
        compiler_params=pltpu.CompilerParams(vmem_limit_bytes=BIG_VMEM),
        cost_estimate=pl.CostEstimate(
            flops=2 * total * cols * width,
            bytes_accessed=2 * (total * (cols + width) + cols * width),
            transcendentals=0,
        ),
    )(info, *operands)


def sort_gates_kernel(counts, info, *refs):
    out = refs[-1]
    for i, many in enumerate(counts):
        pieces = refs[sum(counts[:i]) : sum(counts[: i + 1])]
        at = 0
        for ref in pieces:
            cols = ref.shape[1]
            out[info[info.shape[0] - len(counts) + i], :, at : at + cols] = ref[0:2, :]
            at += cols


def sort_gates(info, parts, rows):
    flat = [ref for part in parts for ref in part]
    return pl.pallas_call(
        partial(sort_gates_kernel, [len(p) for p in parts]),
        in_specs=[pl.BlockSpec(memory_space=pltpu.SMEM)]
        + [pl.BlockSpec(memory_space=pltpu.VMEM)] * len(flat),
        out_specs=pl.BlockSpec(memory_space=pltpu.VMEM),
        out_shape=jax.ShapeDtypeStruct((len(parts), 2, rows), F32),
    )(info, *flat)


def spread_kernel(widths, kept, first, places, *refs):
    count = len(refs) - kept - 2 * len(widths) - 1
    blocks, refs = refs[:count], refs[count + kept :]
    outs, scratch, sems = refs[: len(widths)], refs[len(widths) : -1], refs[-1]
    copies, sent = Copies(sems), []
    for i, ref in enumerate(blocks):
        at = 0
        for out, buffer, wide in zip(outs, scratch, widths):
            buffer[i] = ref[:, at : at + wide].astype(F32)
            sent.append(copies.start(buffer.at[i], out.at[places[first + i]]))
            at += wide
    finish(sent)


def spread(places, first, blocks, widths, total, kept=()):
    count, height = len(blocks), blocks[0].shape[0]
    anywhere = pl.BlockSpec(memory_space=pltpu.HBM)
    return pl.pallas_call(
        partial(spread_kernel, widths, len(kept), first),
        in_specs=[pl.BlockSpec(memory_space=pltpu.SMEM)]
        + [pl.BlockSpec(memory_space=pltpu.VMEM)] * count
        + [anywhere] * len(kept),
        out_specs=[anywhere] * len(widths),
        out_shape=[jax.ShapeDtypeStruct((total, height, wide), F32) for wide in widths],
        scratch_shapes=[pltpu.VMEM((count, height, wide), F32) for wide in widths]
        + [pltpu.SemaphoreType.DMA((count * len(widths),))],
        input_output_aliases={1 + count + i: i for i in range(len(kept))},
        compiler_params=pltpu.CompilerParams(vmem_limit_bytes=40 * MIB),
    )(places, *blocks, *kept)


def weight_grad_kernel(heights, a_at, b_at, scale, by_rows, added, info, *refs):
    refs = list(refs)
    take = lambda n: [refs.pop(0) for _ in range(n)]
    a_refs, b_refs, more = take(len(heights[0])), take(len(heights[1])), take(added)
    a_s, b_s, sems = refs[-3:]
    outs = refs[:-3]
    step, steps = pl.program_id(0), pl.num_programs(0)
    tile = outs[0].shape[0 if by_rows else 1]

    def loads(parts, heights_of, scratch, at, tiled):
        made, start = [], 0
        for ref, height in zip(parts, heights_of):
            for t in range(steps_static if tiled else 1):
                wide = tile if tiled else scratch.shape[1]
                made.append(
                    (
                        t,
                        ref.at[:, pl.ds(at + t * wide, wide)],
                        scratch.at[pl.ds(start, height), pl.ds(t * wide, wide)],
                    )
                )
            start += height
        return made

    steps_static = (a_s if by_rows else b_s).shape[1] // tile
    first = loads(a_refs, heights[0], a_s, a_at, by_rows)
    second = loads(b_refs, heights[1], b_s, b_at, not by_rows)
    whole, tiled = (second, first) if by_rows else (first, second)
    tiled.sort(key=lambda entry: entry[0])
    copies = Copies(sems)
    made_whole = [copies.make(src, dst) for _, src, dst in whole]
    made_tiled = [(t, copies.make(src, dst)) for t, src, dst in tiled]

    @pl.when(step == 0)
    def _():
        for made in made_whole:
            made.start()
        for _, made in made_tiled:
            made.start()
        finish(made_whole)

    for t in range(steps_static):

        @pl.when(step == t)
        def _(t=t):
            finish([made for at, made in made_tiled if at == t])

    at = pl.ds(pl.multiple_of(step * tile, 128), tile)
    if by_rows:
        grad = tn(a_s[:, at], b_s[...])
    else:
        grad = tn(a_s[...], b_s[:, at])
    grad = scale * grad
    shards = len(outs) // (1 if by_rows else 2)
    place = lax.rem(step // (steps // shards) - info[2] + shards, shards)
    count = outs[0].shape[0]
    for i, out in enumerate(outs):
        value = grad if by_rows else grad[i // shards * count : (i // shards + 1) * count]

        @pl.when(place == i % shards)
        def _(i=i, out=out, value=value):
            if added:
                out[...] = (value + more[i][...].astype(F32)).astype(BF16)
            else:
                out[...] = value.astype(BF16)


def weight_grad(
    info, shards, a_list, a_at, a_cols, b_list, b_at, b_cols, scale=1.0, by_rows=True, more=()
):
    heights = ([a.shape[0] for a in a_list], [b.shape[0] for b in b_list])
    total = sum(heights[0])
    each = (a_cols if by_rows else b_cols) // shards
    tile = 256 if each % 256 == 0 else each
    tiles = each // tile
    shape = (each, b_cols) if by_rows else (a_cols // 2, each)
    many = shards if by_rows else 2 * shards
    anywhere = pl.BlockSpec(memory_space=pltpu.HBM)

    def tile_of(r):
        def index(i, info):
            at = jnp.clip(i - lax.rem(info[2] + r, shards) * tiles, 0, tiles - 1)
            return (at, 0) if by_rows else (0, at)

        block = (tile, b_cols) if by_rows else (a_cols // 2, tile)
        return pl.BlockSpec(block, index)

    parts_a = len(a_list) * (shards * tiles if by_rows else 1)
    parts_b = len(b_list) * (1 if by_rows else shards * tiles)
    return pl.pallas_call(
        partial(weight_grad_kernel, heights, a_at, b_at, scale, by_rows, len(more)),
        grid_spec=pltpu.PrefetchScalarGridSpec(
            num_scalar_prefetch=1,
            grid=(shards * tiles,),
            in_specs=[anywhere] * (len(a_list) + len(b_list))
            + [tile_of(r) for r in range(len(more))],
            out_specs=[tile_of(i % shards) for i in range(many)],
            scratch_shapes=[
                pltpu.VMEM((total, a_cols), BF16),
                pltpu.VMEM((total, b_cols), BF16),
                pltpu.SemaphoreType.DMA((parts_a + parts_b,)),
            ],
        ),
        out_shape=[jax.ShapeDtypeStruct(shape, BF16)] * many,
        compiler_params=pltpu.CompilerParams(vmem_limit_bytes=BIG_VMEM),
        cost_estimate=pl.CostEstimate(
            flops=2 * total * a_cols * b_cols,
            bytes_accessed=2 * (total * (a_cols + b_cols) + a_cols * b_cols),
            transcendentals=0,
        ),
    )(info, *a_list, *b_list, *more)


def dense_grad_kernel(unit, shards, small_too, info, places, *refs):
    sources, refs = refs[:2], refs[2:]
    extras, refs = (refs[:3], refs[3:]) if small_too else ((), refs)
    mine, theirs, a_s, b_s, scratch, sems = refs[:6]
    copies, sent = Copies(sems), []
    got = [copies.start(ref, to) for ref, to in zip(sources, (a_s, b_s))]
    flat = len(scratch.shape) == 2
    cols = b_s.shape[1]
    count = 2 * mine.shape[0]
    wide = mine.shape[2] // shards
    tile = 256 if flat else 384
    core = info[0] % 2
    if small_too:
        small, width = refs[6], a_s.shape[1]
        turned = jnp.transpose(
            jnp.concatenate([extras[0][...], extras[1][...], jnp.zeros((6, width), F32)], axis=0)
        )
        lanes = lax.broadcasted_iota(jnp.int32, (width, 128), 1)
        small[...] = jnp.where(
            lanes == count,
            turned[:, 0:1],
            jnp.where(lanes == count + 1, turned[:, 1:2], extras[2][...]),
        ).astype(BF16)
        if flat:
            scratch[:, cols:] = small[...]
    finish(got)
    ready = 0
    for t in range(a_s.shape[1] // tile):
        grad = tn(a_s[:, t * tile : (t + 1) * tile], b_s[...]).astype(BF16)
        if flat:
            scratch[t * tile : (t + 1) * tile, 0:cols] = grad
        while (ready + 1) * unit <= (t + 1) * tile:
            if flat:
                block = scratch.at[pl.ds(ready * unit, unit), :]
            else:
                first = ready * unit - t * tile
                scratch[ready, :, 0:cols] = grad[first : first + unit]
                if small_too:
                    scratch[ready, :, cols:] = small[ready * unit : (ready + 1) * unit, :]
                block = scratch.at[ready]
            name, turn = ready % count, ready // count
            place = places[name // 2]
            if shards > 1:
                turn = lax.rem(turn - info[2] + shards, shards)
            at = pl.ds(pl.multiple_of(turn * wide, 128), wide)
            to_mine = copies.make(block, mine.at[place, :, at])
            to_theirs = pltpu.make_async_copy(
                block, theirs.at[place, :, at], sems.at[copies.used - 1]
            )

            @pl.when(core == name % 2)
            def _(one=to_mine):
                one.start()

            @pl.when(core != name % 2)
            def _(one=to_theirs):
                one.start()

            sent.append(to_mine)
            ready += 1
    finish(sent)


def dense_grad(info, places, unit, shards, a, b, extras=()):
    length, rows = a.shape
    cols = b.shape[1]
    chips = places.shape[0]
    wide = cols + (128 if extras else 0)
    here = pl.BlockSpec(memory_space=pltpu.VMEM)
    anywhere = pl.BlockSpec(memory_space=pltpu.HBM)
    small = pl.BlockSpec(memory_space=pltpu.SMEM)
    flat = unit % 16 == 0
    many = rows // unit
    scratch = [
        pltpu.VMEM(a.shape, BF16),
        pltpu.VMEM(b.shape, BF16),
        pltpu.VMEM((rows, wide) if flat else (many, unit, wide), BF16),
        pltpu.SemaphoreType.DMA((2 + many,)),
    ]
    if extras:
        scratch.append(pltpu.VMEM((rows, 128), BF16))
    return pl.pallas_call(
        partial(dense_grad_kernel, unit, shards, bool(extras)),
        in_specs=[small] * 2 + [anywhere] * 2 + [here] * len(extras),
        out_specs=[anywhere] * 2,
        out_shape=[jax.ShapeDtypeStruct((chips, unit, shards * wide), BF16)] * 2,
        scratch_shapes=scratch,
        compiler_params=pltpu.CompilerParams(vmem_limit_bytes=BIG_VMEM),
        cost_estimate=pl.CostEstimate(
            flops=6 * length * rows * cols,
            bytes_accessed=2 * length * (rows + cols),
            transcendentals=0,
        ),
    )(info, places, a, b, *extras)


def normed_back_kernel(grads, weight, tokens, low_out, gain_out):
    grad = nt(grads[...], weight[...])
    rows = tokens[...].astype(F32)
    unit = rows * lax.rsqrt(jnp.mean(rows * rows, axis=-1, keepdims=True) + EPSILON)
    gain_out[...] = jnp.sum(grad * unit, axis=0, keepdims=True)
    low_out[...] = grad.astype(BF16)


def normed_back(grads, weight, tokens):
    length, width = tokens.shape
    here = pl.BlockSpec(memory_space=pltpu.VMEM)
    return pl.pallas_call(
        normed_back_kernel,
        in_specs=[here] * 3,
        out_specs=[here] * 2,
        out_shape=[
            jax.ShapeDtypeStruct((length, width), BF16),
            jax.ShapeDtypeStruct((1, width), F32),
        ],
        compiler_params=pltpu.CompilerParams(vmem_limit_bytes=40 * MIB),
        cost_estimate=pl.CostEstimate(
            flops=2 * length * width * grads.shape[1],
            bytes_accessed=2 * (grads.size + weight.size + 2 * tokens.size),
            transcendentals=0,
        ),
    )(grads, weight, tokens)


def project_kernel(shards, q_cols, k_cols, unit, info, places, own_ref, gain_ref, *refs):
    token_refs, refs = refs[:shards], refs[shards:]
    blocks, (normed_out, cols_out, out, tokens_out, w_s, t_s, sems) = refs[:-7], refs[-7:]
    count = own_ref.shape[0]
    rows = token_refs[0].shape[0]
    copies = Copies(sems)
    shard = info[2]
    key_at, value_at = q_cols * shards, (q_cols + k_cols) * shards
    made, to = [], 0
    for s in range(shards):
        at = pl.ds(pl.multiple_of(info[2 + s] * rows, 16), rows)
        made.append(copies.start(token_refs[s], t_s.at[at]))
    for at, wide in ((0, q_cols), (key_at, k_cols), (value_at, k_cols)):
        cols = pl.ds(pl.multiple_of(at + shard * wide, 128), wide)
        made.append(
            copies.start(
                own_ref.at[:, cols],
                w_s.at[pl.ds(pl.multiple_of(shard * count, 16), count), pl.ds(to, wide)],
            )
        )
        to += wide
    for i, ref in enumerate(blocks):
        at = pl.ds(pl.multiple_of(places[i] * unit, 16), unit)
        made.append(copies.start(ref.at[pl.ds(0, unit)], w_s.at[at]))
    finish(made[:shards])
    value = t_s[...].astype(F32)
    normed_out[...] = (
        value
        * lax.rsqrt(jnp.mean(value * value, axis=-1, keepdims=True) + EPSILON)
        * gain_ref[...]
    ).astype(BF16)
    finish(made[shards:])
    sent = [copies.start(w_s, cols_out), copies.start(t_s, tokens_out)]
    out[...] = nn(normed_out[...], w_s[...])
    finish(sent)


def project(info, places, own, gain, tokens, blocks, shards, q_cols, k_cols, unit):
    rows, width = tokens[0].shape
    cols = q_cols + 2 * k_cols
    anywhere = pl.BlockSpec(memory_space=pltpu.HBM)
    here = pl.BlockSpec(memory_space=pltpu.VMEM)
    small = pl.BlockSpec(memory_space=pltpu.SMEM)
    return pl.pallas_call(
        partial(project_kernel, shards, q_cols, k_cols, unit),
        in_specs=[small, small, anywhere, here] + [anywhere] * (shards + len(blocks)),
        out_specs=[here, anywhere, here, anywhere],
        out_shape=[
            jax.ShapeDtypeStruct((shards * rows, width), BF16),
            jax.ShapeDtypeStruct((width, cols), BF16),
            jax.ShapeDtypeStruct((shards * rows, cols), F32),
            jax.ShapeDtypeStruct((shards * rows, width), BF16),
        ],
        scratch_shapes=[
            pltpu.VMEM((width, cols), BF16),
            pltpu.VMEM((shards * rows, width), BF16),
            pltpu.SemaphoreType.DMA((shards + 5 + len(blocks),)),
        ],
        compiler_params=pltpu.CompilerParams(vmem_limit_bytes=BIG_VMEM),
        cost_estimate=pl.CostEstimate(
            flops=2 * shards * rows * width * cols,
            bytes_accessed=2 * (width * cols + shards * rows * (2 * width + 2 * cols)),
            transcendentals=0,
        ),
    )(info, places, own, gain, *tokens, *blocks)


def router_back_kernel(experts, info, gate_ref, share_ref, second_ref, router_ref, grad_ref, add_ref):
    core = info[0] % 2
    rows = second_ref.shape[0]
    turned = jnp.transpose(
        jnp.concatenate([gate_ref[c] for c in range(experts // 2)], axis=0)
    )
    kept = jnp.concatenate([turned, jnp.zeros((rows, 128 - experts), F32)], axis=1)
    lanes = lax.broadcasted_iota(jnp.int32, (rows, 128), 1)
    swapped = jnp.where(lanes % 2 == 0, pltpu.roll(kept, 127, 1), pltpu.roll(kept, 1, 1))
    gates = jnp.where(core == 0, kept, swapped)
    share = share_ref[...]
    dot = jnp.sum(share * gates, axis=1, keepdims=True)
    low = (share * (gates - dot)).astype(BF16)
    grad_ref[...] = tn(second_ref[...], low)
    add_ref[...] = nt(low, router_ref[...])


def router_back(info, gates, shares, second, router, experts):
    rows, width = second.shape
    here = pl.BlockSpec(memory_space=pltpu.VMEM)
    return pl.pallas_call(
        partial(router_back_kernel, experts),
        in_specs=[pl.BlockSpec(memory_space=pltpu.SMEM)] + [here] * 4,
        out_specs=[here] * 2,
        out_shape=[
            jax.ShapeDtypeStruct((width, 128), F32),
            jax.ShapeDtypeStruct((rows, width), F32),
        ],
        compiler_params=pltpu.CompilerParams(vmem_limit_bytes=16 * MIB),
    )(info, gates, shares, second, router)


def middle_back_kernel(own, right, left, add, middle, gain, upstream, low_out, grad_out, gain_out):
    grad = own[...].astype(F32) + right[...].astype(F32) + left[...].astype(F32) + add[...]
    rows = middle[...]
    scale = lax.rsqrt(jnp.mean(rows * rows, axis=-1, keepdims=True) + EPSILON)
    unit = rows * scale
    share = jnp.sum(grad * unit, axis=0, keepdims=True)
    gain_out[...] = share + jnp.where(pl.program_id(0) == 0, 0.0, gain_out[...])
    weighted = grad * gain[...]
    dot = jnp.mean(weighted * unit, axis=-1, keepdims=True)
    total = upstream[...].astype(F32) + scale * (weighted - unit * dot)
    grad_out[...] = total
    low_out[...] = (RES_SCALE * total).astype(BF16)


def middle_back(own, right, left, add, middle, gain, upstream):
    rows, width = middle.shape
    block = rows // 4
    some = pl.BlockSpec((block, width), lambda i: (i, 0))
    one = pl.BlockSpec((1, width), lambda i: (0, 0))
    return pl.pallas_call(
        middle_back_kernel,
        grid=(4,),
        in_specs=[some] * 5 + [one, some],
        out_specs=[some, some, one],
        out_shape=[
            jax.ShapeDtypeStruct((rows, width), BF16),
            jax.ShapeDtypeStruct((rows, width), F32),
            jax.ShapeDtypeStruct((1, width), F32),
        ],
        compiler_params=pltpu.CompilerParams(vmem_limit_bytes=BIG_VMEM),
    )(own, right, left, add, middle, gain, upstream)


def ring_add_kernel(right, left, front, back, *outs):
    half = right.shape[0]
    if half < front.shape[0]:
        right_out, left_out = outs
        right_out[:half] = add_low(right[...], front[:half])
        right_out[half:] = front[half:]
        left_out[:half] = back[:half]
        left_out[half:] = add_low(left[...], back[half:])
        return
    for came, own, places in ((right, front, outs[: len(outs) // 2]), (left, back, outs[len(outs) // 2 :])):
        at = 0
        for out in places:
            rows = out.shape[0]
            out[...] = add_low(came[at : at + rows], own[at : at + rows])
            at += rows


def add_both(right, left, front, back, halved=False):
    here = pl.BlockSpec(memory_space=pltpu.VMEM)
    rows, width = front.shape
    shapes = [(rows // 2, width)] * 4 if halved else [(rows, width)] * 2
    return pl.pallas_call(
        ring_add_kernel,
        in_specs=[here] * 4,
        out_specs=[here] * len(shapes),
        out_shape=[jax.ShapeDtypeStruct(shape, front.dtype) for shape in shapes],
        compiler_params=pltpu.CompilerParams(vmem_limit_bytes=16 * MIB),
        cost_estimate=pl.CostEstimate(flops=1, bytes_accessed=12 * front.size, transcendentals=0),
    )(right, left, front, back)


def sum_blocks_kernel(plan, starts, *refs):
    arrays, refs = refs[: 2 * len(starts)], refs[2 * len(starts) :]
    many = len(plan)
    total = sum(len(came) for _, _, _, came in plan)
    refs, outs, (scratch, sems) = refs[:total], refs[total : total + many], refs[-2:]
    copies = Copies(sems)
    made = []
    for i, (place, low, high, _) in enumerate(plan):
        made.append([])
        for start, pair in zip(starts, (arrays[k : k + 2] for k in range(0, len(arrays), 2))):
            first, last = max(low, start), min(high, start + pair[0].shape[2])
            if first >= last:
                continue
            for j, ref in enumerate(pair):
                made[-1].append(
                    copies.start(
                        ref.at[place, :, pl.ds(first - start, last - first)],
                        scratch.at[2 * i + j, :, pl.ds(first - low, last - first)],
                    )
                )
    at = 0
    for i, (_, low, high, came) in enumerate(plan):
        finish(made[i])
        wide = high - low
        value = scratch[2 * i, :, :wide].astype(F32) + scratch[2 * i + 1, :, :wide].astype(F32)
        outs[i][...] = value.astype(BF16)
        for start, stop in came:
            part = value[:, start - low : stop - low] + refs[at][...].astype(F32)
            at += 1
            if (start, stop) == (low, high):
                value = part
            outs[i][:, start - low : stop - low] = part.astype(BF16)


def sum_blocks(pairs, wanted):
    unit = pairs[0][0].shape[1]
    starts = [sum(p[0].shape[2] for p in pairs[:i]) for i in range(len(pairs))]
    every = sum(p[0].shape[2] for p in pairs)
    plan, flat = [], []
    for place, low, high, came in wanted:
        plan.append((place, low, high, [(at, at + c.shape[1]) for at, c in came]))
        flat += [c for _, c in came]
    anywhere = pl.BlockSpec(memory_space=pltpu.HBM)
    here = pl.BlockSpec(memory_space=pltpu.VMEM)
    arrays = [array for pair in pairs for array in pair]
    return pl.pallas_call(
        partial(sum_blocks_kernel, plan, starts),
        in_specs=[anywhere] * len(arrays) + [here] * len(flat),
        out_specs=[here] * len(plan),
        out_shape=[jax.ShapeDtypeStruct((unit, high - low), BF16) for _, low, high, _ in plan],
        scratch_shapes=[
            pltpu.VMEM((2 * len(plan), unit, every), BF16),
            pltpu.SemaphoreType.DMA((len(arrays) * len(plan),)),
        ],
        compiler_params=pltpu.CompilerParams(vmem_limit_bytes=16 * MIB),
        cost_estimate=pl.CostEstimate(
            flops=1, bytes_accessed=6 * len(plan) * unit * every, transcendentals=0
        ),
    )(*arrays, *flat)


def body(
    tokens,
    segment_ids,
    routes,
    norm1_gain,
    norm2_gain,
    qkv_weight,
    out_weight,
    route_weight,
    expert_in,
    expert_down,
    cotangent,
):
    rows, width = tokens.shape
    shards = lax.axis_size("shard")
    chips = lax.axis_size("chip")
    experts = 2 * chips
    length = rows * shards
    q_cols = QUERY_HEADS // shards * HEAD_SIZE
    k_cols = KEY_VALUE_HEADS // shards * HEAD_SIZE
    own_cols = q_cols + 2 * k_cols
    query_width = QUERY_HEADS * HEAD_SIZE
    pair_width = KEY_VALUE_HEADS * HEAD_SIZE
    ffe = expert_down.shape[1]
    cut = width // shards
    shard = lax.axis_index("shard")
    core = lax.axis_index("core")
    chip = lax.axis_index("chip")
    walk = ring_chips(chips)
    ahead = [(walk[i], walk[(i + 1) % chips]) for i in range(chips)]
    behind = [(b, a) for a, b in ahead]
    half_ring = chips // 2
    order = [0]
    for step in range(1, half_ring):
        order += [-step, step]
    order.append(half_ring)
    place_of = {c: i for i, c in enumerate(walk)}
    chip_tables = np.array([[walk[(place_of[c] + o) % chips] for o in order] for c in range(chips)])
    senders = jnp.asarray(chip_tables, jnp.int32)[chip]
    info = jnp.concatenate(
        [
            jnp.stack([2 * chip + core, 2 * chip + 1 - core]),
            (shard - jnp.arange(shards) + shards) % shards,
            senders,
        ]
    ).astype(jnp.int32)
    slot_of = lambda i: 2 + shards + i
    both_cores = jnp.concatenate([2 * senders + core, 2 * senders + 1 - core])
    rel_tables = np.array([[list(row).index(c) for c in range(chips)] for row in chip_tables])
    chip_places = jnp.asarray(rel_tables, jnp.int32)[chip]

    def to_shard(value, step):
        return lax.ppermute(value, "shard", [(i, (i + step) % shards) for i in range(shards)])

    def to_core(value):
        return lax.ppermute(value, "core", [(0, 1), (1, 0)])

    def in_order(pieces):
        out = []
        for j in range(shards):
            value = pieces[0]
            for s in range(1, shards):
                value = jnp.where((shard - j + shards) % shards == s, pieces[s], value)
            out.append(value)
        return out

    def exchange_shards(piece_for):
        got = [piece_for(shard)]
        for s in range(1, shards):
            got.append(to_shard(piece_for(lax.rem(shard + s, shards)), s))
        return got

    def sum_shards(piece_for):
        got = exchange_shards(piece_for)
        total = got[0].astype(F32)
        for piece in got[1:]:
            total = total + piece.astype(F32)
        return total

    def to_holders(parts):
        return [parts[0]] + [to_shard(parts[s], s) for s in range(1, shards)]

    def ring_step(pair, cut_far=False):
        right, left = pair
        if cut_far:
            right, left = right[: rows // 2], left[rows // 2 :]
        return lax.ppermute(right, "chip", ahead), lax.ppermute(left, "chip", behind)

    def ring_gather(value):
        out, pair = [value], (value, value)
        for step in range(1, half_ring + 1):
            pair = ring_step(pair, step == half_ring)
            out += pair
        return out

    def ring_start(parts):
        return lax.ppermute(parts[-2], "chip", ahead), lax.ppermute(parts[-1], "chip", behind)

    def ring_add(parts, step, got):
        return tuple(add_both(*got, parts[2 * step], parts[2 * step - 1]))

    def ring_send(sent):
        return lax.ppermute(sent[0], "chip", ahead), lax.ppermute(sent[1], "chip", behind)

    def ring_end(parts, got):
        return parts[0].astype(F32) + got[0].astype(F32) + got[1].astype(F32)

    def plane_gather(value, beside, use_early):
        right = left = value
        got = [value]
        half = value.shape[1] // 256 * 128
        for step in range(1, half_ring + 1):
            if step > 1:
                right, left, beside[step] = lax.optimization_barrier(
                    (right, left, beside.get(step, ()))
                )
            if step == half_ring:
                right, left = right[:, :half], left[:, half:]
            right = lax.ppermute(right, "chip", ahead)
            left = lax.ppermute(left, "chip", behind)
            if step < half_ring:
                got += [right, left]
        early = 2 * half_ring - 3
        used = use_early(got[:early] + [to_core(v) for v in got[:early]])
        right, left, used = lax.optimization_barrier((right, left, used))
        late = got[early:] + [jnp.concatenate([right, left], axis=1)]
        return used, late + [to_core(v) for v in late]

    def block_ring(values, beside):
        right = left = values
        got = [values]
        for step in range(1, half_ring + 1):
            if step > 1:
                right, left, beside = lax.optimization_barrier(
                    (right, left, beside)
                ) if step == 3 else (*lax.optimization_barrier((right, left)), beside)
            right = [lax.ppermute(v, "chip", ahead) for v in right]
            got.append(right)
            if step < half_ring:
                left = [lax.ppermute(v, "chip", behind) for v in left]
                got.append(left)
        return got + [[to_core(v) for v in values] for values in got], beside

    def own_columns(rows_at, count, target):
        return jnp.concatenate(
            [
                lax.dynamic_slice(qkv_weight, (rows_at, at + target * cols), (count, cols))
                for at, cols in (
                    (0, q_cols),
                    (query_width, k_cols),
                    (query_width + pair_width, k_cols),
                )
            ],
            axis=1,
        )

    unit = cut // experts
    name = 2 * chip + core
    units = [
        to_shard(own_columns(name * unit, unit, lax.rem(shard + s, shards)), s)
        for s in range(1, shards)
    ]
    tokens_got = [tokens] + [to_shard(tokens, s) for s in range(1, shards)]
    extras = jnp.concatenate(
        [norm1_gain, norm2_gain, segment_ids.astype(BF16), route_weight.reshape(-1)]
    ).reshape(-1, 256)
    extras = [extras] + [to_shard(extras, s) for s in range(1, shards)]
    named = jnp.pad(routes.T.astype(BF16), ((0, 16 - routes.shape[1]), (0, own_cols - rows)))
    together = unit % 16 == 0
    if together:
        units[0] = jnp.concatenate([units[0], named], axis=0)
    else:
        units.append(named)
    blocks, (tokens_got, extras) = block_ring(units, (tokens_got, extras))

    held_in, held_down = tie((expert_in[0], expert_down[0]), tokens_got)
    down_own = [held_down] + [to_shard(held_down, s) for s in range(1, shards)]
    in_own = [held_in] + [to_shard(held_in, s) for s in range(1, shards)]
    layouts = ([(s, 0, cut, cut) for s in range(shards)],) * 2
    blocks, down_own, upstream = lax.optimization_barrier((blocks, down_own, cotangent))
    dy_pair = ring_step((upstream, upstream))
    upstream_chunks = [cotangent, *dy_pair]
    named_chunks = [b[0 if together else -1] for b in blocks[:chips]]
    named_at = unit if together else 0
    block_list = [b[s] for s in range(shards - 1) for b in blocks]
    block_places = jnp.concatenate(
        [info[2 + s] * experts + both_cores for s in range(1, shards)]
    ).astype(jnp.int32)
    extras = jnp.stack(in_order(extras)).reshape(shards, -1)
    gain_one = extras[:, :cut].reshape(1, -1).astype(F32)
    gain_two = extras[:, cut : 2 * cut].reshape(1, -1).astype(F32)
    segments = extras[:, 2 * cut : 2 * cut + rows].reshape(-1).astype(F32)
    router = extras[:, 2 * cut + rows :].reshape(width, experts)
    router_wide = jnp.pad(router, ((0, 0), (0, 128 - experts)))

    inputs = tokens.astype(F32)
    if together:
        normed, qkv_cols, projected, all_tokens = project(
            info, block_places, qkv_weight, gain_one, tokens_got, block_list, shards, q_cols, k_cols, unit
        )
    else:
        placed = jnp.zeros((shards * experts, unit, own_cols), BF16)
        for i, piece in enumerate(block_list):
            placed = lax.dynamic_update_index_in_dim(placed, piece, block_places[i], 0)
        qkv_cols = lax.dynamic_update_slice(
            placed.reshape(width, own_cols), own_columns(0, cut, shard), (shard * cut, 0)
        )
        all_tokens = jnp.concatenate(in_order(tokens_got), axis=0)
        wide_tokens = all_tokens.astype(F32)
        normed = (wide_tokens * rms_scale(wide_tokens) * gain_one).astype(BF16)
        projected = nn(normed, qkv_cols)
    places = jnp.arange(length)
    inverse = jnp.power(ROPE_BASE, -(jnp.arange(HEAD_SIZE // 2) * 2.0 / HEAD_SIZE))
    angles = places.astype(F32)[:, None] * inverse[None, :]
    cosine = jnp.concatenate([jnp.cos(angles)] * 4, axis=1)
    sine = jnp.concatenate([-jnp.sin(angles), jnp.sin(angles)] * 2, axis=1)
    projected, dy_pair = lax.optimization_barrier((projected, dy_pair))
    dy_pair = ring_step(dy_pair)
    upstream_chunks += dy_pair
    qkv, probs, head_out = attend(projected, cosine, sine, segments)
    branch = nn(head_out, out_weight).astype(BF16)
    branch, in_own, dy_pair = lax.optimization_barrier((branch, in_own, dy_pair))
    dy_pair = ring_step(dy_pair)
    upstream_chunks += dy_pair
    rows_of = lambda value, j: lax.dynamic_slice(value, (j * rows, 0), (rows, value.shape[1]))
    middle = inputs + RES_SCALE * sum_shards(lambda j: rows_of(branch, j))
    middle, dy_pair = lax.optimization_barrier((middle, dy_pair))
    weights = [in_own, down_own, [to_core(w) for w in in_own], [to_core(w) for w in down_own]]
    scale_two = rms_scale(middle)
    second = (middle * scale_two * gain_two).astype(BF16)

    second_chunks, pair = [second], (second, second)
    dy_hops = 3
    row_parts, gate_parts, lows, mixeds = [], [], [], []
    for step in range(half_ring + 1):
        first = max(0, 2 * step - 1)
        picks = list(range(first, len(second_chunks)))
        if step < half_ring:
            pair = ring_step(pair, step == half_ring - 1)
            second_chunks += pair
        far = step == half_ring
        slots = [(named_at, 0, rows)] * len(picks)
        if step == half_ring:
            slots = [(named_at, 0, rows), (named_at, rows // 2, rows)]
        low, mixed, row, gate, shares = run_experts(
            slots,
            info,
            [second_chunks[i] for i in picks],
            [upstream_chunks[i] for i in picks],
            [named_chunks[min(i, chips - 1)] for i in picks],
            router_wide,
            weights,
            layouts,
        )
        if step == 0:
            own_shares = shares
        if not far:
            pair, low, dy_pair = lax.optimization_barrier((pair, low, dy_pair))
            second_chunks[-2:] = pair
            last = dy_hops == half_ring - 1
            if dy_hops < half_ring and (not last or step == half_ring - 2):
                dy_hops += 1
                dy_pair = ring_step(tie(dy_pair, pair), last)
                upstream_chunks += dy_pair
        lows.append(low)
        mixeds.append(mixed)
        row_parts += row
        gate_parts += [gate] if far else [[g] for g in gate]

    def make_in(sent, at, more=()):
        return weight_grad(
            info, shards, second_chunks, 0, width, tie(lows, sent), at, 2 * ffe, more=more
        )

    got = ring_start(row_parts)
    made = make_in((), 2 * ffe)
    got, made = lax.optimization_barrier((got, made))
    in_other = [to_core(piece) for piece in made]
    for hop, step in enumerate(range(half_ring - 1, 0, -1)):
        sent = ring_add(row_parts, step, got)
        got = ring_send(sent)
        if hop == 0:
            in_parts = make_in(sent, 0, in_other)
            got, in_parts = lax.optimization_barrier((got, in_parts))
            in_got = to_holders(in_parts)
        if hop == 1:
            out_parts = run_results(
                info, tie(mixeds, sent), weights, layouts, [p.shape[0] for p in row_parts]
            )
            gate_home = sort_gates(info, tie(gate_parts, sent), rows)
            gate_home = lax.all_to_all(
                gate_home, "chip", split_axis=0, concat_axis=0, tiled=True
            )
            got, out_parts, gate_home = lax.optimization_barrier((got, out_parts, gate_home))
        if hop == 2:
            router_add = router_back(
                info, tie(gate_home, sent), own_shares, second, router_wide, experts
            )
            down_parts = weight_grad(
                info,
                shards,
                tie(mixeds, (sent, router_add)),
                0,
                2 * ffe,
                upstream_chunks,
                0,
                width,
                RES_SCALE,
                by_rows=False,
            )
            got, down_parts = lax.optimization_barrier((got, down_parts))
    grad_route, router_add = router_add
    out_got = ring_start(tie(out_parts, got))
    attn_low, middle_grads, grad_gain_two = middle_back(
        row_parts[0], *got, router_add, middle, gain_two, cotangent
    )
    attn_low, out_got = lax.optimization_barrier((attn_low, out_got))
    attn_low, in_got = lax.optimization_barrier((attn_low, in_got))

    low = lambda value: value.astype(BF16)
    sent = ring_add(out_parts, half_ring - 1, out_got)
    got = ring_send(sent)
    attn_got = [attn_low] + [to_shard(attn_low, s) for s in range(1, shards)]
    down_other = [to_core(piece) for piece in tie(down_parts[shards:], (attn_low, sent))]
    down_parts = [add_low(a, b) for a, b in zip(down_parts[:shards], down_other)]
    attn_got, got, down_parts = lax.optimization_barrier((attn_got, got, down_parts))
    if half_ring > 2:
        got = ring_send(ring_add(out_parts, half_ring - 2, got))

    down_got = to_holders(down_parts)
    projected_grads, attn_grads = attend_back(info, qkv, probs, out_weight, cosine, sine, attn_got)
    normed_low, grad_gain_one = normed_back(projected_grads, qkv_cols, all_tokens)
    got, normed_low, grad_gain_one, down_got = lax.optimization_barrier(
        (got, normed_low, grad_gain_one, down_got)
    )
    for step in range(half_ring - 3, 0, -1):
        sent = ring_add(out_parts, step, got)
        projected_grads, attn_grads, sent = lax.optimization_barrier(
            (projected_grads, attn_grads, sent)
        )
        got = ring_send(sent)

    mine_out, theirs_out = dense_grad(info, chip_places, unit, 1, head_out, attn_grads)
    theirs_out = to_core(theirs_out)
    mine_qkv, theirs_qkv = dense_grad(
        info,
        chip_places,
        unit,
        shards,
        tie(normed, mine_out),
        projected_grads,
        (grad_gain_one, grad_gain_two, grad_route),
    )
    wide = own_cols + 128
    mine_qkv, theirs_qkv, got = lax.optimization_barrier((mine_qkv, theirs_qkv, got))
    theirs_qkv = to_core(theirs_qkv)
    pairs = ((mine_qkv, theirs_qkv), (mine_out, theirs_out))
    every = mine_qkv.shape[2] + mine_out.shape[2]
    half = every // 256 * 128
    right, left = sum_blocks(pairs, [(chips - 1, 0, half, []), (chips - 1, half, every, [])])
    right, left = lax.ppermute(right, "chip", ahead), lax.ppermute(left, "chip", behind)
    right, left, normed_low = lax.optimization_barrier((right, left, normed_low))
    normed_got = exchange_shards(lambda j: rows_of(normed_low, j))
    for step in range(half_ring - 1, 0, -1):
        wanted = [
            (2 * step, 0, every, [(0, right)]),
            (2 * step - 1, 0, every, [(every - left.shape[1], left)]),
        ]
        if step == 1:
            wanted.append((0, 0, every, []))
        right, left, *own = sum_blocks(pairs, wanted)
        right = lax.ppermute(right, "chip", ahead)
        left = lax.ppermute(left, "chip", behind)
        right, left = lax.optimization_barrier((right, left))
        if step == half_ring - 2:
            right, left, normed_got = lax.optimization_barrier((right, left, normed_got))
    dense = low(own[0].astype(F32) + right.astype(F32) + left.astype(F32))
    mixed = in_order(
        [dense[:, :wide]]
        + [to_shard(dense[:, s * wide : (s + 1) * wide], s) for s in range(1, shards)]
    )
    merged = jnp.concatenate(
        [g[:, :q_cols] for g in mixed]
        + [g[:, q_cols : q_cols + k_cols] for g in mixed]
        + [g[:, q_cols + k_cols : own_cols] for g in mixed]
        + [low(sum(g[:, own_cols:].astype(F32) for g in mixed)), dense[:, shards * wide :]],
        axis=1,
    )

    total = lambda pieces: sum(p.astype(F32) for p in pieces)
    input_grads = rms_back(inputs, rms_scale(inputs), gain_one, total(normed_got))
    grad_tokens = middle_grads + input_grads
    grad_down, grad_in = total(down_got), total(in_got)

    block_out = low(middle + RES_SCALE * ring_end(out_parts, got))
    beside = {2: block_out, half_ring - 1: (grad_tokens, grad_down, grad_in)}
    all_cols = query_width + 2 * pair_width
    widths = [all_cols, 128, width]
    cores = jnp.split(both_cores.astype(jnp.int32), 2)
    count = 2 * half_ring - 3
    places = jnp.concatenate([c[:count] for c in cores] + [c[count:] for c in cores])
    spread_out, late = plane_gather(
        merged, beside, lambda early: spread(places, 0, early, widths, experts)
    )
    block_out = beside[2]
    grad_tokens, grad_down, grad_in = beside[half_ring - 1]
    spread_out = spread(places, 2 * count, late, widths, experts, spread_out)
    grad_qkv, small, grad_out = [out.reshape(-1, out.shape[-1]) for out in spread_out]
    return (
        block_out,
        grad_tokens,
        small[:, experts],
        small[:, experts + 1],
        grad_qkv,
        grad_out,
        small[:, :experts],
        grad_in[None],
        grad_down[None],
    )


def solution(mesh):
    chips = mesh.shape["expert"] // 2
    grid = Mesh(
        mesh.devices.reshape(chips, 2, mesh.shape["shard"]), ("chip", "core", "shard")
    )
    expert = ("chip", "core")
    every = ("chip", "core", "shard")
    in_specs = (
        P(every, None),
        P(every),
        P(every, None),
        P("shard"),
        P("shard"),
        P("shard", None),
        P("shard", None),
        P("shard", None),
        P(expert, "shard", None),
        P(expert, None, "shard"),
        P(every, None),
    )
    out_specs = (
        P(every, None),
        P(every, None),
        P("shard"),
        P("shard"),
        P("shard", None),
        P("shard", None),
        P("shard", None),
        P(expert, "shard", None),
        P(expert, None, "shard"),
    )
    return jax.shard_map(body, mesh=grid, in_specs=in_specs, out_specs=out_specs, check_vma=False)
```
